32 devices in a mesh: dp: 16 (over z, y, x), mp: 2 (over core).
Axes of the slice: x: 2, y: 2, z: 4, core: 2. Of those that a mesh axis runs over, the one named last changes fastest.
Arguments:
- source: bfloat16 [256, 8, 512], P('dp'), may hold values from -6 to 6
- target: bfloat16 [256, 8, 512], P('dp'), may hold values from -6 to 6
- lengths: int32 [256, 2], P('dp'), may hold values from 1 to 8, as said below
- destinations: int32 [256], P('dp'), may hold values from 0 to 15, as said below
- cotangent: bfloat16 [256, 8, 512], P('dp'), may hold values from -6 to 6
- square_master: float32 [12, 512, 512], P(None, 'dp', 'mp'), may hold values from -2 to 2
- wide_master: float32 [4, 512, 2048], P(None, 'dp', 'mp'), may hold values from -2 to 2
- norm_master: float32 [10, 512], P(None, 'dp'), may hold values from -2 to 4
- square_rows: float32 [12, 512], P(None, 'dp'), may hold values from 61.44 to 245.76
- square_cols: float32 [12, 512], P(None, 'mp'), may hold values from 61.44 to 245.76
- wide_rows: float32 [4, 512], P(None, 'dp'), may hold values from 102.4 to 409.6
- wide_cols: float32 [4, 2048], P(None, 'mp'), may hold values from 102.4 to 409.6
- gain_offset_moment: float32 [10, 512], P(None, 'dp'), may hold values from 307.2 to 1228.8
Outputs:
- decoded: bfloat16 [256, 8, 512], P('dp', 'mp')
- source_grad: float32 [256, 8, 512], P('dp', 'mp')
- target_grad: float32 [256, 8, 512], P('dp')
- square_grad: float32 [12, 512, 512], P(None, 'dp', 'mp')
- square_rows_new: float32 [12, 512], P(None, 'dp')
- square_cols_new: float32 [12, 512], P(None, 'mp')
- updated_square_masters: float32 [12, 512, 512], P(None, 'dp', 'mp')
- square_copy: bfloat16 [12, 512, 512], P(None, 'dp', 'mp')
- wide_grad: float32 [4, 512, 2048], P(None, 'dp', 'mp')
- wide_rows_new: float32 [4, 512], P(None, 'dp')
- wide_cols_new: float32 [4, 2048], P(None, 'mp')
- wide_new: float32 [4, 512, 2048], P(None, 'dp', 'mp')
- wide_copy: bfloat16 [4, 512, 2048], P(None, 'dp', 'mp')
- norm_grad: float32 [10, 512], P(None, 'dp')
- norm_second_new: float32 [10, 512], P(None, 'dp')
- norm_new: float32 [10, 512], P(None, 'dp')
- norm_copy: bfloat16 [10, 512], P(None, 'dp')
The draws below stay inside these ranges and needn't reach their ends.
Inputs may be any that keep to these rules, and one draw needn't show every extreme that they name: Column 0 holds source lengths and column 1 target lengths; each column holds 8 at least once. `destinations`: among the 16 pairs of each device, every device is named exactly 1 times.
All inputs are finite; a program needn't handle non-finite values.
Results may differ from the reference program's by a relative error of at most 0.02.
The reference program's roundings to bfloat16 on the way count: a program that leaves them out, or rounds other values in their place, can miss the bound.
Values may be sent and summed in bfloat16 or wider, within the bound.
A program may use at most 192 MiB of HBM per device.

```python
import math
import jax
import jax.numpy as jnp
from jax import lax

D = 512
FF = 2048
HEADS = 8
LEN = 8
PER_PEER = 1
SENT_DEV = 16
SENTS = 256
N_DP = 16


def draw_square_master(key, part):
    key = jax.random.fold_in(key, 11)
    noise = jnp.clip(jax.random.normal(key, (12, D, D), jnp.float32), -4.0, 4.0)
    factor = jnp.where(jnp.arange(12) % 4 == 3, 3.0, 1.0) * D ** (-0.5)
    return noise * factor[:, None, None]


def draw_wide_master(key, part):
    key = jax.random.fold_in(key, 12)
    noise = jnp.clip(jax.random.normal(key, (4, D, FF), jnp.float32), -4.0, 4.0)
    factor = jnp.where(jnp.arange(4) % 2 == 0, D ** (-0.5), FF ** (-0.5))
    return noise * factor[:, None, None]


def draw_norm_master(key, part):
    key = jax.random.fold_in(key, 13)
    first_key, second_key = jax.random.split(key)
    ramp = jnp.arange(D, dtype=jnp.float32) / (D - 1)
    rising = 0.6 + 1.2 * ramp
    jitter = jnp.exp(jax.random.uniform(first_key, (5, D), jnp.float32, -0.2, 0.2))
    offsets = 0.3 * jnp.clip(jax.random.normal(second_key, (5, D), jnp.float32), -4.0, 4.0)
    return jnp.concatenate([rising[None, :] * jitter, offsets], axis=0)


def draw_lengths(key, part):
    key = jax.random.fold_in(key, 21)
    first_key, second_key, tertiary_seed = jax.random.split(key, 3)
    first_draw = jax.random.randint(first_key, (SENTS, 2), 1, LEN + 1)
    second_draw = jax.random.randint(second_key, (SENTS, 2), 1, LEN + 1)
    shorter = jnp.minimum(first_draw, second_draw)
    longest_at = jax.random.randint(tertiary_seed, (2,), 0, SENTS)
    row_ids = jnp.arange(SENTS)[:, None]
    return jnp.where(row_ids == longest_at[None, :], LEN, shorter).astype(jnp.int32)


def shuffle_slots(key):
    base_slots = (jnp.arange(SENT_DEV, dtype=jnp.int32) // PER_PEER).astype(jnp.int32)
    return jax.random.permutation(key, base_slots)


def draw_destinations(key, part):
    key = jax.random.fold_in(key, 31)
    random_seeds_per_unit = jax.random.split(key, N_DP)
    return jax.vmap(shuffle_slots)(random_seeds_per_unit).reshape(SENTS).astype(jnp.int32)


def block_levels(stream_key, dims, shards, low, largest):
    gain = 1.0
    for dim, blocks in shards:
        heights = jax.random.uniform(jax.random.fold_in(jax.random.fold_in(stream_key, 6), dim), (blocks,), jnp.float32, low / len(shards), largest / len(shards))
        gain = gain * jnp.repeat(jnp.exp(heights), dims[dim] // blocks).reshape((-1,) + (1,) * (len(dims) - 1 - dim))
    return gain


def bell_draw(stream_key, extent, deviation, most, shards=(), kind=jnp.bfloat16):
    entries = deviation * jax.random.normal(stream_key, extent, jnp.float32)
    if shards:
        entries = entries * block_levels(stream_key, extent, shards, -0.22, 0.18)
    return jnp.clip(entries, -most, most).astype(kind)


def setup_inputs(seed: int = 0) -> dict:
    arg_keys = jax.random.split(jax.random.key(seed), 14)
    source = bell_draw(arg_keys[0], (SENTS, LEN, D), 1.0, 6.0, ((0, 16),))
    target = bell_draw(arg_keys[1], (SENTS, LEN, D), 1.0, 6.0, ((0, 16),))
    lengths = draw_lengths(jax.random.fold_in(arg_keys[13], 71), 0)
    destinations = draw_destinations(jax.random.fold_in(arg_keys[13], 71), 0)
    cotangent = bell_draw(arg_keys[4], (SENTS, LEN, D), 1.0, 6.0, ((0, 16),))
    square_master = draw_square_master(jax.random.fold_in(arg_keys[13], 71), 0)
    wide_master = draw_wide_master(jax.random.fold_in(arg_keys[13], 71), 0)
    norm_master = draw_norm_master(jax.random.fold_in(arg_keys[13], 71), 0)
    square_rows = jnp.clip(jnp.exp(math.log(245.76) - 1.3862944 * jax.random.uniform(arg_keys[8], (12, D), jnp.float32) ** block_levels(arg_keys[8], (12, D), ((1, 16),), -0.2, 0.2)), 61.44, 245.76)
    square_cols = jnp.clip(jnp.exp(math.log(245.76) - 1.3862944 * jax.random.uniform(arg_keys[9], (12, D), jnp.float32) ** block_levels(arg_keys[9], (12, D), ((1, 2),), -0.2, 0.2)), 61.44, 245.76)
    wide_rows = jnp.clip(jnp.exp(math.log(409.6) - 1.3862944 * jax.random.uniform(arg_keys[10], (4, D), jnp.float32) ** block_levels(arg_keys[10], (4, D), ((1, 16),), -0.2, 0.2)), 102.4, 409.6)
    wide_cols = jnp.clip(jnp.exp(math.log(409.6) - 1.3862944 * jax.random.uniform(arg_keys[11], (4, FF), jnp.float32) ** block_levels(arg_keys[11], (4, FF), ((1, 2),), -0.2, 0.2)), 102.4, 409.6)
    gain_offset_moment = jnp.clip(jnp.exp(math.log(1228.8) - 1.3862944 * jax.random.uniform(arg_keys[12], (10, D), jnp.float32) ** block_levels(arg_keys[12], (10, D), ((1, 16),), -0.2, 0.2)), 307.2, 1228.8)
    return {"source": source, "target": target, "lengths": lengths, "destinations": destinations, "cotangent": cotangent, "square_master": square_master, "wide_master": wide_master, "norm_master": norm_master, "square_rows": square_rows, "square_cols": square_cols, "wide_rows": wide_rows, "wide_cols": wide_cols, "gain_offset_moment": gain_offset_moment}


RATE = 0.03
NORM_RATE = 0.2
EXACT_PRECISION = lax.Precision.HIGHEST

@jax.custom_vjp
def low(v):
    return lax.optimization_barrier(v.astype(jnp.bfloat16)).astype(jnp.float32)

@jax.custom_vjp
def low_back(v):
    return v

def low_keep(v):
    return (low(v), None)

def low_pass(kept, grad):
    return (grad,)

def back_keep(v):
    return (v, None)

def back_low(kept, grad):
    return (low(grad),)
low.defvjp(low_keep, low_pass)
low_back.defvjp(back_keep, back_low)

def project(input_tensor, weight_matrix):
    return jnp.einsum('rft,tv->rfv', input_tensor, weight_matrix, precision=EXACT_PRECISION)

def project_back(input_tensor, weight_matrix):
    return jnp.einsum('cxk,ak->cxa', input_tensor, weight_matrix, precision=EXACT_PRECISION)

def layer_norm(residual, gain_row, bias_row):
    centred = residual - lax.optimization_barrier(jnp.mean(residual, axis=-1, keepdims=True))
    spread = lax.rsqrt(lax.optimization_barrier(jnp.mean(centred * centred, axis=-1, keepdims=True)) + 1e-05)
    return centred * spread * gain_row + bias_row

def attention(query_in, key_in, matrices, allowed):
    sentences, slots, model_width = query_in.shape
    head_size = model_width // HEADS
    queries = low(low_back(project(query_in, matrices[0]))).reshape(sentences, slots, HEADS, head_size)
    key_rows = low(low_back(project(key_in, matrices[1]))).reshape(sentences, slots, HEADS, head_size)
    content_lines = low(low_back(project(key_in, matrices[2]))).reshape(sentences, slots, HEADS, head_size)
    scores = low_back(jnp.einsum('sqhe,skhe->shqk', queries, key_rows, precision=EXACT_PRECISION) * head_size ** (-0.5))
    scores = jnp.where(allowed[:, None], scores, -1000000000.0)
    attn_probs = low(jax.nn.softmax(scores, axis=-1))
    mixed_heads = jnp.einsum('shqk,skhe->sqhe', attn_probs, content_lines, precision=EXACT_PRECISION)
    mixed_heads = low(low_back(mixed_heads.reshape(sentences, slots, model_width)))
    return low_back(project_back(mixed_heads, matrices[3]))

def feed_forward(inputs, up_matrix, down_matrix):
    hidden = low_back(project(inputs, up_matrix))
    active = low(low_back(jax.nn.gelu(hidden)))
    return low_back(project_back(active, down_matrix))

def key_mask(counts):
    positions = jnp.arange(LEN, dtype=jnp.int32)
    return jnp.broadcast_to(positions[None, None, :] < counts[:, None, None], (counts.shape[0], LEN, LEN))

def regroup_index(destinations):
    dest_rows = destinations.reshape(N_DP, SENT_DEV).astype(jnp.int32)
    send_order = jnp.argsort(dest_rows, axis=1, stable=True).astype(jnp.int32)
    home_place = jnp.argsort(send_order, axis=1, stable=True).astype(jnp.int32)
    source_dev = jnp.arange(N_DP, dtype=jnp.int32)[:, None]
    new_index = dest_rows * SENT_DEV + source_dev * PER_PEER + home_place - dest_rows * PER_PEER
    new_index = new_index.reshape(SENTS).astype(jnp.int32)
    return jnp.zeros((SENTS,), jnp.int32).at[new_index].set(jnp.arange(SENTS, dtype=jnp.int32))

def forward(square, wide, norms, source, target, lengths, moved_lengths, inverse):
    square = low(square)
    wide = low(wide)
    norms = low(norms)
    gain_rows = norms[:5]
    bias_rows = norms[5:]
    positions = jnp.arange(LEN, dtype=jnp.int32)
    causal = positions[None, :] <= positions[:, None]
    residual = source + attention(source, source, square[0:4], key_mask(lengths[:, 0]))
    hidden = layer_norm(residual, gain_rows[0], bias_rows[0])
    residual = hidden + feed_forward(low(hidden), wide[0], wide[1])
    memory = low(low_back(layer_norm(residual, gain_rows[1], bias_rows[1])))
    memory = jnp.take(memory, inverse, axis=0)
    target = jnp.take(low_back(target), inverse, axis=0)
    self_mask = key_mask(moved_lengths[:, 1]) & causal[None]
    residual = target + attention(target, target, square[4:8], self_mask)
    first_norm = layer_norm(residual, gain_rows[2], bias_rows[2])
    residual = first_norm + attention(low(first_norm), memory, square[8:12], key_mask(moved_lengths[:, 0]))
    second_norm = layer_norm(residual, gain_rows[3], bias_rows[3])
    residual = second_norm + feed_forward(low(second_norm), wide[2], wide[3])
    return layer_norm(residual, gain_rows[4], bias_rows[4])

def factored(gradient, master, rows, columns):
    squares = gradient * gradient
    rows_new = 0.5 * rows + 0.5 * lax.optimization_barrier(jnp.mean(squares, axis=2))
    cols_new = 0.5 * columns + 0.5 * lax.optimization_barrier(jnp.mean(squares, axis=1))
    level = lax.optimization_barrier(jnp.mean(rows_new, axis=1))
    second = rows_new[:, :, None] * cols_new[:, None, :] / level[:, None, None]
    return (rows_new, cols_new, master - RATE * gradient * lax.rsqrt(second))

def reference(source, target, lengths, destinations, cotangent, square_master, wide_master, norm_master, square_rows, square_cols, wide_rows, wide_cols, gain_offset_moment):
    inverse = regroup_index(destinations)
    moved_lengths = jnp.take(lengths, inverse, axis=0)

    def run(square, wide, norms, source_in, target_in):
        return forward(square, wide, norms, source_in, target_in, lengths, moved_lengths, inverse)
    decoded, pullback = jax.vjp(run, square_master, wide_master, norm_master, source.astype(jnp.float32), target.astype(jnp.float32))
    square_grad, wide_grad, norm_grad, source_grad, target_grad = pullback(cotangent.astype(jnp.float32))
    square_rows_new, square_cols_new, updated_square_masters = factored(square_grad, square_master, square_rows, square_cols)
    wide_rows_new, wide_cols_new, wide_new = factored(wide_grad, wide_master, wide_rows, wide_cols)
    norm_second_new = 0.5 * gain_offset_moment + 0.5 * norm_grad * norm_grad
    norm_new = norm_master - NORM_RATE * norm_grad * lax.rsqrt(norm_second_new)
    return (decoded.astype(jnp.bfloat16), source_grad, target_grad, square_grad, square_rows_new, square_cols_new, updated_square_masters, updated_square_masters.astype(jnp.bfloat16), wide_grad, wide_rows_new, wide_cols_new, wide_new, wide_new.astype(jnp.bfloat16), norm_grad, norm_second_new, norm_new, norm_new.astype(jnp.bfloat16))
```

```python
import types

import jax
import jax.numpy as jnp
from jax import lax
from jax.experimental import pallas as pl
from jax.experimental.pallas import tpu as pltpu
from jax.sharding import PartitionSpec as P

FF = 2048
HEADS = 8
MICRO = 2


RATE = 0.03
NORM_RATE = 0.2


def rounded(input_tensor):
    return input_tensor.astype(jnp.bfloat16)


def identity(input_tensor):
    return input_tensor


def project(input_tensor, weight_matrix):
    return jnp.einsum(
        "rft,tv->rfv", input_tensor, weight_matrix, preferred_element_type=jnp.float32
    )


def project_back(input_tensor, weight_matrix):
    return jnp.einsum(
        "cxk,ak->cxa", input_tensor, weight_matrix, preferred_element_type=jnp.float32
    )


def outer_sum(first_factor_array, second_factor_array):
    return jnp.einsum(
        "zmb,zmf->bf", first_factor_array, second_factor_array, preferred_element_type=jnp.float32
    )


def split_heads(input_tensor, head_size):
    return input_tensor.reshape(
        input_tensor.shape[0], input_tensor.shape[1], input_tensor.shape[2] // head_size, head_size
    )


def merge_heads(input_tensor):
    return input_tensor.reshape(
        input_tensor.shape[0], input_tensor.shape[1], input_tensor.shape[2] * input_tensor.shape[3]
    )


def layer_norm(residual, gain_row, bias_row):
    centred = residual - jnp.mean(residual, axis=-1, keepdims=True)
    spread = lax.rsqrt(jnp.mean(centred * centred, axis=-1, keepdims=True) + 1e-05)
    normed = centred * spread
    return (normed * gain_row + bias_row, (normed, spread))


def norm_back(upstream, gain_row, kept_state, pick):
    normed, spread = kept_state
    scaled = upstream * gain_row
    centred_grad = (
        scaled
        - jnp.mean(scaled, axis=-1, keepdims=True)
        - normed * jnp.mean(scaled * normed, axis=-1, keepdims=True)
    )
    return (
        centred_grad * spread,
        jnp.sum(pick(upstream * normed), axis=(0, 1)),
        jnp.sum(pick(upstream), axis=(0, 1)),
    )


def attend_forward(query_in, key_in, matrices, start_index, allowed, head_size):
    queries = split_heads(rounded(project(query_in, matrices[start_index])), head_size)
    key_rows = split_heads(rounded(project(key_in, matrices[start_index + 1])), head_size)
    content_lines = split_heads(rounded(project(key_in, matrices[start_index + 2])), head_size)
    scores = jnp.einsum(
        "sqhe,skhe->shqk", queries, key_rows, preferred_element_type=jnp.float32
    ) * head_size ** (-0.5)
    scores = jnp.where(allowed[:, None], scores, -1000000000.0)
    attn_probs = jax.nn.softmax(scores, axis=-1)
    probs_low = rounded(attn_probs)
    mixed_heads = rounded(
        merge_heads(
            jnp.einsum(
                "shqk,skhe->sqhe", probs_low, content_lines, preferred_element_type=jnp.float32
            )
        )
    )
    partial_value = project_back(mixed_heads, matrices[start_index + 3])
    return (partial_value, (queries, key_rows, content_lines, attn_probs, probs_low, mixed_heads))


def attend_back(upstream, query_in, key_in, matrices, start_index, kept_state, head_size):
    queries, key_rows, content_lines, attn_probs, probs_low, mixed_heads = kept_state
    scale = head_size ** (-0.5)
    out_grad = outer_sum(upstream, mixed_heads)
    mixed_grad = split_heads(rounded(project(upstream, matrices[start_index + 3])), head_size)
    prob_grad = jnp.einsum(
        "sqhe,skhe->shqk", mixed_grad, content_lines, preferred_element_type=jnp.float32
    )
    value_grad = rounded(
        jnp.einsum("shqk,sqhe->skhe", probs_low, mixed_grad, preferred_element_type=jnp.float32)
    )
    score_grad = rounded(
        attn_probs * (prob_grad - jnp.sum(attn_probs * prob_grad, axis=-1, keepdims=True))
    )
    query_grad = rounded(
        jnp.einsum("shqk,skhe->sqhe", score_grad, key_rows, preferred_element_type=jnp.float32)
        * scale
    )
    key_grad = rounded(
        jnp.einsum("shqk,sqhe->skhe", score_grad, queries, preferred_element_type=jnp.float32)
        * scale
    )
    query_grad = merge_heads(query_grad)
    key_grad = merge_heads(key_grad)
    value_grad = merge_heads(value_grad)
    weight_grads = (
        outer_sum(query_in, query_grad),
        outer_sum(key_in, key_grad),
        outer_sum(key_in, value_grad),
        out_grad,
    )
    asking_piece = project_back(query_grad, matrices[start_index])
    key_part = project_back(key_grad, matrices[start_index + 1]) + project_back(
        value_grad, matrices[start_index + 2]
    )
    return (asking_piece, key_part, weight_grads)


def expand_forward(inputs, matrices, start_index):
    hidden = project(inputs, matrices[start_index])
    active = rounded(jax.nn.gelu(hidden))
    return (project_back(active, matrices[start_index + 1]), (hidden, active))


def expand_back(upstream, inputs, matrices, start_index, kept_state):
    hidden, active = kept_state
    down_grad = outer_sum(upstream, active)
    active_grad = rounded(project(upstream, matrices[start_index + 1]))
    unused, pullback = jax.vjp(jax.nn.gelu, hidden)
    hidden_grad = rounded(pullback(active_grad.astype(jnp.float32))[0])
    up_grad = outer_sum(inputs, hidden_grad)
    return (project_back(hidden_grad, matrices[start_index]), up_grad, down_grad)


def accumulate(totals, position, addend):
    totals[position] = addend if totals[position] is None else totals[position] + addend


def shards(
    source,
    target,
    lengths,
    destinations,
    cotangent,
    square_master,
    wide_master,
    norm_master,
    square_rows,
    square_cols,
    wide_rows,
    wide_cols,
    gain_offset_moment,
):
    peer_count = lax.axis_size("dp")
    sent_dev = source.shape[0]
    slot_count = source.shape[1]
    model_width = source.shape[2]
    per_peer = sent_dev // peer_count
    head_size = model_width // HEADS
    per_block = sent_dev // MICRO
    half_len = slot_count // lax.axis_size("mp")
    half_start = lax.axis_index("mp") * half_len
    send_order = jnp.argsort(destinations, stable=True)
    home_place = jnp.argsort(send_order, stable=True)

    def own_half(input_tensor):
        return lax.dynamic_slice_in_dim(input_tensor, half_start, half_len, 1)

    def share_total(partial_value):
        return lax.psum_scatter(partial_value, "mp", scatter_dimension=1, tiled=True)

    def add_branch(residual, partial_value):
        return residual + share_total(partial_value)

    def low_rows(value):
        return lax.all_gather(rounded(value), "mp", axis=1, tiled=True)

    def by_peer(input_tensor):
        return jnp.take(input_tensor, send_order, axis=0).reshape(
            (peer_count, per_peer) + input_tensor.shape[1:]
        )

    def flatten(input_tensor):
        return input_tensor.reshape((sent_dev,) + input_tensor.shape[2:])

    moved_lengths = flatten(
        lax.all_to_all(by_peer(lengths), "dp", split_axis=0, concat_axis=0, tiled=True)
    )
    square_low, wide_low, norm_low = (
        lax.all_gather(rounded(square_master), "dp", axis=1, tiled=True),
        lax.all_gather(rounded(wide_master), "dp", axis=1, tiled=True),
        lax.all_gather(rounded(norm_master), "dp", axis=1, tiled=True),
    )
    gain_rows = norm_low[:5].astype(jnp.float32)
    bias_rows = norm_low[5:].astype(jnp.float32)
    positions = jnp.arange(slot_count)
    causal = positions[None, :] <= positions[:, None]

    def key_mask(counts):
        return jnp.broadcast_to(
            positions[None, None, :] < counts[:, None, None],
            (counts.shape[0], slot_count, slot_count),
        )

    square_grads = [None] * 12
    wide_grads = [None] * 4
    gain_grads = [None] * 5
    bias_grads = [None] * 5

    def norm_step(upstream, position, kept_state):
        residual_grad, gain_grad, bias_grad = norm_back(
            upstream, gain_rows[position], kept_state, identity
        )
        accumulate(gain_grads, position, gain_grad)
        accumulate(bias_grads, position, bias_grad)
        return residual_grad

    def attend_step(upstream_low, query_in, key_in, start_index, kept_state):
        asking_piece, key_part, weight_grads = attend_back(
            upstream_low, query_in, key_in, square_low, start_index, kept_state, head_size
        )
        for offset in range(4):
            accumulate(square_grads, start_index + offset, weight_grads[offset])
        return (asking_piece, key_part)

    def expand_step(upstream_low, inputs, start_index, kept_state):
        partial_value, up_grad, down_grad = expand_back(
            upstream_low, inputs, wide_low, start_index, kept_state
        )
        accumulate(wide_grads, start_index, up_grad)
        accumulate(wide_grads, start_index + 1, down_grad)
        return partial_value

    encoder_kept = []
    encoded_pieces = []
    for micro_index in range(MICRO):
        row_start = micro_index * per_block
        source_block = source[row_start : row_start + per_block]
        allowed = key_mask(lengths[row_start : row_start + per_block, 0])
        partial_value, attend_kept = attend_forward(
            source_block, source_block, square_low, 0, allowed, head_size
        )
        hidden, hidden_kept = layer_norm(
            add_branch(own_half(source_block).astype(jnp.float32), partial_value),
            gain_rows[0],
            bias_rows[0],
        )
        hidden_low = low_rows(hidden)
        partial_value, expand_kept = expand_forward(hidden_low, wide_low, 0)
        memory, memory_kept = layer_norm(
            add_branch(hidden, partial_value), gain_rows[1], bias_rows[1]
        )
        encoded_pieces.append(low_rows(memory))
        encoder_kept.append((attend_kept, hidden_kept, hidden_low, expand_kept, memory_kept))
    memory_all = jnp.concatenate(encoded_pieces, axis=0)
    moved_memory, moved_target = (
        lax.all_to_all(by_peer(memory_all), "dp", split_axis=0, concat_axis=0, tiled=True),
        lax.all_to_all(by_peer(target), "dp", split_axis=0, concat_axis=0, tiled=True),
    )
    moved_memory = flatten(moved_memory)
    moved_target = flatten(moved_target)
    decoded_parts = []
    memory_back = []
    target_back = []
    for micro_index in range(MICRO):
        row_start = micro_index * per_block
        target_block = moved_target[row_start : row_start + per_block]
        memory_block = moved_memory[row_start : row_start + per_block]
        counts = moved_lengths[row_start : row_start + per_block]
        self_mask = key_mask(counts[:, 1]) & causal[None]
        cross_attention_mask = key_mask(counts[:, 0])
        partial_value, self_kept = attend_forward(
            target_block, target_block, square_low, 4, self_mask, head_size
        )
        first_norm, first_kept = layer_norm(
            add_branch(own_half(target_block).astype(jnp.float32), partial_value),
            gain_rows[2],
            bias_rows[2],
        )
        first_low = low_rows(first_norm)
        partial_value, cross_kept = attend_forward(
            first_low, memory_block, square_low, 8, cross_attention_mask, head_size
        )
        second_norm, second_kept = layer_norm(
            add_branch(first_norm, partial_value), gain_rows[3], bias_rows[3]
        )
        second_low = low_rows(second_norm)
        partial_value, expand_kept = expand_forward(second_low, wide_low, 2)
        output, output_kept = layer_norm(
            add_branch(second_norm, partial_value), gain_rows[4], bias_rows[4]
        )
        decoded_parts.append(identity(rounded(output)))
        upstream = norm_step(
            own_half(cotangent[row_start : row_start + per_block]).astype(jnp.float32),
            4,
            output_kept,
        )
        upstream = add_branch(upstream, expand_step(low_rows(upstream), second_low, 2, expand_kept))
        upstream = norm_step(upstream, 3, second_kept)
        asking_piece, key_part = attend_step(
            low_rows(upstream), first_low, memory_block, 8, cross_kept
        )
        asking_piece, key_part = share_total((asking_piece, key_part))
        memory_back.append(low_rows(key_part))
        upstream = norm_step(upstream + asking_piece, 2, first_kept)
        asking_piece, key_part = attend_step(
            low_rows(upstream), target_block, target_block, 4, self_kept
        )
        target_back.append(low_rows(add_branch(upstream, asking_piece + key_part)))
    returned_memory, returned_target = (
        lax.all_to_all(
            jnp.concatenate(memory_back, axis=0).reshape(
                peer_count, per_peer, slot_count, model_width
            ),
            "dp",
            split_axis=0,
            concat_axis=0,
            tiled=True,
        ),
        lax.all_to_all(
            jnp.concatenate(target_back, axis=0).reshape(
                peer_count, per_peer, slot_count, model_width
            ),
            "dp",
            split_axis=0,
            concat_axis=0,
            tiled=True,
        ),
    )
    memory_gradient = jnp.take(flatten(returned_memory), home_place, axis=0)
    target_grad = jnp.take(flatten(returned_target), home_place, axis=0).astype(jnp.float32)
    source_parts = []
    for micro_index in range(MICRO):
        row_start = micro_index * per_block
        source_block = source[row_start : row_start + per_block]
        attend_kept, hidden_kept, hidden_low, expand_kept, memory_kept = encoder_kept[micro_index]
        upstream = norm_step(
            own_half(memory_gradient[row_start : row_start + per_block]).astype(jnp.float32),
            1,
            memory_kept,
        )
        upstream = add_branch(upstream, expand_step(low_rows(upstream), hidden_low, 0, expand_kept))
        upstream = norm_step(upstream, 0, hidden_kept)
        asking_piece, key_part = attend_step(
            low_rows(upstream), source_block, source_block, 0, attend_kept
        )
        source_parts.append(identity(add_branch(upstream, asking_piece + key_part)))
    square_grad = jnp.stack(square_grads)
    wide_grad = jnp.stack(wide_grads)
    norm_grad = jnp.stack(gain_grads + bias_grads)
    square_grad, wide_grad, norm_grad = (
        lax.psum_scatter(square_grad, "dp", scatter_dimension=1, tiled=True),
        lax.psum_scatter(wide_grad, "dp", scatter_dimension=1, tiled=True),
        lax.psum_scatter(norm_grad, "dp", scatter_dimension=1, tiled=True),
    )
    row_square, row_wide, norm_grad = lax.psum(
        (
            jnp.sum(square_grad * square_grad, axis=2),
            jnp.sum(wide_grad * wide_grad, axis=2),
            norm_grad,
        ),
        "mp",
    )
    square_rows_new = 0.5 * square_rows + 0.5 * (row_square / model_width)
    wide_rows_new = 0.5 * wide_rows + 0.5 * (row_wide / FF)
    col_square, col_wide, level_square, level_wide = lax.psum(
        (
            jnp.sum(square_grad * square_grad, axis=1),
            jnp.sum(wide_grad * wide_grad, axis=1),
            jnp.sum(square_rows_new, axis=1),
            jnp.sum(wide_rows_new, axis=1),
        ),
        "dp",
    )
    square_cols_new = 0.5 * square_cols + 0.5 * (col_square / model_width)
    wide_cols_new = 0.5 * wide_cols + 0.5 * (col_wide / model_width)
    square_second = (
        square_rows_new[:, :, None]
        * square_cols_new[:, None, :]
        / (level_square / model_width)[:, None, None]
    )
    wide_second = (
        wide_rows_new[:, :, None]
        * wide_cols_new[:, None, :]
        / (level_wide / model_width)[:, None, None]
    )
    updated_square_masters = square_master - RATE * square_grad * lax.rsqrt(square_second)
    wide_new = wide_master - RATE * wide_grad * lax.rsqrt(wide_second)
    norm_second_new = 0.5 * gain_offset_moment + 0.5 * norm_grad * norm_grad
    norm_new = norm_master - NORM_RATE * norm_grad * lax.rsqrt(norm_second_new)
    return (
        jnp.concatenate(decoded_parts, axis=0),
        jnp.concatenate(source_parts, axis=0),
        target_grad,
        square_grad,
        square_rows_new,
        square_cols_new,
        updated_square_masters,
        rounded(updated_square_masters),
        wide_grad,
        wide_rows_new,
        wide_cols_new,
        wide_new,
        rounded(wide_new),
        norm_grad,
        norm_second_new,
        norm_new,
        rounded(norm_new),
    )


SQUARE, WIDE = 0, 1
LANES = 128
TOKENS = 256
BLOCK = 128
CHUNK = 64
MESH_IDS = pl.DeviceIdType.MESH
NEG = -1000000000.0
OUTSIDE = -3.0e38
ENC_UNITS = ((SQUARE, 0), (WIDE, 0), (WIDE, 1))
DEC_UNITS = ((SQUARE, 0), (SQUARE, 1), (WIDE, 0), (WIDE, 1))
ALL_UNITS = ((0, 0), (0, 1), (0, 2), (1, 0), (1, 1), (1, 2), (1, 3))


def mm(a, b):
    return jnp.dot(a, b, preferred_element_type=jnp.float32)


def mm_nt(a, b):
    return lax.dot_general(a, b, (((1,), (1,)), ((), ())), preferred_element_type=jnp.float32)


def mm_tn(a, b):
    return lax.dot_general(a, b, (((0,), (0,)), ((), ())), preferred_element_type=jnp.float32)


def repeat(count, body):
    lax.fori_loop(0, count, lambda i, carry: (body(i), carry)[1], 0)


def aligned(i, size):
    return pl.ds(pl.multiple_of(i * size, size), size)


def unit_mats(role, u):
    kind, i = (ENC_UNITS, DEC_UNITS)[role][u]
    if kind == SQUARE:
        return kind, i, 4 * i + 4 * role
    return kind, i, i + 2 * role


def named(refs, *groups):
    return types.SimpleNamespace(**dict(zip([name for group in groups for name in group], refs)))


class Sems:
    def __init__(self, send, recv, count):
        self.send, self.recv, self.count, self.names = send, recv, count, {}

    def at(self, name):
        i = self.names.setdefault(name, len(self.names))
        assert i < self.count
        return self.send.at[i], self.recv.at[i]


SEM_COUNT = 120
(
    S_AX,
    S_AY,
    S_COT,
    S_DEC,
    S_DM,
    S_DT,
    S_FX,
    S_FY,
    S_M,
    S_MEMORY,
    S_NG,
    S_NORM,
    S_RA,
    S_RB,
    S_ROWS,
    S_RQ,
    S_SA,
    S_SB,
    S_SG,
    S_SOURCE,
    S_ST,
    S_T,
    S_TARGET,
    S_TT,
    S_Z,
) = range(25)

SCRATCH = dict(
    WS=((8, 4, 2, 2, 32, 256), jnp.bfloat16),
    WW=((2, 4, 2, 2, 32, 1024), jnp.bfloat16),
    GS=((8, 4, 2, 2, 32, 256), jnp.bfloat16),
    GW=((2, 4, 2, 2, 32, 1024), jnp.bfloat16),
    SB=((12, 32, 256), jnp.bfloat16),
    WB=((4, 32, 1024), jnp.bfloat16),
    R1AS=((8, 2, 2, 32, 256), jnp.bfloat16),
    R1BS=((8, 2, 2, 32, 256), jnp.bfloat16),
    R1AW=((2, 2, 2, 32, 1024), jnp.bfloat16),
    R1BW=((2, 2, 2, 32, 1024), jnp.bfloat16),
    R2AS=((8, 2, 32, 256), jnp.bfloat16),
    R2BS=((8, 2, 32, 256), jnp.bfloat16),
    R2AW=((2, 2, 32, 1024), jnp.bfloat16),
    R2BW=((2, 2, 32, 1024), jnp.bfloat16),
    R3S=((2, 12, 32, 256), jnp.bfloat16),
    R3W=((2, 4, 32, 1024), jnp.bfloat16),
    NB=((16, 16, LANES), jnp.bfloat16),
    RL=((16, 16, LANES), jnp.float32),
    NORM=((16, 512), jnp.float32),
    EXT=((BLOCK, LANES), jnp.float32),
    SEXT=((BLOCK, 640), jnp.bfloat16),
    XEXT=((BLOCK, 640), jnp.bfloat16),
    TSEND=((8, 16, 640), jnp.bfloat16),
    TREC=((16, 16, 640), jnp.bfloat16),
    COT2=((BLOCK, 512), jnp.bfloat16),
    COT=((TOKENS, 512), jnp.float32),
    XT=((TOKENS, 512), jnp.bfloat16),
    MSEND=((8, 2, 16, 512), jnp.bfloat16),
    MREC=((2, 2, 4, 16, 512), jnp.bfloat16),
    DMSEND=((2, 2, 4, 16, 512), jnp.bfloat16),
    MG=((8, 2, 16, 512), jnp.bfloat16),
    DTSEND=((16, 16, 512), jnp.bfloat16),
    TG=((8, 16, 512), jnp.bfloat16),
    DSEND=((BLOCK, 512), jnp.bfloat16),
    DREC=((BLOCK, 512), jnp.bfloat16),
    SGSEND=((BLOCK, 512), jnp.float32),
    SGREC=((BLOCK, 512), jnp.float32),
    PERMT=((2, BLOCK, BLOCK), jnp.bfloat16),
    ALLOW=((2, 2, BLOCK, TOKENS), jnp.float32),
    FILL=((BLOCK, TOKENS), jnp.float32),
    Q=((2, TOKENS, 256), jnp.bfloat16),
    K=((2, TOKENS, 256), jnp.bfloat16),
    V=((2, TOKENS, 256), jnp.bfloat16),
    O=((2, TOKENS, 256), jnp.bfloat16),
    PROB=((2, 4, BLOCK, TOKENS), jnp.float32),
    DO=((TOKENS, 256), jnp.bfloat16),
    DQ=((TOKENS, 256), jnp.bfloat16),
    DK=((TOKENS, 256), jnp.bfloat16),
    DV=((TOKENS, 256), jnp.bfloat16),
    U=((TOKENS, 1024), jnp.float32),
    ACT=((TOKENS, 1024), jnp.bfloat16),
    DU=((TOKENS, 1024), jnp.bfloat16),
    RES=((TOKENS, 512), jnp.float32),
    LOW=((3, TOKENS, 512), jnp.bfloat16),
    XH=((3, TOKENS, 512), jnp.float32),
    RSD=((3, TOKENS, 1), jnp.float32),
    GRAD=((TOKENS, 512), jnp.float32),
    GLOW=((TOKENS, 512), jnp.bfloat16),
    PS=((2, TOKENS, 512), jnp.float32),
    PR=((2, TOKENS, 512), jnp.float32),
    NGR=((4, 16, LANES), jnp.float32),
    NG=((16, 16, LANES), jnp.float32),
    ST=((7, 16, 8, LANES), jnp.float32),
    RQ=((BLOCK, LANES), jnp.float32),
    RQR=((BLOCK, LANES), jnp.float32),
    TT=((7, 8, LANES), jnp.float32),
    TTR=((7, 8, LANES), jnp.float32),
)

INPUTS = dict(
    lengths=0,
    destinations=0,
    source=0,
    target=0,
    cotangent=0,
    square=0,
    wide=0,
    norm=0,
    square_rows=0,
    wide_rows=0,
)
OUTPUTS = dict(
    o_dec=((BLOCK, 512), jnp.bfloat16),
    o_src=((BLOCK, 512), jnp.float32),
    o_tgt=((BLOCK, 512), jnp.float32),
    o_gs=((12, 32, 256), jnp.float32),
    o_gw=((4, 32, 1024), jnp.float32),
    o_cs=((12, 256), jnp.float32),
    o_cw=((4, 1024), jnp.float32),
    o_rq=((BLOCK, LANES), jnp.float32),
    o_rl=((16, LANES), jnp.float32),
    o_tt=((7, 8, LANES), jnp.float32),
    o_ng=((16, LANES), jnp.float32),
)


def exchange_kernel(*refs):
    r = named(refs, INPUTS, OUTPUTS, SCRATCH)
    sems = Sems(refs[-2], refs[-1], SEM_COUNT)
    d = lax.axis_index("dp")
    c = lax.axis_index("mp")
    z = lax.div(d, 4)
    yx = lax.rem(d, 4)
    y = lax.div(yx, 2)
    x = lax.rem(yx, 2)
    role = lax.rem(z, 2)
    x_mate = d + 1 - 2 * x
    y_mate = d + 2 - 4 * y
    partner = d + 4 - 8 * role
    bf, f32 = jnp.bfloat16, jnp.float32

    G = (r.GS, r.GW)
    R1A, R1B = (r.R1AS, r.R1AW), (r.R1BS, r.R1BW)
    R2A, R2B = (r.R2AS, r.R2AW), (r.R2BS, r.R2BW)

    def z_mate(k):
        zz = lax.rem(z + k, 4)
        return zz, zz * 4 + yx

    def copy(src, dst, name, dev, core=None):
        send, recv = sems.at(name)
        return pltpu.make_async_remote_copy(
            src_ref=src,
            dst_ref=dst,
            send_sem=send,
            recv_sem=recv,
            device_id=(dev, c if core is None else core),
            device_id_type=MESH_IDS,
        )

    def wait_in(dst, name):
        copy(dst, dst, name, x_mate).wait_recv()

    def wait_out(src, name):
        copy(src, src, name, x_mate).wait_send()

    def unit(buf, kind, i):
        if kind == SQUARE:
            return buf[0], (slice(4 * i, 4 * i + 4),)
        return buf[1], (i,)

    def part(buf, kind, i, *rest):
        ref, lead = unit(buf, kind, i)
        return ref.at[lead + rest]

    barrier = pltpu.get_barrier_semaphore()
    for k in range(1, 16):
        pl.semaphore_signal(
            barrier, inc=1, device_id=(lax.rem(d + k, 16), c), device_id_type=MESH_IDS
        )
    pl.semaphore_signal(barrier, inc=1, device_id=(d, 1 - c), device_id_type=MESH_IDS)

    for j in range(12):
        r.SB[j] = r.square[j].astype(bf)
    for j in range(4):
        r.WB[j] = r.wide[j].astype(bf)

    def own_weights(first_s, count, first_w):
        for j in range(count):
            r.WS[j, z, y, x] = r.SB[first_s + j]
        for j in range(2):
            r.WW[j, z, y, x] = r.WB[first_w + j]

    pl.when(role == 0)(lambda: own_weights(0, 4, 0))
    pl.when(role == 1)(lambda: own_weights(4, 8, 2))

    lane = lax.broadcasted_iota(jnp.int32, (8, LANES), 1)
    for s in range(16):
        r.EXT[8 * s : 8 * s + 8, :] = jnp.where(
            lane < 32,
            r.lengths[s, 0],
            jnp.where(lane < 64, r.lengths[s, 1], r.destinations[s]),
        ).astype(f32)
    ext_low = r.EXT[...].astype(bf)
    r.SEXT[:, 0:512] = r.source[...]
    r.SEXT[:, 512:640] = ext_low

    row_id = lax.broadcasted_iota(jnp.int32, (BLOCK, BLOCK), 0)
    col_id = lax.broadcasted_iota(jnp.int32, (BLOCK, BLOCK), 1)
    col_z = 2 * (col_id >> 6) + 1 - ((col_id >> 3) & 1)
    col_dev = (col_z * 4 + ((col_id >> 4) & 3)).astype(f32)
    same_slot = (row_id & 7) == (col_id & 7)

    def perm_of(dest_column):
        return jnp.where((dest_column == col_dev) & same_slot, 1.0, 0.0)

    perm_f = perm_of(r.EXT[:, 64:65])
    r.PERMT[0] = perm_f.astype(bf)
    perm = perm_f.T.astype(bf)
    r.TSEND[:, :, 0:512] = mm(perm, r.target[...]).astype(bf).reshape(8, 16, 512)
    r.TSEND[:, :, 512:640] = mm(perm, ext_low).astype(bf).reshape(8, 16, LANES)

    r.NORM[...] = jnp.zeros((16, 512), f32)
    r.NORM[0:10, 0:32] = r.norm[...]
    shift = lax.rem(d, 4) * 32
    r.NB[d] = pltpu.roll(r.NORM[:, 0:LANES], shift, 1).astype(bf)
    r.RL[d] = jnp.zeros((16, LANES), f32)
    r.RL[d, 0:12, 0:32] = r.square_rows[...]
    r.RL[d, 12:16, 0:32] = r.wide_rows[...]

    pl.semaphore_wait(barrier, 16)

    def z_sends(my_role):
        for u in range(4):
            for k in (1, 2, 3):
                target_role = my_role ^ (k & 1)
                if u >= (3, 4)[target_role]:
                    continue
                kind, i, j = unit_mats(target_role, u)
                src = r.SB.at[j : j + 4] if kind == SQUARE else r.WB.at[j]
                copy(src, z_slot(kind, i), (S_Z, u, k), z_mate(k)[1]).start()
            if u == 0:
                early(my_role)

    def z_slot(kind, i):
        if kind == SQUARE:
            return r.WS.at[4 * i : 4 * i + 4, z, y, x]
        return r.WW.at[i, z, y, x]

    def early(my_role):
        for k in range(1, 16):
            dev = lax.rem(d + k, 16)
            copy(r.NB.at[d], r.NB.at[d], S_NORM, dev).start()
        if my_role == 1:
            copy(r.SEXT, r.XEXT, S_SOURCE, partner).start()
        for t in range(8):
            dev = (2 * (t // 4) + 1) * 4 + t % 4
            send = copy(r.TSEND.at[t], r.TREC.at[d], S_TARGET, dev)
            if my_role == 0:
                send.start()
            else:
                pl.when(dev != d)(send.start)

                @pl.when(dev == d)
                def _():
                    r.TREC[d] = r.TSEND[t]

        if my_role == 0:
            copy(r.cotangent, r.COT2, S_COT, partner).start()
        for k in range(1, 16):
            dev = lax.rem(d + k, 16)
            copy(r.RL.at[d], r.RL.at[d], S_ROWS, dev).start()

    def early_sent(my_role):
        wait_out(r.NB.at[0:15], S_NORM)
        wait_out(r.RL.at[0:15], S_ROWS)
        if my_role == 1:
            wait_out(r.SEXT, S_SOURCE)
            wait_out(r.TSEND.at[0:7], S_TARGET)
        else:
            wait_out(r.cotangent, S_COT)
            wait_out(r.TSEND, S_TARGET)
        for u in range(4):
            for k in (1, 2, 3):
                target_role = my_role ^ (k & 1)
                if u < (3, 4)[target_role]:
                    kind, i, j = unit_mats(target_role, u)
                    wait_out(r.SB.at[j : j + 4] if kind == SQUARE else r.WB.at[j], (S_Z, u, k))

    def ag_column(units, u):
        kind, i = units[u]
        for k in (1, 2, 3):
            wait_in(z_slot(kind, i), (S_Z, u, k))
        block = z_slot_of(kind, i, y, x)
        copy(block, block, (S_AX, u), x_mate).start()
        copy(block, block, (S_AY, u), y_mate).start()

    def z_slot_of(kind, i, yy, xx, rows=slice(None)):
        if kind == SQUARE:
            return r.WS.at[4 * i : 4 * i + 4, rows, yy, xx]
        return r.WW.at[i, rows, yy, xx]

    def ag_forward(units, u):
        kind, i = units[u]
        wait_in(z_slot_of(kind, i, y, x), (S_AY, u))
        block = z_slot_of(kind, i, 1 - y, x, slice(0, 2))
        copy(block, block, (S_FX, u), x_mate).start()
        wait_in(z_slot_of(kind, i, y, x), (S_AX, u))
        block = z_slot_of(kind, i, y, 1 - x, slice(2, 4))
        copy(block, block, (S_FY, u), y_mate).start()

    def ag_finish(units, u):
        kind, i = units[u]
        block = z_slot_of(kind, i, y, x, slice(0, 2))
        wait_in(block, (S_FX, u))
        wait_in(block, (S_FY, u))

    def ag_sent(units):
        for u, (kind, i) in enumerate(units):
            block = z_slot_of(kind, i, y, x)
            half = z_slot_of(kind, i, y, x, slice(0, 2))
            wait_out(block, (S_AX, u))
            wait_out(block, (S_AY, u))
            wait_out(half, (S_FX, u))
            wait_out(half, (S_FY, u))

    def rs_first(units, u):
        kind, i = units[u]
        gref, lead = unit(G, kind, i)
        copy(
            gref.at[lead + (slice(0, 2), 1 - y)], part(R1A, kind, i), (S_RA, u), y_mate
        ).start()
        copy(
            gref.at[lead + (slice(2, 4), slice(None), 1 - x)],
            part(R1B, kind, i),
            (S_RB, u),
            x_mate,
        ).start()

    def add_into(ref, index, other):
        ref[index] = (ref[index].astype(f32) + other[...].astype(f32)).astype(bf)

    def rs_second(units, u):
        kind, i = units[u]
        gref, lead = unit(G, kind, i)
        ra, rb = part(R1A, kind, i), part(R1B, kind, i)
        wait_in(ra, (S_RA, u))
        add_into(gref, lead + (slice(0, 2), y), ra)
        copy(
            gref.at[lead + (slice(0, 2), y, 1 - x)], part(R2A, kind, i), (S_SA, u), x_mate
        ).start()
        wait_in(rb, (S_RB, u))
        add_into(gref, lead + (slice(2, 4), slice(None), x), rb)
        copy(
            gref.at[lead + (slice(2, 4), 1 - y, x)], part(R2B, kind, i), (S_SB, u), y_mate
        ).start()

    def rs_third(my_role, units, u):
        kind, i, j = unit_mats(my_role, u)
        gref, lead = unit(G, kind, i)
        ra, rb = part(R2A, kind, i), part(R2B, kind, i)
        wait_in(ra, (S_SA, u))
        add_into(gref, lead + (slice(0, 2), y, x), ra)
        wait_in(rb, (S_SB, u))
        add_into(gref, lead + (slice(2, 4), y, x), rb)
        for k in (1, 2, 3):
            slot = 1 if k == 3 else 0
            zz, dev = z_mate(k)
            if kind == SQUARE:
                dst = r.R3S.at[slot, j : j + 4]
            else:
                dst = r.R3W.at[slot, j]
            copy(gref.at[lead + (zz, y, x)], dst, (S_T, my_role, u, slot, k & 1), dev).start()

    def rs_sent(my_role, units):
        for u, (kind, i) in enumerate(units):
            gref, lead = unit(G, kind, i)
            wait_out(part(R1A, kind, i), (S_RA, u))
            wait_out(part(R1B, kind, i), (S_RB, u))
            wait_out(part(R2A, kind, i), (S_SA, u))
            wait_out(part(R2B, kind, i), (S_SB, u))
            for k in (1, 2, 3):
                slot = 1 if k == 3 else 0
                wait_out(gref.at[lead + (0, y, x)], (S_T, my_role, u, slot, k & 1))

    def final_sum(my_role, role_of, u):
        kind, i, j = unit_mats(role_of, u)
        if kind == SQUARE:
            dst = [r.R3S.at[slot, j : j + 4] for slot in (0, 1)]
        else:
            dst = [r.R3W.at[slot, j] for slot in (0, 1)]
        if my_role == role_of:
            wait_in(dst[0], (S_T, role_of, u, 0, 0))
            gref, lead = unit(G, kind, i)
            total = gref[lead + (z, y, x)].astype(f32) + dst[0][...].astype(f32)
        else:
            wait_in(dst[0], (S_T, role_of, u, 0, 1))
            wait_in(dst[1], (S_T, role_of, u, 1, 1))
            total = dst[0][...].astype(f32) + dst[1][...].astype(f32)
        if kind == SQUARE:
            r.o_gs[j : j + 4] = total
        else:
            r.o_gw[j] = total

    def unit_stats(g):
        role_of, u = ALL_UNITS[g]
        kind, i, j = unit_mats(role_of, u)
        lanes = lax.broadcasted_iota(jnp.int32, (32, LANES), 1)
        rows = r.RQ[0:32, :]
        if kind == SQUARE:
            for m in range(4):
                grad = r.o_gs[j + m]
                sq = grad * grad
                cols = jnp.sum(sq, axis=0, keepdims=True)
                for h in range(2):
                    r.ST[g, d, 2 * m + h : 2 * m + h + 1, :] = cols[:, h * LANES : (h + 1) * LANES]
                rows = jnp.where(lanes == j + m, jnp.sum(sq, axis=1, keepdims=True), rows)
        else:
            grad = r.o_gw[j]
            sq = grad * grad
            cols = jnp.sum(sq, axis=0, keepdims=True)
            for h in range(8):
                r.ST[g, d, h : h + 1, :] = cols[:, h * LANES : (h + 1) * LANES]
            rows = jnp.where(lanes == 12 + j, jnp.sum(sq, axis=1, keepdims=True), rows)
        r.RQ[0:32, :] = rows
        for k in range(1, 16):
            dev = lax.rem(d + k, 16)
            copy(r.ST.at[g, d], r.ST.at[g, d], (S_ST, g), dev).start()

    def weight(kind, i, cols=None):
        if kind == SQUARE:
            return r.WS[i].reshape(512, 256)
        if cols is None:
            return r.WW[i].reshape(512, 1024)
        return r.WW[i, :, :, :, :, cols].reshape(512, 256)

    def put_square(i, value):
        r.GS[i] = value.astype(bf).reshape(4, 2, 2, 32, 256)

    def swap(number, partial):
        slot = number % 2
        for half in range(2):
            rows = slice(half * BLOCK, (half + 1) * BLOCK)
            if number >= 2:
                wait_out(r.PS.at[slot, rows], (S_M, number - 2, half))
            r.PS[slot, rows] = partial(rows)
            copy(
                r.PS.at[slot, rows], r.PR.at[slot, rows], (S_M, number, half), d, 1 - c
            ).start()

    def swapped(number, body):
        slot = number % 2
        for half in range(2):
            rows = slice(half * BLOCK, (half + 1) * BLOCK)
            wait_in(r.PR.at[slot, rows], (S_M, number, half))

            def chunk(i):
                at = pl.ds(pl.multiple_of(half * BLOCK + i * CHUNK, CHUNK), CHUNK)
                body(at, half * (BLOCK // CHUNK) + i, r.PS[slot, at] + r.PR[slot, at])

            repeat(BLOCK // CHUNK, chunk)

    def swaps_sent(count):
        for number in (count - 2, count - 1):
            for half in range(2):
                wait_out(r.PS.at[0, 0:BLOCK], (S_M, number, half))

    def norm_forward(residual, kept, which, at):
        centred = residual - jnp.mean(residual, axis=-1, keepdims=True)
        spread = lax.rsqrt(jnp.mean(centred * centred, axis=-1, keepdims=True) + 1e-05)
        normed = centred * spread
        r.XH[kept, at] = normed
        r.RSD[kept, at] = spread
        return normed * r.NORM[which : which + 1, :] + r.NORM[5 + which : 6 + which, :]

    def norm_backward(upstream, kept, which, at):
        normed = r.XH[kept, at]
        scaled = upstream * r.NORM[which : which + 1, :]
        both = upstream * normed
        gain_sum = jnp.sum(both, axis=0, keepdims=True)
        bias_sum = jnp.sum(upstream, axis=0, keepdims=True)
        for b in range(4):
            lanes = slice(b * LANES, (b + 1) * LANES)
            r.NGR[b, which : which + 1, :] += gain_sum[:, lanes]
            r.NGR[b, 5 + which : 6 + which, :] += bias_sum[:, lanes]
        return r.RSD[kept, at] * (
            scaled
            - jnp.mean(scaled, axis=-1, keepdims=True)
            - normed * jnp.mean(scaled * normed, axis=-1, keepdims=True)
        )

    head_lane = lax.broadcasted_iota(jnp.int32, (1, LANES), 1)
    first_head = jnp.where(head_lane < 64, 1.0, 0.0)
    second_head = 1.0 - first_head

    def stacked(value):
        wide_value = value.astype(f32)
        return jnp.concatenate([wide_value * first_head, wide_value * second_head], axis=0).astype(bf)

    def unstacked(value):
        return value[0:BLOCK] * first_head + value[BLOCK:] * second_head

    def pairs(body):
        for blk in range(2):
            for pr in range(2):
                body(blk, slice(blk * BLOCK, (blk + 1) * BLOCK), slice(pr * LANES, (pr + 1) * LANES), 2 * blk + pr)

    def make_masks(slot, count_of, causal):
        row = lax.broadcasted_iota(jnp.int32, (BLOCK, TOKENS), 0)
        col = lax.broadcasted_iota(jnp.int32, (BLOCK, TOKENS), 1) & (BLOCK - 1)
        same = (row >> 3) == (col >> 3)
        r.FILL[...] = jnp.where(same, NEG, OUTSIDE)
        for blk in range(2):
            ok = same & ((col & 7).astype(f32) < count_of(blk))
            if causal:
                ok = ok & ((col & 7) <= (row & 7))
            r.ALLOW[slot, blk] = jnp.where(ok, 1.0, 0.0)

    def attend(kept, mask_slot):
        def one(blk, rows, lanes, n):
            keys = stacked(r.K[kept, rows, lanes])
            scores = mm_nt(r.Q[kept, rows, lanes], keys) * 0.125
            scores = jnp.where(r.ALLOW[mask_slot, blk] > 0.5, scores, r.FILL[...])
            halves = []
            for h in range(2):
                s = scores[:, h * BLOCK : (h + 1) * BLOCK]
                e = jnp.exp(s - jnp.max(s, axis=-1, keepdims=True))
                halves.append(e / jnp.sum(e, axis=-1, keepdims=True))
            probs = jnp.concatenate(halves, axis=1)
            r.PROB[kept, n] = probs
            r.O[kept, rows, lanes] = mm(
                probs.astype(bf), stacked(r.V[kept, rows, lanes])
            ).astype(bf)

        pairs(one)

    def attend_back(kept):
        def one(blk, rows, lanes, n):
            queries = r.Q[kept, rows, lanes]
            keys = stacked(r.K[kept, rows, lanes])
            values = stacked(r.V[kept, rows, lanes])
            out_grad = r.DO[rows, lanes]
            probs = r.PROB[kept, n]
            weighted = probs * mm_nt(out_grad, values)
            halves = []
            for h in range(2):
                w = weighted[:, h * BLOCK : (h + 1) * BLOCK]
                p = probs[:, h * BLOCK : (h + 1) * BLOCK]
                halves.append(w - p * jnp.sum(w, axis=-1, keepdims=True))
            score_grad = jnp.concatenate(halves, axis=1).astype(bf)
            r.DQ[rows, lanes] = (mm(score_grad, keys) * 0.125).astype(bf)
            r.DK[rows, lanes] = (unstacked(mm_tn(score_grad, queries)) * 0.125).astype(bf)
            r.DV[rows, lanes] = unstacked(mm_tn(probs.astype(bf), out_grad)).astype(bf)

        pairs(one)

    def project_all(kept, base, queries, keys):
        r.Q[kept] = mm(queries, weight(SQUARE, base)).astype(bf)
        r.K[kept] = mm(keys, weight(SQUARE, base + 1)).astype(bf)
        r.V[kept] = mm(keys, weight(SQUARE, base + 2)).astype(bf)

    def attention_out(kept, base):
        return lambda rows: mm_nt(r.O[kept, rows], weight(SQUARE, base + 3))

    def attention_back_start(kept, base):
        upstream = r.GLOW[...]
        put_square(base + 3, mm_tn(upstream, r.O[kept]))
        r.DO[...] = mm(upstream, weight(SQUARE, base + 3)).astype(bf)
        attend_back(kept)

    def attention_grads(base, queries, keys):
        put_square(base, mm_tn(queries, r.DQ[...]))
        put_square(base + 1, mm_tn(keys, r.DK[...]))
        put_square(base + 2, mm_tn(keys, r.DV[...]))

    def query_side(base):
        return lambda rows: mm_nt(r.DQ[rows], weight(SQUARE, base))

    def key_side(base):
        return lambda rows: mm_nt(r.DK[rows], weight(SQUARE, base + 1)) + mm_nt(
            r.DV[rows], weight(SQUARE, base + 2)
        )

    def all_sides(base):
        return lambda rows: query_side(base)(rows) + key_side(base)(rows)

    def expand(inputs):
        def one(n):
            cols = aligned(n, 256)
            hidden = mm(inputs, weight(WIDE, 0, cols))
            r.U[:, cols] = hidden
            bent = jnp.tanh(0.7978845608 * (hidden + 0.044715 * hidden * hidden * hidden))
            r.ACT[:, cols] = (0.5 * hidden * (1.0 + bent)).astype(bf)

        repeat(4, one)

    def contract(rows):
        return mm_nt(r.ACT[rows], weight(WIDE, 1))

    def expand_back_down():
        upstream = r.GLOW[...]

        def one(n):
            cols = aligned(n, 256)
            r.GW[1, :, :, :, :, cols] = (
                mm_tn(upstream, r.ACT[:, cols]).astype(bf).reshape(4, 2, 2, 32, 256)
            )

        repeat(4, one)

    def expand_back_up(inputs):
        upstream = r.GLOW[...]

        def one(n):
            cols = aligned(n, 256)
            active_grad = mm(upstream, weight(WIDE, 1, cols)).astype(bf).astype(f32)
            hidden = r.U[:, cols]
            square = hidden * hidden
            bent = jnp.tanh(0.7978845608 * (hidden + 0.044715 * hidden * square))
            slope = 0.5 * (1.0 + bent) + 0.5 * hidden * (1.0 - bent * bent) * 0.7978845608 * (
                1.0 + 3.0 * 0.044715 * square
            )
            hidden_grad = (active_grad * slope).astype(bf)
            r.DU[:, cols] = hidden_grad
            r.GW[0, :, :, :, :, cols] = (
                mm_tn(inputs, hidden_grad).astype(bf).reshape(4, 2, 2, 32, 256)
            )

        repeat(4, one)

    def expand_input(rows):
        return mm_nt(r.DU[rows], weight(WIDE, 0))

    def clear_sums():
        r.NGR[...] = jnp.zeros((4, 16, LANES), f32)
        r.RQ[...] = jnp.zeros((BLOCK, LANES), f32)

    def read_norms():
        wait_in(r.NB.at[0:15], S_NORM)
        for b in range(4):
            total = r.NB[4 * b].astype(f32)
            for i in range(1, 4):
                total = total + r.NB[4 * b + i].astype(f32)
            r.NORM[:, b * LANES : (b + 1) * LANES] = total

    def encoder():
        units = ENC_UNITS
        z_sends(0)
        clear_sums()
        wait_in(r.XEXT, S_SOURCE)
        r.XT[0:BLOCK] = r.source[...]
        r.XT[BLOCK:] = r.XEXT[:, 0:512]
        def counts(blk):
            return r.EXT[:, 0:1] if blk == 0 else r.XEXT[:, 512:640].astype(f32)[:, 0:1]

        make_masks(0, counts, False)
        r.PERMT[1] = perm_of(r.XEXT[:, 512:640].astype(f32)[:, 64:65]).astype(bf)
        ag_column(units, 0)
        read_norms()
        ag_column(units, 1)
        ag_forward(units, 0)
        ag_column(units, 2)
        ag_finish(units, 0)
        x_in = r.XT[...]
        project_all(0, 0, x_in, x_in)
        attend(0, 0)
        swap(0, attention_out(0, 0))
        ag_forward(units, 1)

        def first(at, n, total):
            hidden = norm_forward(r.XT[at].astype(f32) + total, 0, 0, at)
            r.RES[at] = hidden
            r.LOW[0, at] = hidden.astype(bf)

        swapped(0, first)
        ag_finish(units, 1)
        expand(r.LOW[0])
        ag_forward(units, 2)
        ag_finish(units, 2)
        swap(1, contract)

        def second(at, n, total):
            r.LOW[1, at] = norm_forward(r.RES[at] + total, 1, 1, at).astype(bf)

        swapped(1, second)
        for jj in range(2):
            block = r.LOW[1, jj * BLOCK : (jj + 1) * BLOCK]
            r.MSEND[:, jj] = mm_tn(r.PERMT[jj], block).astype(bf).reshape(8, 16, 512)
        zz = lax.div(z, 2)
        for t in range(8):
            dev = (2 * (t // 4) + 1) * 4 + t % 4
            copy(r.MSEND.at[t], r.MREC.at[zz, :, yx], S_MEMORY, dev).start()

        wait_in(r.DREC, S_DEC)
        r.o_dec[...] = r.DREC[...]
        wait_in(r.MG, S_DM)
        for jj in range(2):
            r.GRAD[jj * BLOCK : (jj + 1) * BLOCK] = mm(
                r.PERMT[jj], r.MG[:, jj].reshape(BLOCK, 512)
            )

        def back_one(i):
            at = aligned(i, CHUNK)
            value = norm_backward(r.GRAD[at], 1, 1, at)
            r.GRAD[at] = value
            r.GLOW[at] = value.astype(bf)

        repeat(TOKENS // CHUNK, back_one)
        expand_back_down()
        rs_first(units, 2)
        expand_back_up(r.LOW[0])
        rs_first(units, 1)
        swap(2, expand_input)

        def back_two(at, n, total):
            value = norm_backward(r.GRAD[at] + total, 0, 0, at)
            r.GRAD[at] = value
            r.GLOW[at] = value.astype(bf)

        swapped(2, back_two)
        attention_back_start(0, 0)
        attention_grads(0, r.XT[...], r.XT[...])
        rs_first(units, 0)
        swap(3, all_sides(0))
        rs_second(units, 2)

        def back_three(at, n, total):
            r.GRAD[at] = r.GRAD[at] + total

        swapped(3, back_three)
        r.o_src[...] = r.GRAD[0:BLOCK]
        r.SGSEND[...] = r.GRAD[BLOCK:]
        copy(r.SGSEND, r.SGREC, S_SG, partner).start()
        send_norm_sums()
        rs_second(units, 1)
        rs_third(0, units, 2)
        rs_second(units, 0)
        rs_third(0, units, 1)
        rs_third(0, units, 0)
        wait_out(r.MSEND, S_MEMORY)
        wait_out(r.SGSEND, S_SG)
        swaps_sent(4)
        take_target(0)
        for g in (6, 5, 4, 2, 1, 3, 0):
            final_sum(0, *ALL_UNITS[g])
            unit_stats(g)
        ag_sent(units)
        rs_sent(0, units)
        early_sent(0)

    def send_norm_sums():
        r.NG[d] = r.NGR[z]
        for k in range(1, 16):
            dev = lax.rem(d + k, 16)
            copy(r.NGR.at[lax.div(dev, 4)], r.NG.at[d], S_NG, dev).start()

    def take_target(my_role):
        if my_role == 0:
            wait_in(r.TG, S_DT)
        else:
            wait_in(r.TG.at[0:7], S_DT)
        r.o_tgt[...] = mm(r.PERMT[0], r.TG[...].reshape(BLOCK, 512))

    def decoder():
        units = DEC_UNITS
        z_sends(1)
        clear_sums()
        wait_in(r.TREC.at[0:15], S_TARGET)
        wait_in(r.COT2, S_COT)
        cot = r.COT

        def place(i):
            at = aligned(i, 32)
            both = jnp.concatenate(
                [
                    r.cotangent[at].astype(f32).reshape(4, 1, 8, 512),
                    r.COT2[at].astype(f32).reshape(4, 1, 8, 512),
                ],
                axis=1,
            )
            cot[aligned(i, CHUNK)] = both.reshape(CHUNK, 512)

        repeat(4, place)
        r.XT[...] = r.TREC[:, :, 0:512].reshape(TOKENS, 512)

        def counts(which):
            def get(blk):
                ext = r.TREC[8 * blk : 8 * blk + 8, :, 512:640].reshape(BLOCK, LANES)
                return ext.astype(f32)[:, 32 * which : 32 * which + 1]

            return get

        make_masks(0, counts(1), True)
        make_masks(1, counts(0), False)
        ag_column(units, 0)
        read_norms()
        ag_column(units, 1)
        ag_forward(units, 0)
        ag_column(units, 2)
        ag_column(units, 3)
        ag_finish(units, 0)
        x_in = r.XT[...]
        project_all(0, 0, x_in, x_in)
        attend(0, 0)
        swap(0, attention_out(0, 0))
        ag_forward(units, 1)

        def first(at, n, total):
            hidden = norm_forward(r.XT[at].astype(f32) + total, 0, 2, at)
            r.RES[at] = hidden
            r.LOW[0, at] = hidden.astype(bf)

        swapped(0, first)
        ag_finish(units, 1)
        ag_forward(units, 2)
        r.Q[1] = mm(r.LOW[0], weight(SQUARE, 4)).astype(bf)
        wait_in(r.MREC, S_MEMORY)
        memory = r.MREC[...].reshape(TOKENS, 512)
        r.K[1] = mm(memory, weight(SQUARE, 5)).astype(bf)
        r.V[1] = mm(memory, weight(SQUARE, 6)).astype(bf)
        attend(1, 1)
        swap(1, attention_out(1, 4))
        ag_forward(units, 3)

        def second(at, n, total):
            hidden = norm_forward(r.RES[at] + total, 1, 3, at)
            r.RES[at] = hidden
            r.LOW[1, at] = hidden.astype(bf)

        swapped(1, second)
        ag_finish(units, 2)
        expand(r.LOW[1])
        ag_finish(units, 3)
        swap(2, contract)

        def third(at, n, total):
            out = norm_forward(r.RES[at] + total, 2, 4, at)
            rows = aligned(n, 32)
            split = out.reshape(4, 2, 8, 512)
            r.o_dec[rows] = split[:, 0].reshape(32, 512).astype(bf)
            r.DSEND[rows] = split[:, 1].reshape(32, 512).astype(bf)
            value = norm_backward(cot[at], 2, 4, at)
            r.GRAD[at] = value
            r.GLOW[at] = value.astype(bf)

        swapped(2, third)
        expand_back_down()
        rs_first(units, 3)
        copy(r.DSEND, r.DREC, S_DEC, partner).start()
        expand_back_up(r.LOW[1])
        rs_first(units, 2)
        swap(3, expand_input)

        def back_two(at, n, total):
            value = norm_backward(r.GRAD[at] + total, 1, 3, at)
            r.GRAD[at] = value
            r.GLOW[at] = value.astype(bf)

        swapped(3, back_two)
        attention_back_start(1, 4)
        swap(4, key_side(4))
        attention_grads(4, r.LOW[0], r.MREC[...].reshape(TOKENS, 512))

        def back_memory(at, n, total):
            r.LOW[2, at] = total.astype(bf)

        swapped(4, back_memory)
        r.DMSEND[...] = r.LOW[2].reshape(2, 2, 4, 16, 512)
        my_t = lax.div(z, 2) * 4 + yx
        for t in range(8):
            dev = (2 * (t // 4)) * 4 + t % 4
            copy(r.DMSEND.at[t // 4, :, t % 4], r.MG.at[my_t], S_DM, dev).start()
        rs_first(units, 1)
        swap(5, query_side(4))
        rs_second(units, 3)

        def back_three(at, n, total):
            value = norm_backward(r.GRAD[at] + total, 0, 2, at)
            r.GRAD[at] = value
            r.GLOW[at] = value.astype(bf)

        swapped(5, back_three)
        attention_back_start(0, 0)
        attention_grads(0, r.XT[...], r.XT[...])
        rs_first(units, 0)
        swap(6, all_sides(0))
        rs_second(units, 2)

        def back_four(at, n, total):
            r.DTSEND[aligned(n, 4)] = (
                (r.GRAD[at] + total).astype(bf).reshape(4, 16, 512)
            )

        swapped(6, back_four)
        for k in range(1, 16):
            dev = lax.rem(d + k, 16)
            copy(r.DTSEND.at[dev], r.TG.at[my_t], S_DT, dev).start()
        r.TG[my_t] = r.DTSEND[d]
        send_norm_sums()
        rs_third(1, units, 3)
        rs_second(units, 1)
        rs_third(1, units, 2)
        rs_second(units, 0)
        rs_third(1, units, 1)
        rs_third(1, units, 0)
        take_target(1)
        wait_in(r.SGREC, S_SG)
        r.o_src[...] = r.SGREC[...]
        wait_out(r.DTSEND.at[0:15], S_DT)
        wait_out(r.MG, S_DM)
        wait_out(r.DSEND, S_DEC)
        swaps_sent(7)
        for g in (6, 5, 4, 2, 1, 3, 0):
            final_sum(1, *ALL_UNITS[g])
            unit_stats(g)
        ag_sent(units)
        rs_sent(1, units)
        early_sent(1)

    pl.when(role == 0)(encoder)
    pl.when(role == 1)(decoder)

    copy(r.RQ, r.RQR, S_RQ, d, 1 - c).start()
    wait_in(r.NG.at[0:15], S_NG)
    total = r.NG[0]
    for i in range(1, 16):
        total = total + r.NG[i]
    r.o_ng[...] = pltpu.roll(total, lax.rem(LANES - shift, LANES), 1)
    wait_in(r.RL.at[0:15], S_ROWS)
    total = r.RL[0]
    for i in range(1, 16):
        total = total + r.RL[i]
    r.o_rl[...] = jnp.broadcast_to(jnp.sum(total, axis=1, keepdims=True), (16, LANES))
    for g in (6, 5, 4, 2, 1, 3, 0):
        wait_in(r.ST.at[g, 0:15], (S_ST, g))
        total = r.ST[g, 0]
        for i in range(1, 16):
            total = total + r.ST[g, i]
        r.TT[g] = jnp.broadcast_to(jnp.sum(total, axis=1, keepdims=True), (8, LANES))
        role_of, u = ALL_UNITS[g]
        kind, _, j = unit_mats(role_of, u)
        for h in range(8):
            if kind == SQUARE:
                r.o_cs[j + h // 2 : j + h // 2 + 1, (h % 2) * LANES : (h % 2 + 1) * LANES] = total[h : h + 1]
            else:
                r.o_cw[j : j + 1, h * LANES : (h + 1) * LANES] = total[h : h + 1]
    copy(r.TT, r.TTR, S_TT, d, 1 - c).start()
    wait_in(r.RQR, S_RQ)
    r.o_rq[...] = r.RQ[...] + r.RQR[...]
    wait_in(r.TTR, S_TT)
    r.o_tt[...] = r.TT[...] + r.TTR[...]
    wait_out(r.RQ, S_RQ)
    wait_out(r.TT, S_TT)
    wait_out(r.NG.at[0:15], S_NG)
    for g in range(7):
        wait_out(r.ST.at[g, 0:15], (S_ST, g))


UPDATE_INPUTS = dict(
    square=0,
    wide=0,
    norm=0,
    square_rows=0,
    square_cols=0,
    wide_rows=0,
    wide_cols=0,
    moment=0,
)
UPDATE_OUTPUTS = dict(
    decoded=((16, 4, 512), jnp.bfloat16),
    source_grad=((16, 4, 512), jnp.float32),
    target_grad=((16, 8, 512), jnp.float32),
    square_grad=((12, 32, 256), jnp.float32),
    square_rows_new=((12, 32), jnp.float32),
    square_cols_new=((12, 256), jnp.float32),
    square_new=((12, 32, 256), jnp.float32),
    square_copy=((12, 32, 256), jnp.bfloat16),
    wide_grad=((4, 32, 1024), jnp.float32),
    wide_rows_new=((4, 32), jnp.float32),
    wide_cols_new=((4, 1024), jnp.float32),
    wide_new=((4, 32, 1024), jnp.float32),
    wide_copy=((4, 32, 1024), jnp.bfloat16),
    norm_grad=((10, 32), jnp.float32),
    norm_second_new=((10, 32), jnp.float32),
    norm_new=((10, 32), jnp.float32),
    norm_copy=((10, 32), jnp.bfloat16),
)


def update_kernel(*refs):
    r = named(refs, OUTPUTS, UPDATE_INPUTS, UPDATE_OUTPUTS, dict(rows_pad=0))
    c = lax.axis_index("mp")
    bf, f32 = jnp.bfloat16, jnp.float32

    def own_half(value):
        value = value.astype(f32).reshape(16, 8, 512)
        return jnp.where(c == 0, value[:, 0:4], value[:, 4:8])

    r.decoded[...] = own_half(r.o_dec[...]).astype(bf)
    r.source_grad[...] = own_half(r.o_src[...])
    r.target_grad[...] = r.o_tgt[...].reshape(16, 8, 512)
    pad = r.rows_pad
    pad[...] = jnp.zeros((BLOCK, LANES), f32)
    pad[0:12, 0:32] = r.square_rows[...]
    pad[12:16, 0:32] = r.wide_rows[...]
    lanes = lax.broadcasted_iota(jnp.int32, (BLOCK, LANES), 1)
    widths = jnp.where(lanes < 12, 1.0 / 512, 1.0 / FF)
    rows_new = 0.5 * pad[...].T + 0.5 * (r.o_rq[...] * widths)
    rows_back = rows_new.T
    r.square_rows_new[...] = rows_back[0:12, 0:32]
    r.wide_rows_new[...] = rows_back[12:16, 0:32]
    square_cols = 0.5 * r.square_cols[...] + 0.5 * (r.o_cs[...] / 512)
    wide_cols = 0.5 * r.wide_cols[...] + 0.5 * (r.o_cw[...] / 512)
    r.square_cols_new[...] = square_cols
    r.wide_cols_new[...] = wide_cols

    def level(m, total, width):
        return (0.5 * r.o_rl[m : m + 1, 0:1] + 0.5 * (total / width)) / 512

    def update(master, grad, row, col, lvl):
        return master - RATE * grad * lax.rsqrt(row * col / lvl)

    for g, (role, u) in enumerate(ALL_UNITS):
        kind, _, j = unit_mats(role, u)
        if kind == SQUARE:
            for m in range(4):
                sums = r.o_tt[g]
                total = sums[2 * m : 2 * m + 1, 0:1] + sums[2 * m + 1 : 2 * m + 2, 0:1]
                grad = r.o_gs[j + m]
                new = update(
                    r.square[j + m],
                    grad,
                    rows_new[0:32, j + m : j + m + 1],
                    square_cols[j + m : j + m + 1],
                    level(j + m, total, 512),
                )
                r.square_grad[j + m] = grad
                r.square_new[j + m] = new
                r.square_copy[j + m] = new.astype(bf)
        else:
            total = jnp.sum(r.o_tt[g], axis=0, keepdims=True)[:, 0:1]
            grad = r.o_gw[j]
            new = update(
                r.wide[j],
                grad,
                rows_new[0:32, 12 + j : 13 + j],
                wide_cols[j : j + 1],
                level(12 + j, total, FF),
            )
            r.wide_grad[j] = grad
            r.wide_new[j] = new
            r.wide_copy[j] = new.astype(bf)
    norm_grad = r.o_ng[0:10, 0:32]
    second = 0.5 * r.moment[...] + 0.5 * norm_grad * norm_grad
    norm_new = r.norm[...] - NORM_RATE * norm_grad * lax.rsqrt(second)
    r.norm_grad[...] = norm_grad
    r.norm_second_new[...] = second
    r.norm_new[...] = norm_new
    r.norm_copy[...] = norm_new.astype(bf)


def small_shards(
    source,
    target,
    lengths,
    destinations,
    cotangent,
    square_master,
    wide_master,
    norm_master,
    square_rows,
    square_cols,
    wide_rows,
    wide_cols,
    gain_offset_moment,
):
    vmem = pl.BlockSpec(memory_space=pltpu.VMEM)
    smem = pl.BlockSpec(memory_space=pltpu.SMEM)
    moved = pl.pallas_call(
        exchange_kernel,
        out_shape=[jax.ShapeDtypeStruct(*v) for v in OUTPUTS.values()],
        in_specs=[smem, smem] + [vmem] * 8,
        out_specs=[vmem] * len(OUTPUTS),
        scratch_shapes=[pltpu.VMEM(*v) for v in SCRATCH.values()]
        + [pltpu.SemaphoreType.DMA((SEM_COUNT,)), pltpu.SemaphoreType.DMA((SEM_COUNT,))],
        compiler_params=pltpu.CompilerParams(
            collective_id=0, has_side_effects=True, vmem_limit_bytes=56 << 20
        ),
    )(
        lengths,
        destinations,
        source.reshape(BLOCK, 512),
        target.reshape(BLOCK, 512),
        cotangent.reshape(BLOCK, 512),
        square_master,
        wide_master,
        norm_master,
        square_rows,
        wide_rows,
    )
    return tuple(
        pl.pallas_call(
            update_kernel,
            out_shape=[jax.ShapeDtypeStruct(*v) for v in UPDATE_OUTPUTS.values()],
            in_specs=[vmem] * (len(OUTPUTS) + len(UPDATE_INPUTS)),
            out_specs=[vmem] * len(UPDATE_OUTPUTS),
            scratch_shapes=[pltpu.VMEM((BLOCK, LANES), jnp.float32)],
            compiler_params=pltpu.CompilerParams(vmem_limit_bytes=32 << 20),
        )(
            *moved,
            square_master,
            wide_master,
            norm_master,
            square_rows,
            square_cols,
            wide_rows,
            wide_cols,
            gain_offset_moment,
        )
    )


def solution(mesh):
    return jax.shard_map(
        small_shards if dict(mesh.shape) == {"dp": 16, "mp": 2} else shards,
        mesh=mesh,
        in_specs=(
            P("dp", None, None),
            P("dp", None, None),
            P("dp", None),
            P("dp"),
            P("dp", None, None),
            P(None, "dp", "mp"),
            P(None, "dp", "mp"),
            P(None, "dp"),
            P(None, "dp"),
            P(None, "mp"),
            P(None, "dp"),
            P(None, "mp"),
            P(None, "dp"),
        ),
        out_specs=(
            P("dp", "mp", None),
            P("dp", "mp", None),
            P("dp", None, None),
            P(None, "dp", "mp"),
            P(None, "dp"),
            P(None, "mp"),
            P(None, "dp", "mp"),
            P(None, "dp", "mp"),
            P(None, "dp", "mp"),
            P(None, "dp"),
            P(None, "mp"),
            P(None, "dp", "mp"),
            P(None, "dp", "mp"),
            P(None, "dp"),
            P(None, "dp"),
            P(None, "dp"),
            P(None, "dp"),
        ),
        check_vma=False,
    )
```

```python
import types

import jax
import jax.numpy as jnp
from jax import lax
from jax.experimental import pallas as pl
from jax.experimental.pallas import tpu as pltpu
from jax.sharding import PartitionSpec as P

FF = 2048
HEADS = 8
MICRO = 2


RATE = 0.03
NORM_RATE = 0.2


def rounded(input_tensor):
    return input_tensor.astype(jnp.bfloat16)


def identity(input_tensor):
    return input_tensor


def project(input_tensor, weight_matrix):
    return jnp.einsum(
        "rft,tv->rfv", input_tensor, weight_matrix, preferred_element_type=jnp.float32
    )


def project_back(input_tensor, weight_matrix):
    return jnp.einsum(
        "cxk,ak->cxa", input_tensor, weight_matrix, preferred_element_type=jnp.float32
    )


def outer_sum(first_factor_array, second_factor_array):
    return jnp.einsum(
        "zmb,zmf->bf", first_factor_array, second_factor_array, preferred_element_type=jnp.float32
    )


def split_heads(input_tensor, head_size):
    return input_tensor.reshape(
        input_tensor.shape[0], input_tensor.shape[1], input_tensor.shape[2] // head_size, head_size
    )


def merge_heads(input_tensor):
    return input_tensor.reshape(
        input_tensor.shape[0], input_tensor.shape[1], input_tensor.shape[2] * input_tensor.shape[3]
    )


def layer_norm(residual, gain_row, bias_row):
    centred = residual - jnp.mean(residual, axis=-1, keepdims=True)
    spread = lax.rsqrt(jnp.mean(centred * centred, axis=-1, keepdims=True) + 1e-05)
    normed = centred * spread
    return (normed * gain_row + bias_row, (normed, spread))


def norm_back(upstream, gain_row, kept_state, pick):
    normed, spread = kept_state
    scaled = upstream * gain_row
    centred_grad = (
        scaled
        - jnp.mean(scaled, axis=-1, keepdims=True)
        - normed * jnp.mean(scaled * normed, axis=-1, keepdims=True)
    )
    return (
        centred_grad * spread,
        jnp.sum(pick(upstream * normed), axis=(0, 1)),
        jnp.sum(pick(upstream), axis=(0, 1)),
    )


def attend_forward(query_in, key_in, matrices, start_index, allowed, head_size):
    queries = split_heads(rounded(project(query_in, matrices[start_index])), head_size)
    key_rows = split_heads(rounded(project(key_in, matrices[start_index + 1])), head_size)
    content_lines = split_heads(rounded(project(key_in, matrices[start_index + 2])), head_size)
    scores = jnp.einsum(
        "sqhe,skhe->shqk", queries, key_rows, preferred_element_type=jnp.float32
    ) * head_size ** (-0.5)
    scores = jnp.where(allowed[:, None], scores, -1000000000.0)
    attn_probs = jax.nn.softmax(scores, axis=-1)
    probs_low = rounded(attn_probs)
    mixed_heads = rounded(
        merge_heads(
            jnp.einsum(
                "shqk,skhe->sqhe", probs_low, content_lines, preferred_element_type=jnp.float32
            )
        )
    )
    partial_value = project_back(mixed_heads, matrices[start_index + 3])
    return (partial_value, (queries, key_rows, content_lines, attn_probs, probs_low, mixed_heads))


def attend_back(upstream, query_in, key_in, matrices, start_index, kept_state, head_size):
    queries, key_rows, content_lines, attn_probs, probs_low, mixed_heads = kept_state
    scale = head_size ** (-0.5)
    out_grad = outer_sum(upstream, mixed_heads)
    mixed_grad = split_heads(rounded(project(upstream, matrices[start_index + 3])), head_size)
    prob_grad = jnp.einsum(
        "sqhe,skhe->shqk", mixed_grad, content_lines, preferred_element_type=jnp.float32
    )
    value_grad = rounded(
        jnp.einsum("shqk,sqhe->skhe", probs_low, mixed_grad, preferred_element_type=jnp.float32)
    )
    score_grad = rounded(
        attn_probs * (prob_grad - jnp.sum(attn_probs * prob_grad, axis=-1, keepdims=True))
    )
    query_grad = rounded(
        jnp.einsum("shqk,skhe->sqhe", score_grad, key_rows, preferred_element_type=jnp.float32)
        * scale
    )
    key_grad = rounded(
        jnp.einsum("shqk,sqhe->skhe", score_grad, queries, preferred_element_type=jnp.float32)
        * scale
    )
    query_grad = merge_heads(query_grad)
    key_grad = merge_heads(key_grad)
    value_grad = merge_heads(value_grad)
    weight_grads = (
        outer_sum(query_in, query_grad),
        outer_sum(key_in, key_grad),
        outer_sum(key_in, value_grad),
        out_grad,
    )
    asking_piece = project_back(query_grad, matrices[start_index])
    key_part = project_back(key_grad, matrices[start_index + 1]) + project_back(
        value_grad, matrices[start_index + 2]
    )
    return (asking_piece, key_part, weight_grads)


def expand_forward(inputs, matrices, start_index):
    hidden = project(inputs, matrices[start_index])
    active = rounded(jax.nn.gelu(hidden))
    return (project_back(active, matrices[start_index + 1]), (hidden, active))


def expand_back(upstream, inputs, matrices, start_index, kept_state):
    hidden, active = kept_state
    down_grad = outer_sum(upstream, active)
    active_grad = rounded(project(upstream, matrices[start_index + 1]))
    unused, pullback = jax.vjp(jax.nn.gelu, hidden)
    hidden_grad = rounded(pullback(active_grad.astype(jnp.float32))[0])
    up_grad = outer_sum(inputs, hidden_grad)
    return (project_back(hidden_grad, matrices[start_index]), up_grad, down_grad)


def accumulate(totals, position, addend):
    totals[position] = addend if totals[position] is None else totals[position] + addend


def shards(
    source,
    target,
    lengths,
    destinations,
    cotangent,
    square_master,
    wide_master,
    norm_master,
    square_rows,
    square_cols,
    wide_rows,
    wide_cols,
    gain_offset_moment,
):
    peer_count = lax.axis_size("dp")
    sent_dev = source.shape[0]
    slot_count = source.shape[1]
    model_width = source.shape[2]
    per_peer = sent_dev // peer_count
    head_size = model_width // HEADS
    per_block = sent_dev // MICRO
    half_len = slot_count // lax.axis_size("mp")
    half_start = lax.axis_index("mp") * half_len
    send_order = jnp.argsort(destinations, stable=True)
    home_place = jnp.argsort(send_order, stable=True)

    def own_half(input_tensor):
        return lax.dynamic_slice_in_dim(input_tensor, half_start, half_len, 1)

    def share_total(partial_value):
        return lax.psum_scatter(partial_value, "mp", scatter_dimension=1, tiled=True)

    def add_branch(residual, partial_value):
        return residual + share_total(partial_value)

    def low_rows(value):
        return lax.all_gather(rounded(value), "mp", axis=1, tiled=True)

    def by_peer(input_tensor):
        return jnp.take(input_tensor, send_order, axis=0).reshape(
            (peer_count, per_peer) + input_tensor.shape[1:]
        )

    def flatten(input_tensor):
        return input_tensor.reshape((sent_dev,) + input_tensor.shape[2:])

    moved_lengths = flatten(
        lax.all_to_all(by_peer(lengths), "dp", split_axis=0, concat_axis=0, tiled=True)
    )
    square_low, wide_low, norm_low = (
        lax.all_gather(rounded(square_master), "dp", axis=1, tiled=True),
        lax.all_gather(rounded(wide_master), "dp", axis=1, tiled=True),
        lax.all_gather(rounded(norm_master), "dp", axis=1, tiled=True),
    )
    gain_rows = norm_low[:5].astype(jnp.float32)
    bias_rows = norm_low[5:].astype(jnp.float32)
    positions = jnp.arange(slot_count)
    causal = positions[None, :] <= positions[:, None]

    def key_mask(counts):
        return jnp.broadcast_to(
            positions[None, None, :] < counts[:, None, None],
            (counts.shape[0], slot_count, slot_count),
        )

    square_grads = [None] * 12
    wide_grads = [None] * 4
    gain_grads = [None] * 5
    bias_grads = [None] * 5

    def norm_step(upstream, position, kept_state):
        residual_grad, gain_grad, bias_grad = norm_back(
            upstream, gain_rows[position], kept_state, identity
        )
        accumulate(gain_grads, position, gain_grad)
        accumulate(bias_grads, position, bias_grad)
        return residual_grad

    def attend_step(upstream_low, query_in, key_in, start_index, kept_state):
        asking_piece, key_part, weight_grads = attend_back(
            upstream_low, query_in, key_in, square_low, start_index, kept_state, head_size
        )
        for offset in range(4):
            accumulate(square_grads, start_index + offset, weight_grads[offset])
        return (asking_piece, key_part)

    def expand_step(upstream_low, inputs, start_index, kept_state):
        partial_value, up_grad, down_grad = expand_back(
            upstream_low, inputs, wide_low, start_index, kept_state
        )
        accumulate(wide_grads, start_index, up_grad)
        accumulate(wide_grads, start_index + 1, down_grad)
        return partial_value

    encoder_kept = []
    encoded_pieces = []
    for micro_index in range(MICRO):
        row_start = micro_index * per_block
        source_block = source[row_start : row_start + per_block]
        allowed = key_mask(lengths[row_start : row_start + per_block, 0])
        partial_value, attend_kept = attend_forward(
            source_block, source_block, square_low, 0, allowed, head_size
        )
        hidden, hidden_kept = layer_norm(
            add_branch(own_half(source_block).astype(jnp.float32), partial_value),
            gain_rows[0],
            bias_rows[0],
        )
        hidden_low = low_rows(hidden)
        partial_value, expand_kept = expand_forward(hidden_low, wide_low, 0)
        memory, memory_kept = layer_norm(
            add_branch(hidden, partial_value), gain_rows[1], bias_rows[1]
        )
        encoded_pieces.append(low_rows(memory))
        encoder_kept.append((attend_kept, hidden_kept, hidden_low, expand_kept, memory_kept))
    memory_all = jnp.concatenate(encoded_pieces, axis=0)
    moved_memory, moved_target = (
        lax.all_to_all(by_peer(memory_all), "dp", split_axis=0, concat_axis=0, tiled=True),
        lax.all_to_all(by_peer(target), "dp", split_axis=0, concat_axis=0, tiled=True),
    )
    moved_memory = flatten(moved_memory)
    moved_target = flatten(moved_target)
    decoded_parts = []
    memory_back = []
    target_back = []
    for micro_index in range(MICRO):
        row_start = micro_index * per_block
        target_block = moved_target[row_start : row_start + per_block]
        memory_block = moved_memory[row_start : row_start + per_block]
        counts = moved_lengths[row_start : row_start + per_block]
        self_mask = key_mask(counts[:, 1]) & causal[None]
        cross_attention_mask = key_mask(counts[:, 0])
        partial_value, self_kept = attend_forward(
            target_block, target_block, square_low, 4, self_mask, head_size
        )
        first_norm, first_kept = layer_norm(
            add_branch(own_half(target_block).astype(jnp.float32), partial_value),
            gain_rows[2],
            bias_rows[2],
        )
        first_low = low_rows(first_norm)
        partial_value, cross_kept = attend_forward(
            first_low, memory_block, square_low, 8, cross_attention_mask, head_size
        )
        second_norm, second_kept = layer_norm(
            add_branch(first_norm, partial_value), gain_rows[3], bias_rows[3]
        )
        second_low = low_rows(second_norm)
        partial_value, expand_kept = expand_forward(second_low, wide_low, 2)
        output, output_kept = layer_norm(
            add_branch(second_norm, partial_value), gain_rows[4], bias_rows[4]
        )
        decoded_parts.append(identity(rounded(output)))
        upstream = norm_step(
            own_half(cotangent[row_start : row_start + per_block]).astype(jnp.float32),
            4,
            output_kept,
        )
        upstream = add_branch(upstream, expand_step(low_rows(upstream), second_low, 2, expand_kept))
        upstream = norm_step(upstream, 3, second_kept)
        asking_piece, key_part = attend_step(
            low_rows(upstream), first_low, memory_block, 8, cross_kept
        )
        asking_piece, key_part = share_total((asking_piece, key_part))
        memory_back.append(low_rows(key_part))
        upstream = norm_step(upstream + asking_piece, 2, first_kept)
        asking_piece, key_part = attend_step(
            low_rows(upstream), target_block, target_block, 4, self_kept
        )
        target_back.append(low_rows(add_branch(upstream, asking_piece + key_part)))
    returned_memory, returned_target = (
        lax.all_to_all(
            jnp.concatenate(memory_back, axis=0).reshape(
                peer_count, per_peer, slot_count, model_width
            ),
            "dp",
            split_axis=0,
            concat_axis=0,
            tiled=True,
        ),
        lax.all_to_all(
            jnp.concatenate(target_back, axis=0).reshape(
                peer_count, per_peer, slot_count, model_width
            ),
            "dp",
            split_axis=0,
            concat_axis=0,
            tiled=True,
        ),
    )
    memory_gradient = jnp.take(flatten(returned_memory), home_place, axis=0)
    target_grad = jnp.take(flatten(returned_target), home_place, axis=0).astype(jnp.float32)
    source_parts = []
    for micro_index in range(MICRO):
        row_start = micro_index * per_block
        source_block = source[row_start : row_start + per_block]
        attend_kept, hidden_kept, hidden_low, expand_kept, memory_kept = encoder_kept[micro_index]
        upstream = norm_step(
            own_half(memory_gradient[row_start : row_start + per_block]).astype(jnp.float32),
            1,
            memory_kept,
        )
        upstream = add_branch(upstream, expand_step(low_rows(upstream), hidden_low, 0, expand_kept))
        upstream = norm_step(upstream, 0, hidden_kept)
        asking_piece, key_part = attend_step(
            low_rows(upstream), source_block, source_block, 0, attend_kept
        )
        source_parts.append(identity(add_branch(upstream, asking_piece + key_part)))
    square_grad = jnp.stack(square_grads)
    wide_grad = jnp.stack(wide_grads)
    norm_grad = jnp.stack(gain_grads + bias_grads)
    square_grad, wide_grad, norm_grad = (
        lax.psum_scatter(square_grad, "dp", scatter_dimension=1, tiled=True),
        lax.psum_scatter(wide_grad, "dp", scatter_dimension=1, tiled=True),
        lax.psum_scatter(norm_grad, "dp", scatter_dimension=1, tiled=True),
    )
    row_square, row_wide, norm_grad = lax.psum(
        (
            jnp.sum(square_grad * square_grad, axis=2),
            jnp.sum(wide_grad * wide_grad, axis=2),
            norm_grad,
        ),
        "mp",
    )
    square_rows_new = 0.5 * square_rows + 0.5 * (row_square / model_width)
    wide_rows_new = 0.5 * wide_rows + 0.5 * (row_wide / FF)
    col_square, col_wide, level_square, level_wide = lax.psum(
        (
            jnp.sum(square_grad * square_grad, axis=1),
            jnp.sum(wide_grad * wide_grad, axis=1),
            jnp.sum(square_rows_new, axis=1),
            jnp.sum(wide_rows_new, axis=1),
        ),
        "dp",
    )
    square_cols_new = 0.5 * square_cols + 0.5 * (col_square / model_width)
    wide_cols_new = 0.5 * wide_cols + 0.5 * (col_wide / model_width)
    square_second = (
        square_rows_new[:, :, None]
        * square_cols_new[:, None, :]
        / (level_square / model_width)[:, None, None]
    )
    wide_second = (
        wide_rows_new[:, :, None]
        * wide_cols_new[:, None, :]
        / (level_wide / model_width)[:, None, None]
    )
    updated_square_masters = square_master - RATE * square_grad * lax.rsqrt(square_second)
    wide_new = wide_master - RATE * wide_grad * lax.rsqrt(wide_second)
    norm_second_new = 0.5 * gain_offset_moment + 0.5 * norm_grad * norm_grad
    norm_new = norm_master - NORM_RATE * norm_grad * lax.rsqrt(norm_second_new)
    return (
        jnp.concatenate(decoded_parts, axis=0),
        jnp.concatenate(source_parts, axis=0),
        target_grad,
        square_grad,
        square_rows_new,
        square_cols_new,
        updated_square_masters,
        rounded(updated_square_masters),
        wide_grad,
        wide_rows_new,
        wide_cols_new,
        wide_new,
        rounded(wide_new),
        norm_grad,
        norm_second_new,
        norm_new,
        rounded(norm_new),
    )


SQUARE, WIDE = 0, 1
LANES = 128
TOKENS = 256
BLOCK = 128
CHUNK = 64
MESH_IDS = pl.DeviceIdType.MESH
NEG = -1000000000.0
OUTSIDE = -3.0e38
ENC_UNITS = ((SQUARE, 0), (WIDE, 0), (WIDE, 1))
DEC_UNITS = ((SQUARE, 0), (SQUARE, 1), (WIDE, 0), (WIDE, 1))
ALL_UNITS = ((0, 0), (0, 1), (0, 2), (1, 0), (1, 1), (1, 2), (1, 3))


def mm(a, b):
    return jnp.dot(a, b, preferred_element_type=jnp.float32)


def mm_nt(a, b):
    return lax.dot_general(a, b, (((1,), (1,)), ((), ())), preferred_element_type=jnp.float32)


def mm_tn(a, b):
    return lax.dot_general(a, b, (((0,), (0,)), ((), ())), preferred_element_type=jnp.float32)


def repeat(count, body):
    lax.fori_loop(0, count, lambda i, carry: (body(i), carry)[1], 0)


def aligned(i, size):
    return pl.ds(pl.multiple_of(i * size, size), size)


def unit_mats(role, u):
    kind, i = (ENC_UNITS, DEC_UNITS)[role][u]
    if kind == SQUARE:
        return kind, i, 4 * i + 4 * role
    return kind, i, i + 2 * role


def named(refs, *groups):
    return types.SimpleNamespace(**dict(zip([name for group in groups for name in group], refs)))


class Sems:
    def __init__(self, send, recv, count):
        self.send, self.recv, self.count, self.names = send, recv, count, {}

    def at(self, name):
        i = self.names.setdefault(name, len(self.names))
        assert i < self.count
        return self.send.at[i], self.recv.at[i]


SEM_COUNT = 176
NEAR_COUNT = 16
(
    S_AX,
    S_AY,
    S_COT,
    S_DEC,
    S_DM,
    S_DT,
    S_FX,
    S_FY,
    S_M,
    S_MEMORY,
    S_NG,
    S_NORM,
    S_RA,
    S_RB,
    S_RQ,
    S_SA,
    S_SB,
    S_SG,
    S_SOURCE,
    S_ST,
    S_SU,
    S_NH,
    S_EXT,
    S_SOURCE2,
    S_MEMORY2,
    S_DM2,
    S_DT2,
    S_T,
    S_TARGET,
    S_TT,
    S_Z,
) = range(31)

SCRATCH = dict(
    WS=((8, 4, 2, 2, 32, 256), jnp.bfloat16),
    WW=((2, 4, 2, 2, 32, 1024), jnp.bfloat16),
    GS=((8, 4, 2, 2, 32, 256), jnp.bfloat16),
    GW=((2, 4, 2, 2, 32, 1024), jnp.bfloat16),
    SB=((12, 32, 256), jnp.bfloat16),
    WB=((4, 32, 1024), jnp.bfloat16),
    R1AS=((8, 2, 2, 32, 256), jnp.bfloat16),
    R1BS=((8, 2, 2, 32, 256), jnp.bfloat16),
    R1AW=((2, 2, 2, 32, 1024), jnp.bfloat16),
    R1BW=((2, 2, 2, 32, 1024), jnp.bfloat16),
    R2AS=((8, 2, 32, 256), jnp.bfloat16),
    R2BS=((8, 2, 32, 256), jnp.bfloat16),
    R2AW=((2, 2, 32, 1024), jnp.bfloat16),
    R2BW=((2, 2, 32, 1024), jnp.bfloat16),
    R3S=((2, 12, 32, 256), jnp.bfloat16),
    R3W=((2, 4, 32, 1024), jnp.bfloat16),
    NB=((16, 16, LANES), jnp.bfloat16),
    RL=((16, LANES), jnp.float32),
    NORM=((16, 512), jnp.float32),
    EXT=((BLOCK, LANES), jnp.float32),
    SEXT=((BLOCK, LANES), jnp.bfloat16),
    XHALF=((2, BLOCK, 256), jnp.bfloat16),
    XEXT=((BLOCK, LANES), jnp.bfloat16),
    TSEND=((8, 16, 640), jnp.bfloat16),
    TREC=((16, 16, 640), jnp.bfloat16),
    COT2=((BLOCK, 512), jnp.bfloat16),
    COT=((TOKENS, 512), jnp.float32),
    XT=((TOKENS, 512), jnp.bfloat16),
    MSEND=((8, 2, 16, 512), jnp.bfloat16),
    MREC=((2, 2, 2, 4, 16, 256), jnp.bfloat16),
    MEM=((TOKENS, 512), jnp.bfloat16),
    DMSEND=((2, 2, 4, 16, 512), jnp.bfloat16),
    MG=((2, 8, 2, 16, 256), jnp.bfloat16),
    DTSEND=((16, 16, 512), jnp.bfloat16),
    TG=((2, 8, 16, 256), jnp.bfloat16),
    DSEND=((BLOCK, 512), jnp.bfloat16),
    DREC=((BLOCK, 512), jnp.bfloat16),
    SGSEND=((16, 4, 512), jnp.float32),
    SGREC=((16, 4, 512), jnp.float32),
    PERMT=((2, BLOCK, BLOCK), jnp.bfloat16),
    ALLOW=((2, 2, BLOCK, TOKENS), jnp.float32),
    FILL=((BLOCK, TOKENS), jnp.float32),
    Q=((2, TOKENS, 256), jnp.bfloat16),
    K=((2, TOKENS, 256), jnp.bfloat16),
    V=((2, TOKENS, 256), jnp.bfloat16),
    O=((2, TOKENS, 256), jnp.bfloat16),
    PROB=((2, 4, BLOCK, TOKENS), jnp.float32),
    DO=((TOKENS, 256), jnp.bfloat16),
    DQ=((TOKENS, 256), jnp.bfloat16),
    DK=((TOKENS, 256), jnp.bfloat16),
    DV=((TOKENS, 256), jnp.bfloat16),
    U=((TOKENS, 1024), jnp.float32),
    ACT=((TOKENS, 1024), jnp.bfloat16),
    DU=((TOKENS, 1024), jnp.bfloat16),
    RES=((TOKENS, 512), jnp.float32),
    LOW=((3, TOKENS, 512), jnp.bfloat16),
    XH=((3, TOKENS, 512), jnp.float32),
    RSD=((3, TOKENS, 1), jnp.float32),
    GRAD=((TOKENS, 512), jnp.float32),
    GLOW=((TOKENS, 512), jnp.bfloat16),
    PS=((2, TOKENS, 512), jnp.float32),
    PR=((2, TOKENS, 512), jnp.float32),
    NGR=((4, 16, LANES), jnp.float32),
    NG=((4, 16, LANES), jnp.float32),
    NH=((4, 16, LANES), jnp.float32),
    ST=((7, 4, 8, LANES), jnp.float32),
    SU=((7, 4, 8, LANES), jnp.float32),
    RQ=((BLOCK, LANES), jnp.float32),
    RQR=((BLOCK, LANES), jnp.float32),
    TT=((7, 8, LANES), jnp.float32),
    SM=((12, 32, 256), jnp.float32),
    WM=((4, 32, 1024), jnp.float32),
    SRC=((BLOCK, 512), jnp.bfloat16),
    TGT=((BLOCK, 512), jnp.bfloat16),
    COT1=((BLOCK, 512), jnp.bfloat16),
    F_DEC=((BLOCK, 512), jnp.bfloat16),
    F_SRC=((16, 4, 512), jnp.float32),
    F_TGT=((BLOCK, 512), jnp.float32),
    F_GS=((12, 32, 256), jnp.float32),
    F_GW=((4, 32, 1024), jnp.float32),
    TTR=((7, 8, LANES), jnp.float32),
)

INPUTS = dict(
    lengths=0,
    destinations=0,
    source=0,
    target=0,
    cotangent=0,
    square=0,
    wide=0,
    norm=0,
    square_rows=0,
    wide_rows=0,
)
OUTPUTS = dict(
    o_dec=((BLOCK, 512), jnp.bfloat16),
    o_src=((16, 4, 512), jnp.float32),
    o_tgt=((BLOCK, 512), jnp.float32),
    o_gs=((12, 32, 256), jnp.float32),
    o_gw=((4, 32, 1024), jnp.float32),
    o_cs=((12, 256), jnp.float32),
    o_cw=((4, 1024), jnp.float32),
    o_rq=((BLOCK, LANES), jnp.float32),
    o_rl=((16, LANES), jnp.float32),
    o_tt=((7, 8, LANES), jnp.float32),
    o_ng=((16, LANES), jnp.float32),
)


def exchange_kernel(*refs):
    r = named(refs, INPUTS, OUTPUTS, SCRATCH)
    sems = Sems(refs[-3], refs[-2], SEM_COUNT)
    near = refs[-1]
    d = lax.axis_index("dp")
    c = lax.axis_index("mp")
    z = lax.div(d, 4)
    yx = lax.rem(d, 4)
    y = lax.div(yx, 2)
    x = lax.rem(yx, 2)
    role = lax.rem(z, 2)
    x_mate = d + 1 - 2 * x
    y_mate = d + 2 - 4 * y
    partner = d + 4 - 8 * role
    bf, f32 = jnp.bfloat16, jnp.float32

    G = (r.GS, r.GW)
    R1A, R1B = (r.R1AS, r.R1AW), (r.R1BS, r.R1BW)
    R2A, R2B = (r.R2AS, r.R2AW), (r.R2BS, r.R2BW)

    def z_mate(k):
        zz = lax.rem(z + k, 4)
        return zz, zz * 4 + yx

    def copy(src, dst, name, dev, core=None):
        send, recv = sems.at(name)
        return pltpu.make_async_remote_copy(
            src_ref=src,
            dst_ref=dst,
            send_sem=send,
            recv_sem=recv,
            device_id=(dev, c if core is None else core),
            device_id_type=MESH_IDS,
        )

    def local(src, dst, i):
        return pltpu.make_async_copy(src, dst, near.at[i])

    my_half = pl.ds(pl.multiple_of(c * 256, 256), 256)

    def hand_over(ref, name):
        copy(ref.at[c], ref.at[c], name, d, 1 - c).start()
        wait_in(ref.at[0], name)
        wait_out(ref.at[0], name)

    def plane_mates():
        return (x_mate, y_mate, z * 4 + 3 - yx)

    def in_order(ref, lead=()):
        total = ref[lead + (0,)]
        for i in range(1, 4):
            total = total + ref[lead + (i,)]
        return total

    def wait_in(dst, name):
        copy(dst, dst, name, x_mate).wait_recv()

    def wait_out(src, name):
        copy(src, src, name, x_mate).wait_send()

    def unit(buf, kind, i):
        if kind == SQUARE:
            return buf[0], (slice(4 * i, 4 * i + 4),)
        return buf[1], (i,)

    def part(buf, kind, i, *rest):
        ref, lead = unit(buf, kind, i)
        return ref.at[lead + rest]

    loads = [
        local(r.target, r.TGT, 0),
        local(r.source, r.SRC, 1),
        local(r.square, r.SM, 2),
        local(r.wide, r.WM, 3),
        local(r.cotangent, r.COT1, 4),
    ]
    for load in loads:
        load.start()
    barrier = pltpu.get_barrier_semaphore()
    for k in range(1, 16):
        pl.semaphore_signal(
            barrier, inc=1, device_id=(lax.rem(d + k, 16), c), device_id_type=MESH_IDS
        )
    pl.semaphore_signal(barrier, inc=1, device_id=(d, 1 - c), device_id_type=MESH_IDS)

    lane = lax.broadcasted_iota(jnp.int32, (8, LANES), 1)
    for s in range(16):
        r.EXT[8 * s : 8 * s + 8, :] = jnp.where(
            lane < 32,
            r.lengths[0, s],
            jnp.where(lane < 64, r.lengths[1, s], r.destinations[s]),
        ).astype(f32)
    ext_low = r.EXT[...].astype(bf)
    r.SEXT[...] = ext_low

    row_id = lax.broadcasted_iota(jnp.int32, (BLOCK, BLOCK), 0)
    col_id = lax.broadcasted_iota(jnp.int32, (BLOCK, BLOCK), 1)
    col_z = 2 * (col_id >> 6) + 1 - ((col_id >> 3) & 1)
    col_dev = (col_z * 4 + ((col_id >> 4) & 3)).astype(f32)
    same_slot = (row_id & 7) == (col_id & 7)

    def perm_of(dest_column):
        return jnp.where((dest_column == col_dev) & same_slot, 1.0, 0.0)

    perm_f = perm_of(r.EXT[:, 64:65])
    r.PERMT[0] = perm_f.astype(bf)
    perm = perm_f.T.astype(bf)
    loads[0].wait()
    r.TSEND[:, :, 0:512] = mm(perm, r.TGT[...]).astype(bf).reshape(8, 16, 512)
    r.TSEND[:, :, 512:640] = mm(perm, ext_low).astype(bf).reshape(8, 16, LANES)

    r.NORM[...] = jnp.zeros((16, 512), f32)
    r.NORM[0:10, 0:32] = r.norm[...]
    shift = lax.rem(d, 4) * 32
    r.NB[d] = pltpu.roll(r.NORM[:, 0:LANES], shift, 1).astype(bf)
    r.RL[...] = jnp.zeros((16, LANES), f32)
    r.RL[0:12, 0:32] = r.square_rows[...]
    r.RL[12:16, 0:32] = r.wide_rows[...]

    loads[1].wait()
    loads[2].wait()
    loads[3].wait()
    for j in range(12):
        r.SB[j] = r.SM[j].astype(bf)
    for j in range(4):
        r.WB[j] = r.WM[j].astype(bf)

    def own_weights(first_s, count, first_w):
        for j in range(count):
            r.WS[j, z, y, x] = r.SB[first_s + j]
        for j in range(2):
            r.WW[j, z, y, x] = r.WB[first_w + j]

    pl.when(role == 0)(lambda: own_weights(0, 4, 0))
    pl.when(role == 1)(lambda: own_weights(4, 8, 2))

    loads[4].wait()
    pl.semaphore_wait(barrier, 16)

    def z_slot(kind, i, k=0, yy=None, xx=None):
        zz = lax.rem(z + 4 - k, 4)
        at = (zz, y if yy is None else yy, x if xx is None else xx)
        if kind == SQUARE:
            return r.WS.at[(slice(4 * i, 4 * i + 4),) + at]
        return r.WW.at[(i,) + at]

    def z_send(my_role, target_role, u):
        kind, i, j = unit_mats(target_role, u)
        src = r.SB.at[j : j + 4] if kind == SQUARE else r.WB.at[j]
        for k in (2,) if my_role == target_role else (1, 3):
            copy(src, z_slot(kind, i), (S_Z, u, k), z_mate(k)[1]).start()

    def z_sent(my_role):
        for target_role, u in ALL_UNITS:
            kind, i, j = unit_mats(target_role, u)
            src = r.SB.at[j : j + 4] if kind == SQUARE else r.WB.at[j]
            for k in (2,) if my_role == target_role else (1, 3):
                wait_out(src, (S_Z, u, k))

    def send_norms():
        for k in range(1, 16):
            dev = lax.rem(d + k, 16)
            copy(r.NB.at[d], r.NB.at[d], S_NORM, dev).start()

    def send_target(my_role):
        for t in range(8):
            dev = (2 * (t // 4) + 1) * 4 + t % 4
            send = copy(r.TSEND.at[t], r.TREC.at[d], S_TARGET, dev)
            if my_role == 0:
                send.start()
            else:
                pl.when(dev != d)(send.start)

                @pl.when(dev == d)
                def _():
                    r.TREC[d] = r.TSEND[t]

    def ag_own(units):
        for u, (kind, i) in enumerate(units):
            ag_plane(kind, i, u, 0)

    def ag_plane(kind, i, u, k):
        block = z_slot(kind, i, k)
        copy(block, block, (S_AX, u, k), x_mate).start()
        copy(block, block, (S_AY, u, k), y_mate).start()

    def ag_column(units, u):
        kind, i = units[u]
        for k in (1, 3, 2):
            wait_in(z_slot(kind, i), (S_Z, u, k))
            ag_plane(kind, i, u, k)

    def ag_forward(units, u):
        kind, i = units[u]
        for k in (0, 1, 3, 2):
            if k < 2:
                wait_in(z_slot(kind, i), (S_AY, u, k))
                block = z_slot(kind, i, k, yy=1 - y)
                copy(block, block, (S_FX, u, k), x_mate).start()
            else:
                wait_in(z_slot(kind, i), (S_AX, u, k))
                block = z_slot(kind, i, k, xx=1 - x)
                copy(block, block, (S_FY, u, k), y_mate).start()

    def ag_finish(units, u):
        kind, i = units[u]
        block = z_slot(kind, i)
        for k in (0, 1, 3, 2):
            wait_in(block, (S_AX if k < 2 else S_AY, u, k))
            wait_in(block, (S_FX if k < 2 else S_FY, u, k))

    def ag_sent(units):
        for u, (kind, i) in enumerate(units):
            block = z_slot(kind, i)
            for k in range(4):
                wait_out(block, (S_AX, u, k))
                wait_out(block, (S_AY, u, k))
                wait_out(block, (S_FX if k < 2 else S_FY, u, k))

    def rs_first(units, u):
        kind, i = units[u]
        gref, lead = unit(G, kind, i)
        copy(
            gref.at[lead + (slice(0, 2), 1 - y)], part(R1A, kind, i), (S_RA, u), y_mate
        ).start()
        copy(
            gref.at[lead + (slice(2, 4), slice(None), 1 - x)],
            part(R1B, kind, i),
            (S_RB, u),
            x_mate,
        ).start()

    def add_into(ref, index, other):
        ref[index] = (ref[index].astype(f32) + other[...].astype(f32)).astype(bf)

    def rs_second(units, u):
        kind, i = units[u]
        gref, lead = unit(G, kind, i)
        ra, rb = part(R1A, kind, i), part(R1B, kind, i)
        wait_in(ra, (S_RA, u))
        add_into(gref, lead + (slice(0, 2), y), ra)
        copy(
            gref.at[lead + (slice(0, 2), y, 1 - x)], part(R2A, kind, i), (S_SA, u), x_mate
        ).start()
        wait_in(rb, (S_RB, u))
        add_into(gref, lead + (slice(2, 4), slice(None), x), rb)
        copy(
            gref.at[lead + (slice(2, 4), 1 - y, x)], part(R2B, kind, i), (S_SB, u), y_mate
        ).start()

    def rs_third(my_role, units, u):
        kind, i, j = unit_mats(my_role, u)
        gref, lead = unit(G, kind, i)
        ra, rb = part(R2A, kind, i), part(R2B, kind, i)
        wait_in(ra, (S_SA, u))
        add_into(gref, lead + (slice(0, 2), y, x), ra)
        wait_in(rb, (S_SB, u))
        add_into(gref, lead + (slice(2, 4), y, x), rb)
        for k in (1, 2, 3):
            slot = 1 if k == 3 else 0
            zz, dev = z_mate(k)
            if kind == SQUARE:
                dst = r.R3S.at[slot, j : j + 4]
            else:
                dst = r.R3W.at[slot, j]
            copy(gref.at[lead + (zz, y, x)], dst, (S_T, my_role, u, slot, k & 1), dev).start()

    def rs_sent(my_role, units):
        for u, (kind, i) in enumerate(units):
            gref, lead = unit(G, kind, i)
            wait_out(part(R1A, kind, i), (S_RA, u))
            wait_out(part(R1B, kind, i), (S_RB, u))
            wait_out(part(R2A, kind, i), (S_SA, u))
            wait_out(part(R2B, kind, i), (S_SB, u))
            for k in (1, 2, 3):
                slot = 1 if k == 3 else 0
                wait_out(gref.at[lead + (0, y, x)], (S_T, my_role, u, slot, k & 1))

    def final_sum(my_role, role_of, u):
        kind, i, j = unit_mats(role_of, u)
        if kind == SQUARE:
            dst = [r.R3S.at[slot, j : j + 4] for slot in (0, 1)]
        else:
            dst = [r.R3W.at[slot, j] for slot in (0, 1)]
        if my_role == role_of:
            wait_in(dst[0], (S_T, role_of, u, 0, 0))
            gref, lead = unit(G, kind, i)
            total = gref[lead + (z, y, x)].astype(f32) + dst[0][...].astype(f32)
        else:
            wait_in(dst[0], (S_T, role_of, u, 0, 1))
            wait_in(dst[1], (S_T, role_of, u, 1, 1))
            total = dst[0][...].astype(f32) + dst[1][...].astype(f32)
        if kind == SQUARE:
            r.F_GS[j : j + 4] = total
        else:
            r.F_GW[j] = total

    def unit_stats(g):
        role_of, u = ALL_UNITS[g]
        kind, i, j = unit_mats(role_of, u)
        lanes = lax.broadcasted_iota(jnp.int32, (32, LANES), 1)
        rows = r.RQ[0:32, :]
        if kind == SQUARE:
            for m in range(4):
                grad = r.F_GS[j + m]
                sq = grad * grad
                cols = jnp.sum(sq, axis=0, keepdims=True)
                for h in range(2):
                    r.ST[g, z, 2 * m + h : 2 * m + h + 1, :] = cols[:, h * LANES : (h + 1) * LANES]
                rows = jnp.where(lanes == j + m, jnp.sum(sq, axis=1, keepdims=True), rows)
        else:
            grad = r.F_GW[j]
            sq = grad * grad
            cols = jnp.sum(sq, axis=0, keepdims=True)
            for h in range(8):
                r.ST[g, z, h : h + 1, :] = cols[:, h * LANES : (h + 1) * LANES]
            rows = jnp.where(lanes == 12 + j, jnp.sum(sq, axis=1, keepdims=True), rows)
        r.RQ[0:32, :] = rows
        for k in (1, 2, 3):
            copy(r.ST.at[g, z], r.ST.at[g, z], (S_ST, g), z_mate(k)[1]).start()

    def spread_unit(g):
        wait_in(r.ST.at[g, 0:3], (S_ST, g))
        r.SU[g, yx] = in_order(r.ST, (g,))
        for dev in plane_mates():
            copy(r.SU.at[g, yx], r.SU.at[g, yx], (S_SU, g), dev).start()

    def store_unit(g):
        kind, i, j = unit_mats(*ALL_UNITS[g])
        if kind == SQUARE:
            return local(r.F_GS.at[j : j + 4], r.o_gs.at[j : j + 4], 8 + g)
        return local(r.F_GW.at[j], r.o_gw.at[j], 8 + g)

    def finish_unit(my_role, g):
        final_sum(my_role, *ALL_UNITS[g])
        store_unit(g).start()
        unit_stats(g)

    def weight(kind, i, cols=None):
        if kind == SQUARE:
            return r.WS[i].reshape(512, 256)
        if cols is None:
            return r.WW[i].reshape(512, 1024)
        return r.WW[i, :, :, :, :, cols].reshape(512, 256)

    def put_square(i, value):
        r.GS[i] = value.astype(bf).reshape(4, 2, 2, 32, 256)

    def swap(number, partial):
        slot = number % 2
        for half in range(2):
            rows = slice(half * BLOCK, (half + 1) * BLOCK)
            if number >= 2:
                wait_out(r.PS.at[slot, rows], (S_M, number - 2, half))
            r.PS[slot, rows] = partial(rows)
            copy(
                r.PS.at[slot, rows], r.PR.at[slot, rows], (S_M, number, half), d, 1 - c
            ).start()

    def swapped(number, body):
        slot = number % 2
        for half in range(2):
            rows = slice(half * BLOCK, (half + 1) * BLOCK)
            wait_in(r.PR.at[slot, rows], (S_M, number, half))

            def chunk(i):
                at = pl.ds(pl.multiple_of(half * BLOCK + i * CHUNK, CHUNK), CHUNK)
                body(at, half * (BLOCK // CHUNK) + i, r.PS[slot, at] + r.PR[slot, at])

            repeat(BLOCK // CHUNK, chunk)

    def swaps_sent(count):
        for number in (count - 2, count - 1):
            for half in range(2):
                wait_out(r.PS.at[0, 0:BLOCK], (S_M, number, half))

    def norm_forward(residual, kept, which, at):
        centred = residual - jnp.mean(residual, axis=-1, keepdims=True)
        spread = lax.rsqrt(jnp.mean(centred * centred, axis=-1, keepdims=True) + 1e-05)
        normed = centred * spread
        r.XH[kept, at] = normed
        r.RSD[kept, at] = spread
        return normed * r.NORM[which : which + 1, :] + r.NORM[5 + which : 6 + which, :]

    def norm_backward(upstream, kept, which, at):
        normed = r.XH[kept, at]
        scaled = upstream * r.NORM[which : which + 1, :]
        both = upstream * normed
        gain_sum = jnp.sum(both, axis=0, keepdims=True)
        bias_sum = jnp.sum(upstream, axis=0, keepdims=True)
        for b in range(4):
            lanes = slice(b * LANES, (b + 1) * LANES)
            r.NGR[b, which : which + 1, :] += gain_sum[:, lanes]
            r.NGR[b, 5 + which : 6 + which, :] += bias_sum[:, lanes]
        return r.RSD[kept, at] * (
            scaled
            - jnp.mean(scaled, axis=-1, keepdims=True)
            - normed * jnp.mean(scaled * normed, axis=-1, keepdims=True)
        )

    head_lane = lax.broadcasted_iota(jnp.int32, (1, LANES), 1)
    first_head = jnp.where(head_lane < 64, 1.0, 0.0)
    second_head = 1.0 - first_head

    def stacked(value):
        wide_value = value.astype(f32)
        return jnp.concatenate([wide_value * first_head, wide_value * second_head], axis=0).astype(bf)

    def unstacked(value):
        return value[0:BLOCK] * first_head + value[BLOCK:] * second_head

    def pairs(body):
        for blk in range(2):
            for pr in range(2):
                body(blk, slice(blk * BLOCK, (blk + 1) * BLOCK), slice(pr * LANES, (pr + 1) * LANES), 2 * blk + pr)

    def make_masks(slot, count_of, causal):
        row = lax.broadcasted_iota(jnp.int32, (BLOCK, TOKENS), 0)
        col = lax.broadcasted_iota(jnp.int32, (BLOCK, TOKENS), 1) & (BLOCK - 1)
        same = (row >> 3) == (col >> 3)
        r.FILL[...] = jnp.where(same, NEG, OUTSIDE)
        for blk in range(2):
            ok = same & ((col & 7).astype(f32) < count_of(blk))
            if causal:
                ok = ok & ((col & 7) <= (row & 7))
            r.ALLOW[slot, blk] = jnp.where(ok, 1.0, 0.0)

    def attend(kept, mask_slot):
        def one(blk, rows, lanes, n):
            keys = stacked(r.K[kept, rows, lanes])
            scores = mm_nt(r.Q[kept, rows, lanes], keys) * 0.125
            scores = jnp.where(r.ALLOW[mask_slot, blk] > 0.5, scores, r.FILL[...])
            halves = []
            for h in range(2):
                s = scores[:, h * BLOCK : (h + 1) * BLOCK]
                e = jnp.exp(s - jnp.max(s, axis=-1, keepdims=True))
                halves.append(e / jnp.sum(e, axis=-1, keepdims=True))
            probs = jnp.concatenate(halves, axis=1)
            r.PROB[kept, n] = probs
            r.O[kept, rows, lanes] = mm(
                probs.astype(bf), stacked(r.V[kept, rows, lanes])
            ).astype(bf)

        pairs(one)

    def attend_back(kept):
        def one(blk, rows, lanes, n):
            queries = r.Q[kept, rows, lanes]
            keys = stacked(r.K[kept, rows, lanes])
            values = stacked(r.V[kept, rows, lanes])
            out_grad = r.DO[rows, lanes]
            probs = r.PROB[kept, n]
            weighted = probs * mm_nt(out_grad, values)
            halves = []
            for h in range(2):
                w = weighted[:, h * BLOCK : (h + 1) * BLOCK]
                p = probs[:, h * BLOCK : (h + 1) * BLOCK]
                halves.append(w - p * jnp.sum(w, axis=-1, keepdims=True))
            score_grad = jnp.concatenate(halves, axis=1).astype(bf)
            r.DQ[rows, lanes] = (mm(score_grad, keys) * 0.125).astype(bf)
            r.DK[rows, lanes] = (unstacked(mm_tn(score_grad, queries)) * 0.125).astype(bf)
            r.DV[rows, lanes] = unstacked(mm_tn(probs.astype(bf), out_grad)).astype(bf)

        pairs(one)

    def project_all(kept, base, queries, keys):
        r.Q[kept] = mm(queries, weight(SQUARE, base)).astype(bf)
        r.K[kept] = mm(keys, weight(SQUARE, base + 1)).astype(bf)
        r.V[kept] = mm(keys, weight(SQUARE, base + 2)).astype(bf)

    def attention_out(kept, base):
        return lambda rows: mm_nt(r.O[kept, rows], weight(SQUARE, base + 3))

    def attention_back_start(kept, base):
        upstream = r.GLOW[...]
        put_square(base + 3, mm_tn(upstream, r.O[kept]))
        r.DO[...] = mm(upstream, weight(SQUARE, base + 3)).astype(bf)
        attend_back(kept)

    def attention_grads(base, queries, keys):
        put_square(base, mm_tn(queries, r.DQ[...]))
        put_square(base + 1, mm_tn(keys, r.DK[...]))
        put_square(base + 2, mm_tn(keys, r.DV[...]))

    def query_side(base):
        return lambda rows: mm_nt(r.DQ[rows], weight(SQUARE, base))

    def key_side(base):
        return lambda rows: mm_nt(r.DK[rows], weight(SQUARE, base + 1)) + mm_nt(
            r.DV[rows], weight(SQUARE, base + 2)
        )

    def all_sides(base):
        return lambda rows: query_side(base)(rows) + key_side(base)(rows)

    def expand(inputs):
        def one(n):
            cols = aligned(n, 256)
            hidden = mm(inputs, weight(WIDE, 0, cols))
            r.U[:, cols] = hidden
            bent = jnp.tanh(0.7978845608 * (hidden + 0.044715 * hidden * hidden * hidden))
            r.ACT[:, cols] = (0.5 * hidden * (1.0 + bent)).astype(bf)

        repeat(4, one)

    def contract(rows):
        return mm_nt(r.ACT[rows], weight(WIDE, 1))

    def expand_back_down():
        upstream = r.GLOW[...]

        def one(n):
            cols = aligned(n, 256)
            r.GW[1, :, :, :, :, cols] = (
                mm_tn(upstream, r.ACT[:, cols]).astype(bf).reshape(4, 2, 2, 32, 256)
            )

        repeat(4, one)

    def expand_back_up(inputs):
        upstream = r.GLOW[...]

        def one(n):
            cols = aligned(n, 256)
            active_grad = mm(upstream, weight(WIDE, 1, cols)).astype(bf).astype(f32)
            hidden = r.U[:, cols]
            square = hidden * hidden
            bent = jnp.tanh(0.7978845608 * (hidden + 0.044715 * hidden * square))
            slope = 0.5 * (1.0 + bent) + 0.5 * hidden * (1.0 - bent * bent) * 0.7978845608 * (
                1.0 + 3.0 * 0.044715 * square
            )
            hidden_grad = (active_grad * slope).astype(bf)
            r.DU[:, cols] = hidden_grad
            r.GW[0, :, :, :, :, cols] = (
                mm_tn(inputs, hidden_grad).astype(bf).reshape(4, 2, 2, 32, 256)
            )

        repeat(4, one)

    def expand_input(rows):
        return mm_nt(r.DU[rows], weight(WIDE, 0))

    def clear_sums():
        r.NGR[...] = jnp.zeros((4, 16, LANES), f32)
        sums = jnp.sum(r.RL[...], axis=1, keepdims=True)
        rows = lax.broadcasted_iota(jnp.int32, (16, LANES), 0)
        lanes = lax.broadcasted_iota(jnp.int32, (16, LANES), 1)
        line = jnp.sum(jnp.where(rows == lanes, sums, 0.0), axis=0, keepdims=True)
        for b in range(4):
            r.NGR[b, 10:11, :] = line
        r.RQ[...] = jnp.zeros((BLOCK, LANES), f32)

    def read_norms():
        wait_in(r.NB.at[0:15], S_NORM)
        for b in range(4):
            total = r.NB[4 * b].astype(f32)
            for i in range(1, 4):
                total = total + r.NB[4 * b + i].astype(f32)
            r.NORM[:, b * LANES : (b + 1) * LANES] = total

    def encoder():
        units = ENC_UNITS
        for u in range(3):
            z_send(0, 0, u)
        ag_own(units)
        send_norms()
        z_send(0, 1, 0)
        z_send(0, 1, 1)
        send_target(0)
        z_send(0, 1, 2)
        z_send(0, 1, 3)
        copy(r.COT1, r.COT2, S_COT, partner).start()
        clear_sums()
        ag_column(units, 0)
        ag_forward(units, 0)
        ag_column(units, 1)
        wait_in(r.XEXT, S_EXT)
        wait_in(r.XHALF.at[0], S_SOURCE)
        hand_over(r.XHALF, S_SOURCE2)
        r.XT[0:BLOCK] = r.SRC[...]
        for half in range(2):
            r.XT[BLOCK:, half * 256 : half * 256 + 256] = r.XHALF[half]
        def counts(blk):
            return r.EXT[:, 0:1] if blk == 0 else r.XEXT[...].astype(f32)[:, 0:1]

        make_masks(0, counts, False)
        r.PERMT[1] = perm_of(r.XEXT[...].astype(f32)[:, 64:65]).astype(bf)
        read_norms()
        ag_column(units, 2)
        ag_finish(units, 0)
        x_in = r.XT[...]
        project_all(0, 0, x_in, x_in)
        attend(0, 0)
        swap(0, attention_out(0, 0))
        ag_forward(units, 1)

        def first(at, n, total):
            hidden = norm_forward(r.XT[at].astype(f32) + total, 0, 0, at)
            r.RES[at] = hidden
            r.LOW[0, at] = hidden.astype(bf)

        swapped(0, first)
        ag_finish(units, 1)
        expand(r.LOW[0])
        ag_forward(units, 2)
        ag_finish(units, 2)
        swap(1, contract)

        def second(at, n, total):
            r.LOW[1, at] = norm_forward(r.RES[at] + total, 1, 1, at).astype(bf)

        swapped(1, second)
        for jj in range(2):
            block = r.LOW[1, jj * BLOCK : (jj + 1) * BLOCK]
            r.MSEND[:, jj] = mm_tn(r.PERMT[jj], block).astype(bf).reshape(8, 16, 512)
        zz = lax.div(z, 2)
        for t in range(8):
            dev = (2 * (t // 4) + 1) * 4 + t % 4
            copy(
                r.MSEND.at[t, :, :, my_half], r.MREC.at[c, zz, :, yx], S_MEMORY, dev
            ).start()

        wait_in(r.DREC, S_DEC)
        r.F_DEC[...] = r.DREC[...]
        local(r.F_DEC, r.o_dec, 5).start()
        wait_in(r.MG.at[0], S_DM)
        hand_over(r.MG, S_DM2)
        for jj in range(2):
            for half in range(2):
                r.GRAD[jj * BLOCK : (jj + 1) * BLOCK, half * 256 : half * 256 + 256] = mm(
                    r.PERMT[jj], r.MG[half, :, jj].reshape(BLOCK, 256)
                )

        def back_one(i):
            at = aligned(i, CHUNK)
            value = norm_backward(r.GRAD[at], 1, 1, at)
            r.GRAD[at] = value
            r.GLOW[at] = value.astype(bf)

        repeat(TOKENS // CHUNK, back_one)
        expand_back_down()
        rs_first(units, 2)
        expand_back_up(r.LOW[0])
        rs_first(units, 1)
        swap(2, expand_input)

        def back_two(at, n, total):
            value = norm_backward(r.GRAD[at] + total, 0, 0, at)
            r.GRAD[at] = value
            r.GLOW[at] = value.astype(bf)

        swapped(2, back_two)
        attention_back_start(0, 0)
        attention_grads(0, r.XT[...], r.XT[...])
        rs_first(units, 0)
        swap(3, all_sides(0))
        rs_second(units, 2)

        def back_three(at, n, total):
            r.GRAD[at] = r.GRAD[at] + total

        swapped(3, back_three)
        for target_ref, value in ((r.F_SRC, r.GRAD[0:BLOCK]), (r.SGSEND, r.GRAD[BLOCK:])):
            value = value.reshape(16, 8, 512)
            target_ref[...] = jnp.where(c == 0, value[:, 0:4], value[:, 4:8])
        local(r.F_SRC, r.o_src, 6).start()
        copy(r.SGSEND, r.SGREC, S_SG, partner).start()
        send_norm_sums()
        finish_unit(0, 6)
        take_target(0)
        rs_second(units, 1)
        rs_third(0, units, 2)
        finish_unit(0, 5)
        rs_second(units, 0)
        finish_unit(0, 4)
        rs_third(0, units, 1)
        finish_unit(0, 2)
        finish_unit(0, 3)
        rs_third(0, units, 0)
        wait_out(r.MREC.at[0], S_MEMORY)
        wait_out(r.SGSEND, S_SG)
        swaps_sent(4)
        spread_norm_sums()
        for g in (6, 5, 4):
            spread_unit(g)
        finish_unit(0, 1)
        spread_unit(2)
        spread_unit(3)
        finish_unit(0, 0)
        spread_unit(1)
        spread_unit(0)
        ag_sent(units)
        rs_sent(0, units)
        z_sent(0)
        wait_out(r.NB.at[0:15], S_NORM)
        wait_out(r.COT1, S_COT)
        wait_out(r.TSEND, S_TARGET)

    def send_norm_sums():
        r.NG[z] = r.NGR[z]
        for k in (1, 2, 3):
            zz, dev = z_mate(k)
            copy(r.NGR.at[zz], r.NG.at[z], S_NG, dev).start()

    def spread_norm_sums():
        wait_in(r.NG.at[0:3], S_NG)
        r.NH[yx] = in_order(r.NG)
        for dev in plane_mates():
            copy(r.NH.at[yx], r.NH.at[yx], S_NH, dev).start()

    def take_target(my_role):
        if my_role == 0:
            wait_in(r.TG.at[0], S_DT)
        else:
            wait_in(r.TG.at[0, 0:7], S_DT)
        hand_over(r.TG, S_DT2)
        for half in range(2):
            r.F_TGT[:, half * 256 : half * 256 + 256] = mm(
                r.PERMT[0], r.TG[half].reshape(BLOCK, 256)
            )
        local(r.F_TGT, r.o_tgt, 7).start()

    def decoder():
        units = DEC_UNITS
        z_send(1, 0, 0)
        copy(r.SRC.at[:, my_half], r.XHALF.at[c], S_SOURCE, partner).start()
        copy(r.SEXT, r.XEXT, S_EXT, partner).start()
        z_send(1, 0, 1)
        z_send(1, 0, 2)
        ag_own(units)
        send_norms()
        for u in range(2):
            z_send(1, 1, u)
        send_target(1)
        for u in range(2, 4):
            z_send(1, 1, u)
        clear_sums()
        ag_column(units, 0)
        ag_forward(units, 0)
        ag_column(units, 1)
        ag_forward(units, 1)
        wait_in(r.TREC.at[0:15], S_TARGET)
        cot = r.COT

        def place(i):
            at = aligned(i, 32)
            both = jnp.concatenate(
                [
                    r.COT1[at].astype(f32).reshape(4, 1, 8, 512),
                    r.COT2[at].astype(f32).reshape(4, 1, 8, 512),
                ],
                axis=1,
            )
            cot[aligned(i, CHUNK)] = both.reshape(CHUNK, 512)

        r.XT[...] = r.TREC[:, :, 0:512].reshape(TOKENS, 512)

        def counts(which):
            def get(blk):
                ext = r.TREC[8 * blk : 8 * blk + 8, :, 512:640].reshape(BLOCK, LANES)
                return ext.astype(f32)[:, 32 * which : 32 * which + 1]

            return get

        make_masks(0, counts(1), True)
        make_masks(1, counts(0), False)
        read_norms()
        ag_column(units, 2)
        ag_column(units, 3)
        ag_finish(units, 0)
        x_in = r.XT[...]
        project_all(0, 0, x_in, x_in)
        attend(0, 0)
        swap(0, attention_out(0, 0))
        ag_forward(units, 2)

        def first(at, n, total):
            hidden = norm_forward(r.XT[at].astype(f32) + total, 0, 2, at)
            r.RES[at] = hidden
            r.LOW[0, at] = hidden.astype(bf)

        swapped(0, first)
        ag_forward(units, 3)
        ag_finish(units, 1)
        wait_in(r.COT2, S_COT)
        repeat(4, place)
        r.Q[1] = mm(r.LOW[0], weight(SQUARE, 4)).astype(bf)
        wait_in(r.MREC.at[0], S_MEMORY)
        hand_over(r.MREC, S_MEMORY2)
        for half in range(2):
            r.MEM[:, half * 256 : half * 256 + 256] = r.MREC[half].reshape(TOKENS, 256)
        memory = r.MEM[...]
        r.K[1] = mm(memory, weight(SQUARE, 5)).astype(bf)
        r.V[1] = mm(memory, weight(SQUARE, 6)).astype(bf)
        attend(1, 1)
        swap(1, attention_out(1, 4))

        def second(at, n, total):
            hidden = norm_forward(r.RES[at] + total, 1, 3, at)
            r.RES[at] = hidden
            r.LOW[1, at] = hidden.astype(bf)

        swapped(1, second)
        ag_finish(units, 2)
        expand(r.LOW[1])
        ag_finish(units, 3)
        swap(2, contract)

        def third(at, n, total):
            out = norm_forward(r.RES[at] + total, 2, 4, at)
            rows = aligned(n, 32)
            split = out.reshape(4, 2, 8, 512)
            r.F_DEC[rows] = split[:, 0].reshape(32, 512).astype(bf)
            r.DSEND[rows] = split[:, 1].reshape(32, 512).astype(bf)
            value = norm_backward(cot[at], 2, 4, at)
            r.GRAD[at] = value
            r.GLOW[at] = value.astype(bf)

        swapped(2, third)
        expand_back_down()
        rs_first(units, 3)
        copy(r.DSEND, r.DREC, S_DEC, partner).start()
        local(r.F_DEC, r.o_dec, 5).start()
        expand_back_up(r.LOW[1])
        rs_first(units, 2)
        swap(3, expand_input)

        def back_two(at, n, total):
            value = norm_backward(r.GRAD[at] + total, 1, 3, at)
            r.GRAD[at] = value
            r.GLOW[at] = value.astype(bf)

        swapped(3, back_two)
        attention_back_start(1, 4)
        swap(4, key_side(4))
        attention_grads(4, r.LOW[0], r.MEM[...])

        def back_memory(at, n, total):
            r.LOW[2, at] = total.astype(bf)

        swapped(4, back_memory)
        r.DMSEND[...] = r.LOW[2].reshape(2, 2, 4, 16, 512)
        my_t = lax.div(z, 2) * 4 + yx
        for t in range(8):
            dev = (2 * (t // 4)) * 4 + t % 4
            copy(
                r.DMSEND.at[t // 4, :, t % 4, :, my_half], r.MG.at[c, my_t], S_DM, dev
            ).start()
        rs_first(units, 1)
        swap(5, query_side(4))
        rs_second(units, 3)

        def back_three(at, n, total):
            value = norm_backward(r.GRAD[at] + total, 0, 2, at)
            r.GRAD[at] = value
            r.GLOW[at] = value.astype(bf)

        swapped(5, back_three)
        attention_back_start(0, 0)
        attention_grads(0, r.XT[...], r.XT[...])
        rs_first(units, 0)
        swap(6, all_sides(0))
        rs_second(units, 2)

        def back_four(at, n, total):
            r.DTSEND[aligned(n, 4)] = (
                (r.GRAD[at] + total).astype(bf).reshape(4, 16, 512)
            )

        swapped(6, back_four)
        for k in range(1, 16):
            dev = lax.rem(d + k, 16)
            copy(r.DTSEND.at[dev, :, my_half], r.TG.at[c, my_t], S_DT, dev).start()
        r.TG[c, my_t] = r.DTSEND[d, :, my_half]
        send_norm_sums()
        rs_third(1, units, 3)
        rs_second(units, 1)
        rs_third(1, units, 2)
        finish_unit(1, 6)
        rs_second(units, 0)
        rs_third(1, units, 1)
        finish_unit(1, 5)
        take_target(1)
        rs_third(1, units, 0)
        finish_unit(1, 4)
        finish_unit(1, 2)
        wait_in(r.SGREC, S_SG)
        r.F_SRC[...] = r.SGREC[...]
        local(r.F_SRC, r.o_src, 6).start()
        wait_out(r.DTSEND.at[0:15, :, 0:256], S_DT)
        wait_out(r.MG.at[0], S_DM)
        wait_out(r.DSEND, S_DEC)
        swaps_sent(7)
        spread_norm_sums()
        for g in (6, 5, 4):
            spread_unit(g)
        finish_unit(1, 3)
        finish_unit(1, 1)
        spread_unit(2)
        spread_unit(3)
        finish_unit(1, 0)
        spread_unit(1)
        spread_unit(0)
        ag_sent(units)
        rs_sent(1, units)
        z_sent(1)
        wait_out(r.NB.at[0:15], S_NORM)
        wait_out(r.SEXT, S_EXT)
        wait_out(r.XHALF.at[0], S_SOURCE)
        wait_out(r.TSEND.at[0:7], S_TARGET)

    pl.when(role == 0)(encoder)
    pl.when(role == 1)(decoder)

    copy(r.RQ, r.RQR, S_RQ, d, 1 - c).start()
    wait_in(r.NH.at[0:3], S_NH)
    total = in_order(r.NH)
    r.o_ng[...] = pltpu.roll(total, lax.rem(LANES - shift, LANES), 1)
    r.o_rl[...] = total
    for g in (6, 5, 4, 2, 3, 1, 0):
        wait_in(r.SU.at[g, 0:3], (S_SU, g))
        total = in_order(r.SU, (g,))
        r.TT[g] = jnp.broadcast_to(jnp.sum(total, axis=1, keepdims=True), (8, LANES))
        role_of, u = ALL_UNITS[g]
        kind, _, j = unit_mats(role_of, u)
        for h in range(8):
            if kind == SQUARE:
                r.o_cs[j + h // 2 : j + h // 2 + 1, (h % 2) * LANES : (h % 2 + 1) * LANES] = total[h : h + 1]
            else:
                r.o_cw[j : j + 1, h * LANES : (h + 1) * LANES] = total[h : h + 1]
    copy(r.TT, r.TTR, S_TT, d, 1 - c).start()
    wait_in(r.RQR, S_RQ)
    r.o_rq[...] = r.RQ[...] + r.RQR[...]
    wait_in(r.TTR, S_TT)
    r.o_tt[...] = r.TT[...] + r.TTR[...]
    wait_out(r.RQ, S_RQ)
    wait_out(r.TT, S_TT)
    wait_out(r.NG.at[0:3], S_NG)
    wait_out(r.NH.at[0:3], S_NH)
    for g in range(7):
        wait_out(r.ST.at[g, 0:3], (S_ST, g))
        wait_out(r.SU.at[g, 0:3], (S_SU, g))
    local(r.F_DEC, r.o_dec, 5).wait()
    local(r.F_SRC, r.o_src, 6).wait()
    local(r.F_TGT, r.o_tgt, 7).wait()
    for g in range(7):
        store_unit(g).wait()


UPDATE_INPUTS = dict(
    square=0,
    wide=0,
    norm=0,
    square_rows=0,
    square_cols=0,
    wide_rows=0,
    wide_cols=0,
    moment=0,
)
UPDATE_OUTPUTS = dict(
    decoded=((16, 4, 512), jnp.bfloat16),
    source_grad=((16, 4, 512), jnp.float32),
    target_grad=((16, 8, 512), jnp.float32),
    square_grad=((12, 32, 256), jnp.float32),
    square_rows_new=((12, 32), jnp.float32),
    square_cols_new=((12, 256), jnp.float32),
    square_new=((12, 32, 256), jnp.float32),
    square_copy=((12, 32, 256), jnp.bfloat16),
    wide_grad=((4, 32, 1024), jnp.float32),
    wide_rows_new=((4, 32), jnp.float32),
    wide_cols_new=((4, 1024), jnp.float32),
    wide_new=((4, 32, 1024), jnp.float32),
    wide_copy=((4, 32, 1024), jnp.bfloat16),
    norm_grad=((10, 32), jnp.float32),
    norm_second_new=((10, 32), jnp.float32),
    norm_new=((10, 32), jnp.float32),
    norm_copy=((10, 32), jnp.bfloat16),
)


def update_kernel(*refs):
    r = named(refs, OUTPUTS, UPDATE_INPUTS, UPDATE_OUTPUTS, dict(rows_pad=0))
    c = lax.axis_index("mp")
    bf, f32 = jnp.bfloat16, jnp.float32

    def own_half(value):
        value = value.astype(f32).reshape(16, 8, 512)
        return jnp.where(c == 0, value[:, 0:4], value[:, 4:8])

    r.decoded[...] = own_half(r.o_dec[...]).astype(bf)
    r.source_grad[...] = r.o_src[...]
    r.target_grad[...] = r.o_tgt[...].reshape(16, 8, 512)
    pad = r.rows_pad
    pad[...] = jnp.zeros((BLOCK, LANES), f32)
    pad[0:12, 0:32] = r.square_rows[...]
    pad[12:16, 0:32] = r.wide_rows[...]
    lanes = lax.broadcasted_iota(jnp.int32, (BLOCK, LANES), 1)
    widths = jnp.where(lanes < 12, 1.0 / 512, 1.0 / FF)
    rows_new = 0.5 * pad[...].T + 0.5 * (r.o_rq[...] * widths)
    rows_back = rows_new.T
    r.square_rows_new[...] = rows_back[0:12, 0:32]
    r.wide_rows_new[...] = rows_back[12:16, 0:32]
    square_cols = 0.5 * r.square_cols[...] + 0.5 * (r.o_cs[...] / 512)
    wide_cols = 0.5 * r.wide_cols[...] + 0.5 * (r.o_cw[...] / 512)
    r.square_cols_new[...] = square_cols
    r.wide_cols_new[...] = wide_cols

    def level(m, total, width):
        return (0.5 * r.o_rl[10:11, m : m + 1] + 0.5 * (total / width)) / 512

    def update(master, grad, row, col, lvl):
        return master - RATE * grad * lax.rsqrt(row * col / lvl)

    for g, (role, u) in enumerate(ALL_UNITS):
        kind, _, j = unit_mats(role, u)
        if kind == SQUARE:
            for m in range(4):
                sums = r.o_tt[g]
                total = sums[2 * m : 2 * m + 1, 0:1] + sums[2 * m + 1 : 2 * m + 2, 0:1]
                grad = r.o_gs[j + m]
                new = update(
                    r.square[j + m],
                    grad,
                    rows_new[0:32, j + m : j + m + 1],
                    square_cols[j + m : j + m + 1],
                    level(j + m, total, 512),
                )
                r.square_grad[j + m] = grad
                r.square_new[j + m] = new
                r.square_copy[j + m] = new.astype(bf)
        else:
            total = jnp.sum(r.o_tt[g], axis=0, keepdims=True)[:, 0:1]
            grad = r.o_gw[j]
            new = update(
                r.wide[j],
                grad,
                rows_new[0:32, 12 + j : 13 + j],
                wide_cols[j : j + 1],
                level(12 + j, total, FF),
            )
            r.wide_grad[j] = grad
            r.wide_new[j] = new
            r.wide_copy[j] = new.astype(bf)
    norm_grad = r.o_ng[0:10, 0:32]
    second = 0.5 * r.moment[...] + 0.5 * norm_grad * norm_grad
    norm_new = r.norm[...] - NORM_RATE * norm_grad * lax.rsqrt(second)
    r.norm_grad[...] = norm_grad
    r.norm_second_new[...] = second
    r.norm_new[...] = norm_new
    r.norm_copy[...] = norm_new.astype(bf)


def small_shards(
    source,
    target,
    lengths,
    destinations,
    cotangent,
    square_master,
    wide_master,
    norm_master,
    square_rows,
    square_cols,
    wide_rows,
    wide_cols,
    gain_offset_moment,
):
    vmem = pl.BlockSpec(memory_space=pltpu.VMEM)
    smem = pl.BlockSpec(memory_space=pltpu.SMEM)
    anywhere = pl.BlockSpec(memory_space=pl.ANY)
    moved = pl.pallas_call(
        exchange_kernel,
        out_shape=[jax.ShapeDtypeStruct(*v) for v in OUTPUTS.values()],
        in_specs=[smem, smem] + [anywhere] * 5 + [vmem] * 3,
        out_specs=[anywhere] * 5 + [vmem] * (len(OUTPUTS) - 5),
        scratch_shapes=[pltpu.VMEM(*v) for v in SCRATCH.values()]
        + [pltpu.SemaphoreType.DMA((n,)) for n in (SEM_COUNT, SEM_COUNT, NEAR_COUNT)],
        compiler_params=pltpu.CompilerParams(
            collective_id=0, has_side_effects=True, vmem_limit_bytes=56 << 20
        ),
    )(
        lengths.T,
        destinations,
        source.reshape(BLOCK, 512),
        target.reshape(BLOCK, 512),
        cotangent.reshape(BLOCK, 512),
        square_master,
        wide_master,
        norm_master,
        square_rows,
        wide_rows,
    )
    return tuple(
        pl.pallas_call(
            update_kernel,
            out_shape=[jax.ShapeDtypeStruct(*v) for v in UPDATE_OUTPUTS.values()],
            in_specs=[vmem] * (len(OUTPUTS) + len(UPDATE_INPUTS)),
            out_specs=[vmem] * len(UPDATE_OUTPUTS),
            scratch_shapes=[pltpu.VMEM((BLOCK, LANES), jnp.float32)],
            compiler_params=pltpu.CompilerParams(vmem_limit_bytes=60 << 20),
        )(
            *moved,
            square_master,
            wide_master,
            norm_master,
            square_rows,
            square_cols,
            wide_rows,
            wide_cols,
            gain_offset_moment,
        )
    )


def solution(mesh):
    return jax.shard_map(
        small_shards if dict(mesh.shape) == {"dp": 16, "mp": 2} else shards,
        mesh=mesh,
        in_specs=(
            P("dp", None, None),
            P("dp", None, None),
            P("dp", None),
            P("dp"),
            P("dp", None, None),
            P(None, "dp", "mp"),
            P(None, "dp", "mp"),
            P(None, "dp"),
            P(None, "dp"),
            P(None, "mp"),
            P(None, "dp"),
            P(None, "mp"),
            P(None, "dp"),
        ),
        out_specs=(
            P("dp", "mp", None),
            P("dp", "mp", None),
            P("dp", None, None),
            P(None, "dp", "mp"),
            P(None, "dp"),
            P(None, "mp"),
            P(None, "dp", "mp"),
            P(None, "dp", "mp"),
            P(None, "dp", "mp"),
            P(None, "dp"),
            P(None, "mp"),
            P(None, "dp", "mp"),
            P(None, "dp", "mp"),
            P(None, "dp"),
            P(None, "dp"),
            P(None, "dp"),
            P(None, "dp"),
        ),
        check_vma=False,
    )
```

```python
import types

import jax
import jax.numpy as jnp
from jax import lax
from jax.experimental import pallas as pl
from jax.experimental.pallas import tpu as pltpu
from jax.sharding import PartitionSpec as P

FF = 2048
HEADS = 8
MICRO = 2


RATE = 0.03
NORM_RATE = 0.2


def rounded(input_tensor):
    return input_tensor.astype(jnp.bfloat16)


def identity(input_tensor):
    return input_tensor


def project(input_tensor, weight_matrix):
    return jnp.einsum(
        "rft,tv->rfv", input_tensor, weight_matrix, preferred_element_type=jnp.float32
    )


def project_back(input_tensor, weight_matrix):
    return jnp.einsum(
        "cxk,ak->cxa", input_tensor, weight_matrix, preferred_element_type=jnp.float32
    )


def outer_sum(first_factor_array, second_factor_array):
    return jnp.einsum(
        "zmb,zmf->bf", first_factor_array, second_factor_array, preferred_element_type=jnp.float32
    )


def split_heads(input_tensor, head_size):
    return input_tensor.reshape(
        input_tensor.shape[0], input_tensor.shape[1], input_tensor.shape[2] // head_size, head_size
    )


def merge_heads(input_tensor):
    return input_tensor.reshape(
        input_tensor.shape[0], input_tensor.shape[1], input_tensor.shape[2] * input_tensor.shape[3]
    )


def layer_norm(residual, gain_row, bias_row):
    centred = residual - jnp.mean(residual, axis=-1, keepdims=True)
    spread = lax.rsqrt(jnp.mean(centred * centred, axis=-1, keepdims=True) + 1e-05)
    normed = centred * spread
    return (normed * gain_row + bias_row, (normed, spread))


def norm_back(upstream, gain_row, kept_state, pick):
    normed, spread = kept_state
    scaled = upstream * gain_row
    centred_grad = (
        scaled
        - jnp.mean(scaled, axis=-1, keepdims=True)
        - normed * jnp.mean(scaled * normed, axis=-1, keepdims=True)
    )
    return (
        centred_grad * spread,
        jnp.sum(pick(upstream * normed), axis=(0, 1)),
        jnp.sum(pick(upstream), axis=(0, 1)),
    )


def attend_forward(query_in, key_in, matrices, start_index, allowed, head_size):
    queries = split_heads(rounded(project(query_in, matrices[start_index])), head_size)
    key_rows = split_heads(rounded(project(key_in, matrices[start_index + 1])), head_size)
    content_lines = split_heads(rounded(project(key_in, matrices[start_index + 2])), head_size)
    scores = jnp.einsum(
        "sqhe,skhe->shqk", queries, key_rows, preferred_element_type=jnp.float32
    ) * head_size ** (-0.5)
    scores = jnp.where(allowed[:, None], scores, -1000000000.0)
    attn_probs = jax.nn.softmax(scores, axis=-1)
    probs_low = rounded(attn_probs)
    mixed_heads = rounded(
        merge_heads(
            jnp.einsum(
                "shqk,skhe->sqhe", probs_low, content_lines, preferred_element_type=jnp.float32
            )
        )
    )
    partial_value = project_back(mixed_heads, matrices[start_index + 3])
    return (partial_value, (queries, key_rows, content_lines, attn_probs, probs_low, mixed_heads))


def attend_back(upstream, query_in, key_in, matrices, start_index, kept_state, head_size):
    queries, key_rows, content_lines, attn_probs, probs_low, mixed_heads = kept_state
    scale = head_size ** (-0.5)
    out_grad = outer_sum(upstream, mixed_heads)
    mixed_grad = split_heads(rounded(project(upstream, matrices[start_index + 3])), head_size)
    prob_grad = jnp.einsum(
        "sqhe,skhe->shqk", mixed_grad, content_lines, preferred_element_type=jnp.float32
    )
    value_grad = rounded(
        jnp.einsum("shqk,sqhe->skhe", probs_low, mixed_grad, preferred_element_type=jnp.float32)
    )
    score_grad = rounded(
        attn_probs * (prob_grad - jnp.sum(attn_probs * prob_grad, axis=-1, keepdims=True))
    )
    query_grad = rounded(
        jnp.einsum("shqk,skhe->sqhe", score_grad, key_rows, preferred_element_type=jnp.float32)
        * scale
    )
    key_grad = rounded(
        jnp.einsum("shqk,sqhe->skhe", score_grad, queries, preferred_element_type=jnp.float32)
        * scale
    )
    query_grad = merge_heads(query_grad)
    key_grad = merge_heads(key_grad)
    value_grad = merge_heads(value_grad)
    weight_grads = (
        outer_sum(query_in, query_grad),
        outer_sum(key_in, key_grad),
        outer_sum(key_in, value_grad),
        out_grad,
    )
    asking_piece = project_back(query_grad, matrices[start_index])
    key_part = project_back(key_grad, matrices[start_index + 1]) + project_back(
        value_grad, matrices[start_index + 2]
    )
    return (asking_piece, key_part, weight_grads)


def expand_forward(inputs, matrices, start_index):
    hidden = project(inputs, matrices[start_index])
    active = rounded(jax.nn.gelu(hidden))
    return (project_back(active, matrices[start_index + 1]), (hidden, active))


def expand_back(upstream, inputs, matrices, start_index, kept_state):
    hidden, active = kept_state
    down_grad = outer_sum(upstream, active)
    active_grad = rounded(project(upstream, matrices[start_index + 1]))
    unused, pullback = jax.vjp(jax.nn.gelu, hidden)
    hidden_grad = rounded(pullback(active_grad.astype(jnp.float32))[0])
    up_grad = outer_sum(inputs, hidden_grad)
    return (project_back(hidden_grad, matrices[start_index]), up_grad, down_grad)


def accumulate(totals, position, addend):
    totals[position] = addend if totals[position] is None else totals[position] + addend


def shards(
    source,
    target,
    lengths,
    destinations,
    cotangent,
    square_master,
    wide_master,
    norm_master,
    square_rows,
    square_cols,
    wide_rows,
    wide_cols,
    gain_offset_moment,
):
    peer_count = lax.axis_size("dp")
    sent_dev = source.shape[0]
    slot_count = source.shape[1]
    model_width = source.shape[2]
    per_peer = sent_dev // peer_count
    head_size = model_width // HEADS
    per_block = sent_dev // MICRO
    half_len = slot_count // lax.axis_size("mp")
    half_start = lax.axis_index("mp") * half_len
    send_order = jnp.argsort(destinations, stable=True)
    home_place = jnp.argsort(send_order, stable=True)

    def own_half(input_tensor):
        return lax.dynamic_slice_in_dim(input_tensor, half_start, half_len, 1)

    def share_total(partial_value):
        return lax.psum_scatter(partial_value, "mp", scatter_dimension=1, tiled=True)

    def add_branch(residual, partial_value):
        return residual + share_total(partial_value)

    def low_rows(value):
        return lax.all_gather(rounded(value), "mp", axis=1, tiled=True)

    def by_peer(input_tensor):
        return jnp.take(input_tensor, send_order, axis=0).reshape(
            (peer_count, per_peer) + input_tensor.shape[1:]
        )

    def flatten(input_tensor):
        return input_tensor.reshape((sent_dev,) + input_tensor.shape[2:])

    moved_lengths = flatten(
        lax.all_to_all(by_peer(lengths), "dp", split_axis=0, concat_axis=0, tiled=True)
    )
    square_low, wide_low, norm_low = (
        lax.all_gather(rounded(square_master), "dp", axis=1, tiled=True),
        lax.all_gather(rounded(wide_master), "dp", axis=1, tiled=True),
        lax.all_gather(rounded(norm_master), "dp", axis=1, tiled=True),
    )
    gain_rows = norm_low[:5].astype(jnp.float32)
    bias_rows = norm_low[5:].astype(jnp.float32)
    positions = jnp.arange(slot_count)
    causal = positions[None, :] <= positions[:, None]

    def key_mask(counts):
        return jnp.broadcast_to(
            positions[None, None, :] < counts[:, None, None],
            (counts.shape[0], slot_count, slot_count),
        )

    square_grads = [None] * 12
    wide_grads = [None] * 4
    gain_grads = [None] * 5
    bias_grads = [None] * 5

    def norm_step(upstream, position, kept_state):
        residual_grad, gain_grad, bias_grad = norm_back(
            upstream, gain_rows[position], kept_state, identity
        )
        accumulate(gain_grads, position, gain_grad)
        accumulate(bias_grads, position, bias_grad)
        return residual_grad

    def attend_step(upstream_low, query_in, key_in, start_index, kept_state):
        asking_piece, key_part, weight_grads = attend_back(
            upstream_low, query_in, key_in, square_low, start_index, kept_state, head_size
        )
        for offset in range(4):
            accumulate(square_grads, start_index + offset, weight_grads[offset])
        return (asking_piece, key_part)

    def expand_step(upstream_low, inputs, start_index, kept_state):
        partial_value, up_grad, down_grad = expand_back(
            upstream_low, inputs, wide_low, start_index, kept_state
        )
        accumulate(wide_grads, start_index, up_grad)
        accumulate(wide_grads, start_index + 1, down_grad)
        return partial_value

    encoder_kept = []
    encoded_pieces = []
    for micro_index in range(MICRO):
        row_start = micro_index * per_block
        source_block = source[row_start : row_start + per_block]
        allowed = key_mask(lengths[row_start : row_start + per_block, 0])
        partial_value, attend_kept = attend_forward(
            source_block, source_block, square_low, 0, allowed, head_size
        )
        hidden, hidden_kept = layer_norm(
            add_branch(own_half(source_block).astype(jnp.float32), partial_value),
            gain_rows[0],
            bias_rows[0],
        )
        hidden_low = low_rows(hidden)
        partial_value, expand_kept = expand_forward(hidden_low, wide_low, 0)
        memory, memory_kept = layer_norm(
            add_branch(hidden, partial_value), gain_rows[1], bias_rows[1]
        )
        encoded_pieces.append(low_rows(memory))
        encoder_kept.append((attend_kept, hidden_kept, hidden_low, expand_kept, memory_kept))
    memory_all = jnp.concatenate(encoded_pieces, axis=0)
    moved_memory, moved_target = (
        lax.all_to_all(by_peer(memory_all), "dp", split_axis=0, concat_axis=0, tiled=True),
        lax.all_to_all(by_peer(target), "dp", split_axis=0, concat_axis=0, tiled=True),
    )
    moved_memory = flatten(moved_memory)
    moved_target = flatten(moved_target)
    decoded_parts = []
    memory_back = []
    target_back = []
    for micro_index in range(MICRO):
        row_start = micro_index * per_block
        target_block = moved_target[row_start : row_start + per_block]
        memory_block = moved_memory[row_start : row_start + per_block]
        counts = moved_lengths[row_start : row_start + per_block]
        self_mask = key_mask(counts[:, 1]) & causal[None]
        cross_attention_mask = key_mask(counts[:, 0])
        partial_value, self_kept = attend_forward(
            target_block, target_block, square_low, 4, self_mask, head_size
        )
        first_norm, first_kept = layer_norm(
            add_branch(own_half(target_block).astype(jnp.float32), partial_value),
            gain_rows[2],
            bias_rows[2],
        )
        first_low = low_rows(first_norm)
        partial_value, cross_kept = attend_forward(
            first_low, memory_block, square_low, 8, cross_attention_mask, head_size
        )
        second_norm, second_kept = layer_norm(
            add_branch(first_norm, partial_value), gain_rows[3], bias_rows[3]
        )
        second_low = low_rows(second_norm)
        partial_value, expand_kept = expand_forward(second_low, wide_low, 2)
        output, output_kept = layer_norm(
            add_branch(second_norm, partial_value), gain_rows[4], bias_rows[4]
        )
        decoded_parts.append(identity(rounded(output)))
        upstream = norm_step(
            own_half(cotangent[row_start : row_start + per_block]).astype(jnp.float32),
            4,
            output_kept,
        )
        upstream = add_branch(upstream, expand_step(low_rows(upstream), second_low, 2, expand_kept))
        upstream = norm_step(upstream, 3, second_kept)
        asking_piece, key_part = attend_step(
            low_rows(upstream), first_low, memory_block, 8, cross_kept
        )
        asking_piece, key_part = share_total((asking_piece, key_part))
        memory_back.append(low_rows(key_part))
        upstream = norm_step(upstream + asking_piece, 2, first_kept)
        asking_piece, key_part = attend_step(
            low_rows(upstream), target_block, target_block, 4, self_kept
        )
        target_back.append(low_rows(add_branch(upstream, asking_piece + key_part)))
    returned_memory, returned_target = (
        lax.all_to_all(
            jnp.concatenate(memory_back, axis=0).reshape(
                peer_count, per_peer, slot_count, model_width
            ),
            "dp",
            split_axis=0,
            concat_axis=0,
            tiled=True,
        ),
        lax.all_to_all(
            jnp.concatenate(target_back, axis=0).reshape(
                peer_count, per_peer, slot_count, model_width
            ),
            "dp",
            split_axis=0,
            concat_axis=0,
            tiled=True,
        ),
    )
    memory_gradient = jnp.take(flatten(returned_memory), home_place, axis=0)
    target_grad = jnp.take(flatten(returned_target), home_place, axis=0).astype(jnp.float32)
    source_parts = []
    for micro_index in range(MICRO):
        row_start = micro_index * per_block
        source_block = source[row_start : row_start + per_block]
        attend_kept, hidden_kept, hidden_low, expand_kept, memory_kept = encoder_kept[micro_index]
        upstream = norm_step(
            own_half(memory_gradient[row_start : row_start + per_block]).astype(jnp.float32),
            1,
            memory_kept,
        )
        upstream = add_branch(upstream, expand_step(low_rows(upstream), hidden_low, 0, expand_kept))
        upstream = norm_step(upstream, 0, hidden_kept)
        asking_piece, key_part = attend_step(
            low_rows(upstream), source_block, source_block, 0, attend_kept
        )
        source_parts.append(identity(add_branch(upstream, asking_piece + key_part)))
    square_grad = jnp.stack(square_grads)
    wide_grad = jnp.stack(wide_grads)
    norm_grad = jnp.stack(gain_grads + bias_grads)
    square_grad, wide_grad, norm_grad = (
        lax.psum_scatter(square_grad, "dp", scatter_dimension=1, tiled=True),
        lax.psum_scatter(wide_grad, "dp", scatter_dimension=1, tiled=True),
        lax.psum_scatter(norm_grad, "dp", scatter_dimension=1, tiled=True),
    )
    row_square, row_wide, norm_grad = lax.psum(
        (
            jnp.sum(square_grad * square_grad, axis=2),
            jnp.sum(wide_grad * wide_grad, axis=2),
            norm_grad,
        ),
        "mp",
    )
    square_rows_new = 0.5 * square_rows + 0.5 * (row_square / model_width)
    wide_rows_new = 0.5 * wide_rows + 0.5 * (row_wide / FF)
    col_square, col_wide, level_square, level_wide = lax.psum(
        (
            jnp.sum(square_grad * square_grad, axis=1),
            jnp.sum(wide_grad * wide_grad, axis=1),
            jnp.sum(square_rows_new, axis=1),
            jnp.sum(wide_rows_new, axis=1),
        ),
        "dp",
    )
    square_cols_new = 0.5 * square_cols + 0.5 * (col_square / model_width)
    wide_cols_new = 0.5 * wide_cols + 0.5 * (col_wide / model_width)
    square_second = (
        square_rows_new[:, :, None]
        * square_cols_new[:, None, :]
        / (level_square / model_width)[:, None, None]
    )
    wide_second = (
        wide_rows_new[:, :, None]
        * wide_cols_new[:, None, :]
        / (level_wide / model_width)[:, None, None]
    )
    updated_square_masters = square_master - RATE * square_grad * lax.rsqrt(square_second)
    wide_new = wide_master - RATE * wide_grad * lax.rsqrt(wide_second)
    norm_second_new = 0.5 * gain_offset_moment + 0.5 * norm_grad * norm_grad
    norm_new = norm_master - NORM_RATE * norm_grad * lax.rsqrt(norm_second_new)
    return (
        jnp.concatenate(decoded_parts, axis=0),
        jnp.concatenate(source_parts, axis=0),
        target_grad,
        square_grad,
        square_rows_new,
        square_cols_new,
        updated_square_masters,
        rounded(updated_square_masters),
        wide_grad,
        wide_rows_new,
        wide_cols_new,
        wide_new,
        rounded(wide_new),
        norm_grad,
        norm_second_new,
        norm_new,
        rounded(norm_new),
    )


SQUARE, WIDE = 0, 1
LANES = 128
TOKENS = 256
BLOCK = 128
CHUNK = 64
MESH_IDS = pl.DeviceIdType.MESH
NEG = -1000000000.0
OUTSIDE = -3.0e38
ENC_UNITS = ((SQUARE, 0), (WIDE, 0), (WIDE, 1))
DEC_UNITS = ((SQUARE, 0), (SQUARE, 1), (WIDE, 0), (WIDE, 1))
ALL_UNITS = ((0, 0), (0, 1), (0, 2), (1, 0), (1, 1), (1, 2), (1, 3))


def mm(a, b):
    return jnp.dot(a, b, preferred_element_type=jnp.float32)


def mm_nt(a, b):
    return lax.dot_general(a, b, (((1,), (1,)), ((), ())), preferred_element_type=jnp.float32)


def mm_tn(a, b):
    return lax.dot_general(a, b, (((0,), (0,)), ((), ())), preferred_element_type=jnp.float32)


def repeat(count, body):
    lax.fori_loop(0, count, lambda i, carry: (body(i), carry)[1], 0, unroll=True)


def aligned(i, size):
    return pl.ds(pl.multiple_of(i * size, size), size)


def unit_mats(role, u):
    kind, i = (ENC_UNITS, DEC_UNITS)[role][u]
    if kind == SQUARE:
        return kind, i, 4 * i + 4 * role
    return kind, i, i + 2 * role


def named(refs, *groups):
    return types.SimpleNamespace(**dict(zip([name for group in groups for name in group], refs)))


class Sems:
    def __init__(self, send, recv, count):
        self.send, self.recv, self.count, self.names = send, recv, count, {}

    def at(self, name):
        i = self.names.setdefault(name, len(self.names))
        assert i < self.count
        return self.send.at[i], self.recv.at[i]


SEM_COUNT = 240
NEAR_COUNT = 16
(
    S_AX,
    S_AY,
    S_COT,
    S_DEC,
    S_DM,
    S_DT,
    S_FX,
    S_FY,
    S_M,
    S_MEMORY,
    S_NG,
    S_NORM,
    S_RA,
    S_RB,
    S_RQ,
    S_SA,
    S_SB,
    S_SG,
    S_SOURCE,
    S_ST,
    S_SU,
    S_SV,
    S_NH,
    S_EXT,
    S_SOURCE2,
    S_MEMORY2,
    S_DM2,
    S_DT2,
    S_T,
    S_TARGET,
    S_TT,
    S_Z,
) = range(32)

SCRATCH = dict(
    WS=((8, 4, 2, 2, 32, 256), jnp.bfloat16),
    WW=((2, 4, 2, 2, 32, 1024), jnp.bfloat16),
    GS=((8, 4, 2, 2, 32, 256), jnp.bfloat16),
    GW=((2, 4, 2, 2, 32, 1024), jnp.bfloat16),
    SB=((12, 32, 256), jnp.bfloat16),
    WB=((4, 32, 1024), jnp.bfloat16),
    R1AS=((8, 2, 2, 32, 256), jnp.bfloat16),
    R1BS=((8, 2, 2, 32, 256), jnp.bfloat16),
    R1AW=((2, 2, 2, 32, 1024), jnp.bfloat16),
    R1BW=((2, 2, 2, 32, 1024), jnp.bfloat16),
    R2AS=((8, 2, 32, 256), jnp.bfloat16),
    R2BS=((8, 2, 32, 256), jnp.bfloat16),
    R2AW=((2, 2, 32, 1024), jnp.bfloat16),
    R2BW=((2, 2, 32, 1024), jnp.bfloat16),
    R3S=((2, 12, 32, 256), jnp.bfloat16),
    R3W=((2, 4, 32, 1024), jnp.bfloat16),
    NB=((16, 16, LANES), jnp.bfloat16),
    RL=((16, LANES), jnp.float32),
    NORM=((16, 512), jnp.float32),
    EXT=((BLOCK, LANES), jnp.float32),
    SEXT=((BLOCK, LANES), jnp.bfloat16),
    XHALF=((2, BLOCK, 256), jnp.bfloat16),
    XEXT=((BLOCK, LANES), jnp.bfloat16),
    TSEND=((8, 16, 640), jnp.bfloat16),
    TREC=((16, 16, 640), jnp.bfloat16),
    COT2=((BLOCK, 512), jnp.bfloat16),
    COT=((TOKENS, 512), jnp.float32),
    XT=((TOKENS, 512), jnp.bfloat16),
    MSEND=((8, 2, 16, 512), jnp.bfloat16),
    MREC=((2, 2, 2, 4, 16, 256), jnp.bfloat16),
    MEM=((TOKENS, 512), jnp.bfloat16),
    DMSEND=((2, 2, 4, 16, 512), jnp.bfloat16),
    MG=((2, 8, 2, 16, 256), jnp.bfloat16),
    DTSEND=((16, 16, 512), jnp.bfloat16),
    TG=((2, 8, 16, 256), jnp.bfloat16),
    DSEND=((BLOCK, 512), jnp.bfloat16),
    DREC=((BLOCK, 512), jnp.bfloat16),
    SGSEND=((16, 4, 512), jnp.float32),
    SGREC=((16, 4, 512), jnp.float32),
    PERMT=((2, BLOCK, BLOCK), jnp.bfloat16),
    ALLOW=((2, 2, BLOCK, TOKENS), jnp.float32),
    FILL=((BLOCK, TOKENS), jnp.float32),
    Q=((2, TOKENS, 256), jnp.bfloat16),
    K=((2, TOKENS, 256), jnp.bfloat16),
    V=((2, TOKENS, 256), jnp.bfloat16),
    O=((2, TOKENS, 256), jnp.bfloat16),
    PROB=((2, 4, BLOCK, TOKENS), jnp.float32),
    DO=((TOKENS, 256), jnp.bfloat16),
    DQ=((TOKENS, 256), jnp.bfloat16),
    DK=((TOKENS, 256), jnp.bfloat16),
    DV=((TOKENS, 256), jnp.bfloat16),
    U=((TOKENS, 1024), jnp.float32),
    ACT=((TOKENS, 1024), jnp.bfloat16),
    DU=((TOKENS, 1024), jnp.bfloat16),
    RES=((TOKENS, 512), jnp.float32),
    LOW=((3, TOKENS, 512), jnp.bfloat16),
    XH=((3, TOKENS, 512), jnp.float32),
    RSD=((3, TOKENS, 1), jnp.float32),
    GRAD=((TOKENS, 512), jnp.float32),
    GLOW=((TOKENS, 512), jnp.bfloat16),
    PS=((2, TOKENS, 512), jnp.bfloat16),
    PR=((2, TOKENS, 512), jnp.bfloat16),
    NGR=((4, 16, LANES), jnp.float32),
    NG=((4, 16, LANES), jnp.float32),
    NH=((4, 16, LANES), jnp.float32),
    ST=((7, 4, 8, LANES), jnp.float32),
    SU=((7, 4, 8, LANES), jnp.float32),
    SV=((16, 8, LANES), jnp.float32),
    RQ=((BLOCK, LANES), jnp.float32),
    RQR=((BLOCK, LANES), jnp.float32),
    TT=((7, 8, LANES), jnp.float32),
    SM=((12, 32, 256), jnp.float32),
    WM=((4, 32, 1024), jnp.float32),
    SRC=((BLOCK, 512), jnp.bfloat16),
    TGT=((BLOCK, 512), jnp.bfloat16),
    COT1=((BLOCK, 512), jnp.bfloat16),
    F_DEC=((BLOCK, 512), jnp.bfloat16),
    F_SRC=((16, 4, 512), jnp.float32),
    F_TGT=((BLOCK, 512), jnp.float32),
    F_GS=((12, 32, 256), jnp.float32),
    F_GW=((4, 32, 1024), jnp.float32),
    TTR=((7, 8, LANES), jnp.float32),
)

INPUTS = dict(
    lengths=0,
    destinations=0,
    source=0,
    target=0,
    cotangent=0,
    square=0,
    wide=0,
    norm=0,
    square_rows=0,
    wide_rows=0,
)
OUTPUTS = dict(
    o_dec=((BLOCK, 512), jnp.bfloat16),
    o_src=((16, 4, 512), jnp.float32),
    o_tgt=((BLOCK, 512), jnp.float32),
    o_gs=((12, 32, 256), jnp.float32),
    o_gw=((4, 32, 1024), jnp.float32),
    o_cs=((12, 256), jnp.float32),
    o_cw=((4, 1024), jnp.float32),
    o_rq=((BLOCK, LANES), jnp.float32),
    o_rl=((16, LANES), jnp.float32),
    o_tt=((7, 8, LANES), jnp.float32),
    o_ng=((16, LANES), jnp.float32),
)


def exchange_kernel(*refs):
    r = named(refs, INPUTS, OUTPUTS, SCRATCH)
    sems = Sems(refs[-3], refs[-2], SEM_COUNT)
    near = refs[-1]
    d = lax.axis_index("dp")
    c = lax.axis_index("mp")
    z = lax.div(d, 4)
    yx = lax.rem(d, 4)
    y = lax.div(yx, 2)
    x = lax.rem(yx, 2)
    role = lax.rem(z, 2)
    x_mate = d + 1 - 2 * x
    y_mate = d + 2 - 4 * y
    partner = d + 4 - 8 * role
    bf, f32 = jnp.bfloat16, jnp.float32

    G = (r.GS, r.GW)
    R1A, R1B = (r.R1AS, r.R1AW), (r.R1BS, r.R1BW)
    R2A, R2B = (r.R2AS, r.R2AW), (r.R2BS, r.R2BW)

    def z_mate(k):
        zz = lax.rem(z + k, 4)
        return zz, zz * 4 + yx

    def copy(src, dst, name, dev, core=None):
        send, recv = sems.at(name)
        return pltpu.make_async_remote_copy(
            src_ref=src,
            dst_ref=dst,
            send_sem=send,
            recv_sem=recv,
            device_id=(dev, c if core is None else core),
            device_id_type=MESH_IDS,
        )

    def local(src, dst, i):
        return pltpu.make_async_copy(src, dst, near.at[i])

    my_half = pl.ds(pl.multiple_of(c * 256, 256), 256)

    def hand_over(ref, name):
        copy(ref.at[c], ref.at[c], name, d, 1 - c).start()
        wait_in(ref.at[0], name)
        wait_out(ref.at[0], name)

    def plane_mates():
        return (x_mate, y_mate, z * 4 + 3 - yx)

    def in_order(ref, lead=()):
        total = ref[lead + (0,)]
        for i in range(1, 4):
            total = total + ref[lead + (i,)]
        return total

    def wait_in(dst, name):
        copy(dst, dst, name, x_mate).wait_recv()

    def wait_out(src, name):
        copy(src, src, name, x_mate).wait_send()

    loads = [
        local(r.target, r.TGT, 0),
        local(r.source, r.SRC, 1),
        local(r.square, r.SM, 2),
        local(r.wide, r.WM, 3),
        local(r.cotangent, r.COT1, 4),
    ]
    for i in (2, 3, 1, 0, 4):
        loads[i].start()
    barrier = pltpu.get_barrier_semaphore()
    for k in range(1, 16):
        pl.semaphore_signal(
            barrier, inc=1, device_id=(lax.rem(d + k, 16), c), device_id_type=MESH_IDS
        )
    pl.semaphore_signal(barrier, inc=1, device_id=(d, 1 - c), device_id_type=MESH_IDS)

    row_id = lax.broadcasted_iota(jnp.int32, (BLOCK, BLOCK), 0)
    col_id = lax.broadcasted_iota(jnp.int32, (BLOCK, BLOCK), 1)
    col_z = 2 * (col_id >> 6) + 1 - ((col_id >> 3) & 1)
    col_dev = (col_z * 4 + ((col_id >> 4) & 3)).astype(f32)
    same_slot = (row_id & 7) == (col_id & 7)

    def perm_of(dest_column):
        return jnp.where((dest_column == col_dev) & same_slot, 1.0, 0.0)

    def cast_weights(role_of, u):
        kind, i, j = unit_mats(role_of, u)
        if kind == SQUARE:
            for m in range(4):
                r.SB[j + m] = r.SM[j + m].astype(bf)

            @pl.when(role == role_of)
            def _():
                for m in range(4):
                    r.WS[4 * i + m, z, y, x] = r.SB[j + m]

        else:
            r.WB[j] = r.WM[j].astype(bf)

            @pl.when(role == role_of)
            def _():
                r.WW[i, z, y, x] = r.WB[j]

    def z_slot(kind, i, k=0, yy=None, xx=None):
        zz = lax.rem(z + 4 - k, 4)
        at = (zz, y if yy is None else yy, x if xx is None else xx)
        if kind == SQUARE:
            return r.WS.at[(slice(4 * i, 4 * i + 4),) + at]
        return r.WW.at[(i,) + at]

    def z_send(my_role, target_role, u):
        kind, i, j = unit_mats(target_role, u)
        src = r.SB.at[j : j + 4] if kind == SQUARE else r.WB.at[j]
        for k in (2,) if my_role == target_role else (1, 3):
            copy(src, z_slot(kind, i), (S_Z, u, k), z_mate(k)[1]).start()

    def z_sent(my_role):
        for target_role, u in ALL_UNITS:
            kind, i, j = unit_mats(target_role, u)
            src = r.SB.at[j : j + 4] if kind == SQUARE else r.WB.at[j]
            for k in (2,) if my_role == target_role else (1, 3):
                wait_out(src, (S_Z, u, k))

    def send_norms():
        for k in range(1, 16):
            dev = lax.rem(d + k, 16)
            copy(r.NB.at[d], r.NB.at[d], S_NORM, dev).start()

    def send_target(my_role):
        for t in range(8):
            dev = (2 * (t // 4) + 1) * 4 + t % 4
            send = copy(r.TSEND.at[t], r.TREC.at[d], S_TARGET, dev)
            if my_role == 0:
                send.start()
            else:
                pl.when(dev != d)(send.start)

                @pl.when(dev == d)
                def _():
                    r.TREC[d] = r.TSEND[t]

    def ag_plane(kind, i, u, k):
        block = z_slot(kind, i, k)
        copy(block, block, (S_AX, u, k), x_mate).start()
        copy(block, block, (S_AY, u, k), y_mate).start()

    def ag_column(units, u):
        kind, i = units[u]
        for k in (1, 3, 2):
            wait_in(z_slot(kind, i), (S_Z, u, k))
            ag_plane(kind, i, u, k)

    def by_x(u, k):
        return (k < 2) == (u % 2 == 0)

    def ag_forward(units, u, ks=(1, 3, 2)):
        kind, i = units[u]
        for k in ks:
            if by_x(u, k):
                wait_in(z_slot(kind, i), (S_AY, u, k))
                block = z_slot(kind, i, k, yy=1 - y)
                copy(block, block, (S_FX, u, k), x_mate).start()
            else:
                wait_in(z_slot(kind, i), (S_AX, u, k))
                block = z_slot(kind, i, k, xx=1 - x)
                copy(block, block, (S_FY, u, k), y_mate).start()

    def ag_finish(units, u):
        kind, i = units[u]
        block = z_slot(kind, i)
        for k in (0, 1, 3, 2):
            wait_in(block, (S_AX if by_x(u, k) else S_AY, u, k))
            wait_in(block, (S_FX if by_x(u, k) else S_FY, u, k))

    def ag_sent(units):
        for u, (kind, i) in enumerate(units):
            block = z_slot(kind, i)
            for k in range(4):
                wait_out(block, (S_AX, u, k))
                wait_out(block, (S_AY, u, k))
                wait_out(block, (S_FX if by_x(u, k) else S_FY, u, k))

    def half_unit(buf, kind, i, h, *rest):
        if kind == SQUARE:
            return buf[0], (slice(4 * i + 2 * h, 4 * i + 2 * h + 2),) + rest
        pad = (slice(None),) * (buf[1].ndim - 2 - len(rest))
        return buf[1], (i,) + rest + pad + (slice(512 * h, 512 * h + 512),)

    def part(buf, kind, i, h, *rest):
        ref, index = half_unit(buf, kind, i, h, *rest)
        return ref.at[index]

    def rs_first(units, u, h):
        kind, i = units[u]
        every = slice(None)
        copy(
            part(G, kind, i, h, slice(0, 2), 1 - y), part(R1A, kind, i, h), (S_RA, u, h), y_mate
        ).start()
        copy(
            part(G, kind, i, h, slice(2, 4), every, 1 - x),
            part(R1B, kind, i, h),
            (S_RB, u, h),
            x_mate,
        ).start()

    def add_into(place, other):
        ref, index = place
        ref[index] = (ref[index].astype(f32) + other[...].astype(f32)).astype(bf)

    def rs_second(units, u, h):
        kind, i = units[u]
        every = slice(None)
        ra, rb = part(R1A, kind, i, h), part(R1B, kind, i, h)
        wait_in(ra, (S_RA, u, h))
        add_into(half_unit(G, kind, i, h, slice(0, 2), y), ra)
        copy(
            part(G, kind, i, h, slice(0, 2), y, 1 - x), part(R2A, kind, i, h), (S_SA, u, h), x_mate
        ).start()
        wait_in(rb, (S_RB, u, h))
        add_into(half_unit(G, kind, i, h, slice(2, 4), every, x), rb)
        copy(
            part(G, kind, i, h, slice(2, 4), 1 - y, x), part(R2B, kind, i, h), (S_SB, u, h), y_mate
        ).start()

    def arrived(role_of, u, h, slot):
        kind, i, j = unit_mats(role_of, u)
        if kind == SQUARE:
            return r.R3S.at[slot, j + 2 * h : j + 2 * h + 2]
        return r.R3W.at[slot, j, :, 512 * h : 512 * h + 512]

    def rs_third(my_role, u, h):
        kind, i, j = unit_mats(my_role, u)
        ra, rb = part(R2A, kind, i, h), part(R2B, kind, i, h)
        wait_in(ra, (S_SA, u, h))
        add_into(half_unit(G, kind, i, h, slice(0, 2), y, x), ra)
        wait_in(rb, (S_SB, u, h))
        add_into(half_unit(G, kind, i, h, slice(2, 4), y, x), rb)
        for k in (2, 1, 3):
            slot = 1 if k == 3 else 0
            zz, dev = z_mate(k)
            copy(
                part(G, kind, i, h, zz, y, x),
                arrived(my_role, u, h, slot),
                (S_T, my_role, u, h, slot, k & 1),
                dev,
            ).start()

    def rs_sent(my_role, units):
        for u, (kind, i) in enumerate(units):
            for h in range(2):
                wait_out(part(R1A, kind, i, h), (S_RA, u, h))
                wait_out(part(R1B, kind, i, h), (S_RB, u, h))
                wait_out(part(R2A, kind, i, h), (S_SA, u, h))
                wait_out(part(R2B, kind, i, h), (S_SB, u, h))
                for k in (1, 2, 3):
                    slot = 1 if k == 3 else 0
                    wait_out(arrived(my_role, u, h, 0), (S_T, my_role, u, h, slot, k & 1))

    def final_sum(my_role, role_of, u):
        kind, i, j = unit_mats(role_of, u)
        for h in range(2):
            first = arrived(role_of, u, h, 0)
            second = arrived(role_of, u, h, 1)
            if my_role == role_of:
                wait_in(first, (S_T, role_of, u, h, 0, 0))
                ref, index = half_unit(G, kind, i, h, z, y, x)
                total = ref[index].astype(f32) + first[...].astype(f32)
            else:
                wait_in(first, (S_T, role_of, u, h, 0, 1))
                wait_in(second, (S_T, role_of, u, h, 1, 1))
                total = first[...].astype(f32) + second[...].astype(f32)
            if kind == SQUARE:
                r.F_GS[j + 2 * h : j + 2 * h + 2] = total
            else:
                r.F_GW[j, :, 512 * h : 512 * h + 512] = total

    def unit_stats(g):
        role_of, u = ALL_UNITS[g]
        kind, i, j = unit_mats(role_of, u)
        lanes = lax.broadcasted_iota(jnp.int32, (32, LANES), 1)
        rows = r.RQ[0:32, :]
        if kind == SQUARE:
            for m in range(4):
                grad = r.F_GS[j + m]
                sq = grad * grad
                cols = jnp.sum(sq, axis=0, keepdims=True)
                for h in range(2):
                    r.ST[g, z, 2 * m + h : 2 * m + h + 1, :] = cols[:, h * LANES : (h + 1) * LANES]
                rows = jnp.where(lanes == j + m, jnp.sum(sq, axis=1, keepdims=True), rows)
        else:
            grad = r.F_GW[j]
            sq = grad * grad
            cols = jnp.sum(sq, axis=0, keepdims=True)
            for h in range(8):
                r.ST[g, z, h : h + 1, :] = cols[:, h * LANES : (h + 1) * LANES]
            rows = jnp.where(lanes == 12 + j, jnp.sum(sq, axis=1, keepdims=True), rows)
        r.RQ[0:32, :] = rows
        if g == 0:
            r.SV[d] = r.ST[0, z]
            for k in range(1, 16):
                copy(r.SV.at[d], r.SV.at[d], S_SV, lax.rem(d + k, 16)).start()
            return
        for k in (1, 2, 3):
            copy(r.ST.at[g, z], r.ST.at[g, z], (S_ST, g), z_mate(k)[1]).start()

    def spread_unit(g):
        wait_in(r.ST.at[g, 0:3], (S_ST, g))
        r.SU[g, yx] = in_order(r.ST, (g,))
        for dev in plane_mates():
            copy(r.SU.at[g, yx], r.SU.at[g, yx], (S_SU, g), dev).start()

    def store_unit(g):
        kind, i, j = unit_mats(*ALL_UNITS[g])
        if kind == SQUARE:
            return local(r.F_GS.at[j : j + 4], r.o_gs.at[j : j + 4], 8 + g)
        return local(r.F_GW.at[j], r.o_gw.at[j], 8 + g)

    def finish_unit(my_role, g):
        final_sum(my_role, *ALL_UNITS[g])
        store_unit(g).start()
        unit_stats(g)

    def weight(kind, i, cols=None):
        if kind == SQUARE:
            return r.WS[i].reshape(512, 256)
        if cols is None:
            return r.WW[i].reshape(512, 1024)
        return r.WW[i, :, :, :, :, cols].reshape(512, 256)

    def put_square(i, value):
        r.GS[i] = value.astype(bf).reshape(4, 2, 2, 32, 256)

    def swap(number, partial):
        slot = number % 2
        for half in range(2):
            rows = slice(half * BLOCK, (half + 1) * BLOCK)
            if number >= 2:
                wait_out(r.PS.at[slot, rows], (S_M, number - 2, half))
            r.PS[slot, rows] = partial(rows).astype(bf)
            copy(
                r.PS.at[slot, rows], r.PR.at[slot, rows], (S_M, number, half), d, 1 - c
            ).start()

    def swapped(number, body):
        slot = number % 2
        for half in range(2):
            rows = slice(half * BLOCK, (half + 1) * BLOCK)
            wait_in(r.PR.at[slot, rows], (S_M, number, half))

            def chunk(i):
                at = pl.ds(pl.multiple_of(half * BLOCK + i * CHUNK, CHUNK), CHUNK)
                body(
                    at,
                    half * (BLOCK // CHUNK) + i,
                    r.PS[slot, at].astype(f32) + r.PR[slot, at].astype(f32),
                )

            repeat(BLOCK // CHUNK, chunk)

    def swaps_sent(count):
        for number in (count - 2, count - 1):
            for half in range(2):
                wait_out(r.PS.at[0, 0:BLOCK], (S_M, number, half))

    def norm_forward(residual, kept, which, at):
        centred = residual - jnp.mean(residual, axis=-1, keepdims=True)
        spread = lax.rsqrt(jnp.mean(centred * centred, axis=-1, keepdims=True) + 1e-05)
        normed = centred * spread
        r.XH[kept, at] = normed
        r.RSD[kept, at] = spread
        return normed * r.NORM[which : which + 1, :] + r.NORM[5 + which : 6 + which, :]

    def norm_backward(upstream, kept, which, at):
        normed = r.XH[kept, at]
        scaled = upstream * r.NORM[which : which + 1, :]
        both = upstream * normed
        gain_sum = jnp.sum(both, axis=0, keepdims=True)
        bias_sum = jnp.sum(upstream, axis=0, keepdims=True)
        for b in range(4):
            lanes = slice(b * LANES, (b + 1) * LANES)
            r.NGR[b, which : which + 1, :] += gain_sum[:, lanes]
            r.NGR[b, 5 + which : 6 + which, :] += bias_sum[:, lanes]
        return r.RSD[kept, at] * (
            scaled
            - jnp.mean(scaled, axis=-1, keepdims=True)
            - normed * jnp.mean(scaled * normed, axis=-1, keepdims=True)
        )

    head_lane = lax.broadcasted_iota(jnp.int32, (1, LANES), 1)
    first_head = jnp.where(head_lane < 64, 1.0, 0.0)
    second_head = 1.0 - first_head

    def stacked(value):
        wide_value = value.astype(f32)
        return jnp.concatenate([wide_value * first_head, wide_value * second_head], axis=0).astype(bf)

    def unstacked(value):
        return value[0:BLOCK] * first_head + value[BLOCK:] * second_head

    def pairs(body):
        for blk in range(2):
            for pr in range(2):
                body(blk, slice(blk * BLOCK, (blk + 1) * BLOCK), slice(pr * LANES, (pr + 1) * LANES), 2 * blk + pr)

    def make_masks(slot, count_of, causal):
        row = lax.broadcasted_iota(jnp.int32, (BLOCK, TOKENS), 0)
        col = lax.broadcasted_iota(jnp.int32, (BLOCK, TOKENS), 1) & (BLOCK - 1)
        same = (row >> 3) == (col >> 3)
        r.FILL[...] = jnp.where(same, NEG, OUTSIDE)
        for blk in range(2):
            ok = same & ((col & 7).astype(f32) < count_of(blk))
            if causal:
                ok = ok & ((col & 7) <= (row & 7))
            r.ALLOW[slot, blk] = jnp.where(ok, 1.0, 0.0)

    def attend(kept, mask_slot):
        def one(blk, rows, lanes, n):
            keys = stacked(r.K[kept, rows, lanes])
            scores = mm_nt(r.Q[kept, rows, lanes], keys) * 0.125
            scores = jnp.where(r.ALLOW[mask_slot, blk] > 0.5, scores, r.FILL[...])
            halves = []
            for h in range(2):
                s = scores[:, h * BLOCK : (h + 1) * BLOCK]
                e = jnp.exp(s - jnp.max(s, axis=-1, keepdims=True))
                halves.append(e / jnp.sum(e, axis=-1, keepdims=True))
            probs = jnp.concatenate(halves, axis=1)
            r.PROB[kept, n] = probs
            r.O[kept, rows, lanes] = mm(
                probs.astype(bf), stacked(r.V[kept, rows, lanes])
            ).astype(bf)

        pairs(one)

    def attend_back(kept):
        def one(blk, rows, lanes, n):
            queries = r.Q[kept, rows, lanes]
            keys = stacked(r.K[kept, rows, lanes])
            values = stacked(r.V[kept, rows, lanes])
            out_grad = r.DO[rows, lanes]
            probs = r.PROB[kept, n]
            weighted = probs * mm_nt(out_grad, values)
            halves = []
            for h in range(2):
                w = weighted[:, h * BLOCK : (h + 1) * BLOCK]
                p = probs[:, h * BLOCK : (h + 1) * BLOCK]
                halves.append(w - p * jnp.sum(w, axis=-1, keepdims=True))
            score_grad = jnp.concatenate(halves, axis=1).astype(bf)
            r.DQ[rows, lanes] = (mm(score_grad, keys) * 0.125).astype(bf)
            r.DK[rows, lanes] = (unstacked(mm_tn(score_grad, queries)) * 0.125).astype(bf)
            r.DV[rows, lanes] = unstacked(mm_tn(probs.astype(bf), out_grad)).astype(bf)

        pairs(one)

    def project_all(kept, base, queries, keys):
        r.Q[kept] = mm(queries, weight(SQUARE, base)).astype(bf)
        r.K[kept] = mm(keys, weight(SQUARE, base + 1)).astype(bf)
        r.V[kept] = mm(keys, weight(SQUARE, base + 2)).astype(bf)

    def attention_out(kept, base):
        return lambda rows: mm_nt(r.O[kept, rows], weight(SQUARE, base + 3))

    def attention_back_start(kept, base):
        upstream = r.GLOW[...]
        r.DO[...] = mm(upstream, weight(SQUARE, base + 3)).astype(bf)
        attend_back(kept)

    def query_side(base):
        return lambda rows: mm_nt(r.DQ[rows], weight(SQUARE, base))

    def key_side(base):
        return lambda rows: mm_nt(r.DK[rows], weight(SQUARE, base + 1)) + mm_nt(
            r.DV[rows], weight(SQUARE, base + 2)
        )

    def all_sides(base):
        return lambda rows: query_side(base)(rows) + key_side(base)(rows)

    def expand(inputs):
        def one(n):
            cols = aligned(n, 256)
            hidden = mm(inputs, weight(WIDE, 0, cols))
            r.U[:, cols] = hidden
            bent = jnp.tanh(0.7978845608 * (hidden + 0.044715 * hidden * hidden * hidden))
            r.ACT[:, cols] = (0.5 * hidden * (1.0 + bent)).astype(bf)

        repeat(4, one)

    def contract(rows):
        return mm_nt(r.ACT[rows], weight(WIDE, 1))

    def expand_back_down(h):
        upstream = r.GLOW[...]

        def one(n):
            cols = aligned(2 * h + n, 256)
            r.GW[1, :, :, :, :, cols] = (
                mm_tn(upstream, r.ACT[:, cols]).astype(bf).reshape(4, 2, 2, 32, 256)
            )

        repeat(2, one)

    def expand_back_hidden():
        upstream = r.GLOW[...]

        def one(n):
            cols = aligned(n, 256)
            active_grad = mm(upstream, weight(WIDE, 1, cols)).astype(bf).astype(f32)
            hidden = r.U[:, cols]
            square = hidden * hidden
            bent = jnp.tanh(0.7978845608 * (hidden + 0.044715 * hidden * square))
            slope = 0.5 * (1.0 + bent) + 0.5 * hidden * (1.0 - bent * bent) * 0.7978845608 * (
                1.0 + 3.0 * 0.044715 * square
            )
            r.DU[:, cols] = (active_grad * slope).astype(bf)

        repeat(4, one)

    def expand_back_up(inputs, h):
        def one(n):
            cols = aligned(2 * h + n, 256)
            r.GW[0, :, :, :, :, cols] = (
                mm_tn(inputs, r.DU[:, cols]).astype(bf).reshape(4, 2, 2, 32, 256)
            )

        repeat(2, one)

    def expand_input(rows):
        return mm_nt(r.DU[rows], weight(WIDE, 0))

    def clear_sums():
        r.NGR[...] = jnp.zeros((4, 16, LANES), f32)
        sums = jnp.sum(r.RL[...], axis=1, keepdims=True)
        rows = lax.broadcasted_iota(jnp.int32, (16, LANES), 0)
        lanes = lax.broadcasted_iota(jnp.int32, (16, LANES), 1)
        line = jnp.sum(jnp.where(rows == lanes, sums, 0.0), axis=0, keepdims=True)
        for b in range(4):
            r.NGR[b, 10:11, :] = line
        r.RQ[...] = jnp.zeros((BLOCK, LANES), f32)

    def read_norms():
        wait_in(r.NB.at[0:15], S_NORM)
        for b in range(4):
            total = r.NB[4 * b].astype(f32)
            for i in range(1, 4):
                total = total + r.NB[4 * b + i].astype(f32)
            r.NORM[:, b * LANES : (b + 1) * LANES] = total

    def by_role(body):
        pl.when(role == 0)(lambda: body(0))
        pl.when(role == 1)(lambda: body(1))

    def start_unit(u):
        def body(my_role):
            if u < 3:
                z_send(my_role, 0, u)
            units = (ENC_UNITS, DEC_UNITS)[my_role]
            if u < len(units):
                ag_plane(*units[u], u, 0)

        by_role(body)

    loads[2].wait()
    cast_weights(0, 0)
    cast_weights(1, 0)
    pl.semaphore_wait(barrier, 16)
    start_unit(0)
    loads[3].wait()
    cast_weights(0, 1)
    cast_weights(1, 1)
    start_unit(1)
    cast_weights(0, 2)
    cast_weights(1, 2)
    start_unit(2)
    cast_weights(1, 3)
    start_unit(3)

    r.NORM[...] = jnp.zeros((16, 512), f32)
    r.NORM[0:10, 0:32] = r.norm[...]
    shift = lax.rem(d, 4) * 32
    r.NB[d] = pltpu.roll(r.NORM[:, 0:LANES], shift, 1).astype(bf)
    r.RL[...] = jnp.zeros((16, LANES), f32)
    r.RL[0:12, 0:32] = r.square_rows[...]
    r.RL[12:16, 0:32] = r.wide_rows[...]

    send_norms()

    lane = lax.broadcasted_iota(jnp.int32, (8, LANES), 1)
    for s in range(16):
        r.EXT[8 * s : 8 * s + 8, :] = jnp.where(
            lane < 32,
            r.lengths[0, s],
            jnp.where(lane < 64, r.lengths[1, s], r.destinations[s]),
        ).astype(f32)
    ext_low = r.EXT[...].astype(bf)
    r.SEXT[...] = ext_low

    loads[1].wait()

    @pl.when(role == 1)
    def _():
        copy(r.SRC.at[:, my_half], r.XHALF.at[c], S_SOURCE, partner).start()
        copy(r.SEXT, r.XEXT, S_EXT, partner).start()

    def later_units(my_role, us):
        for u in us:
            z_send(my_role, 1, u)

    by_role(lambda my_role: later_units(my_role, (0, 1)))

    perm_f = perm_of(r.EXT[:, 64:65])
    r.PERMT[0] = perm_f.astype(bf)
    perm = perm_f.T.astype(bf)
    loads[0].wait()
    r.TSEND[:, :, 0:512] = mm(perm, r.TGT[...]).astype(bf).reshape(8, 16, 512)
    r.TSEND[:, :, 512:640] = mm(perm, ext_low).astype(bf).reshape(8, 16, LANES)

    loads[4].wait()

    def last_starts(my_role):
        send_target(my_role)
        later_units(my_role, (2, 3))
        if my_role == 0:
            copy(r.COT1, r.COT2, S_COT, partner).start()

    by_role(last_starts)

    def encoder():
        units = ENC_UNITS
        clear_sums()
        for u in range(3):
            ag_forward(units, u, (0,))
        ag_column(units, 0)
        ag_forward(units, 0)
        ag_column(units, 1)
        wait_in(r.XEXT, S_EXT)
        wait_in(r.XHALF.at[0], S_SOURCE)
        hand_over(r.XHALF, S_SOURCE2)
        r.XT[0:BLOCK] = r.SRC[...]
        for half in range(2):
            r.XT[BLOCK:, half * 256 : half * 256 + 256] = r.XHALF[half]
        def counts(blk):
            return r.EXT[:, 0:1] if blk == 0 else r.XEXT[...].astype(f32)[:, 0:1]

        make_masks(0, counts, False)
        r.PERMT[1] = perm_of(r.XEXT[...].astype(f32)[:, 64:65]).astype(bf)
        read_norms()
        ag_column(units, 2)
        ag_finish(units, 0)
        x_in = r.XT[...]
        project_all(0, 0, x_in, x_in)
        attend(0, 0)
        swap(0, attention_out(0, 0))
        ag_forward(units, 1)

        def first(at, n, total):
            hidden = norm_forward(r.XT[at].astype(f32) + total, 0, 0, at)
            r.RES[at] = hidden
            r.LOW[0, at] = hidden.astype(bf)

        swapped(0, first)
        ag_finish(units, 1)
        expand(r.LOW[0])
        ag_forward(units, 2)
        ag_finish(units, 2)
        swap(1, contract)

        def second(at, n, total):
            r.LOW[1, at] = norm_forward(r.RES[at] + total, 1, 1, at).astype(bf)

        swapped(1, second)
        for jj in range(2):
            block = r.LOW[1, jj * BLOCK : (jj + 1) * BLOCK]
            r.MSEND[:, jj] = mm_tn(r.PERMT[jj], block).astype(bf).reshape(8, 16, 512)
        zz = lax.div(z, 2)
        for t in range(8):
            dev = (2 * (t // 4) + 1) * 4 + t % 4
            copy(
                r.MSEND.at[t, :, :, my_half], r.MREC.at[c, zz, :, yx], S_MEMORY, dev
            ).start()

        wait_in(r.DREC, S_DEC)
        r.F_DEC[...] = r.DREC[...]
        local(r.F_DEC, r.o_dec, 5).start()
        wait_in(r.MG.at[0], S_DM)
        hand_over(r.MG, S_DM2)
        for jj in range(2):
            for half in range(2):
                r.GRAD[jj * BLOCK : (jj + 1) * BLOCK, half * 256 : half * 256 + 256] = mm(
                    r.PERMT[jj], r.MG[half, :, jj].reshape(BLOCK, 256)
                )

        def back_one(i):
            at = aligned(i, CHUNK)
            value = norm_backward(r.GRAD[at], 1, 1, at)
            r.GRAD[at] = value
            r.GLOW[at] = value.astype(bf)

        repeat(TOKENS // CHUNK, back_one)
        for h in range(2):
            expand_back_down(h)
            rs_first(units, 2, h)
        expand_back_hidden()
        swap(2, expand_input)
        for h in range(2):
            expand_back_up(r.LOW[0], h)
            rs_first(units, 1, h)

        def back_two(at, n, total):
            value = norm_backward(r.GRAD[at] + total, 0, 0, at)
            r.GRAD[at] = value
            r.GLOW[at] = value.astype(bf)

        swapped(2, back_two)
        attention_back_start(0, 0)
        put_square(3, mm_tn(r.GLOW[...], r.O[0]))
        put_square(2, mm_tn(r.XT[...], r.DV[...]))
        rs_first(units, 0, 1)
        put_square(0, mm_tn(r.XT[...], r.DQ[...]))
        put_square(1, mm_tn(r.XT[...], r.DK[...]))
        rs_first(units, 0, 0)
        rs_second(units, 2, 0)
        rs_second(units, 2, 1)
        swap(3, all_sides(0))

        def back_three(at, n, total):
            r.GRAD[at] = r.GRAD[at] + total

        swapped(3, back_three)
        for target_ref, value in ((r.F_SRC, r.GRAD[0:BLOCK]), (r.SGSEND, r.GRAD[BLOCK:])):
            value = value.reshape(16, 8, 512)
            target_ref[...] = jnp.where(c == 0, value[:, 0:4], value[:, 4:8])
        local(r.F_SRC, r.o_src, 6).start()
        copy(r.SGSEND, r.SGREC, S_SG, partner).start()
        send_norm_sums()
        finish_unit(0, 6)
        rs_second(units, 1, 0)
        rs_second(units, 1, 1)
        rs_third(0, 2, 0)
        rs_third(0, 2, 1)
        take_target(0)
        finish_unit(0, 5)
        rs_second(units, 0, 1)
        rs_second(units, 0, 0)
        rs_third(0, 1, 0)
        rs_third(0, 1, 1)
        finish_unit(0, 4)
        finish_unit(0, 2)
        rs_third(0, 0, 1)
        rs_third(0, 0, 0)
        finish_unit(0, 3)
        wait_out(r.MREC.at[0], S_MEMORY)
        wait_out(r.SGSEND, S_SG)
        swaps_sent(4)
        spread_norm_sums()
        for g in (6, 5, 4):
            spread_unit(g)
        finish_unit(0, 1)
        spread_unit(2)
        spread_unit(3)
        finish_unit(0, 0)
        spread_unit(1)
        ag_sent(units)
        rs_sent(0, units)
        z_sent(0)
        wait_out(r.NB.at[0:15], S_NORM)
        wait_out(r.COT1, S_COT)
        wait_out(r.TSEND, S_TARGET)

    def send_norm_sums():
        r.NG[z] = r.NGR[z]
        for k in (1, 2, 3):
            zz, dev = z_mate(k)
            copy(r.NGR.at[zz], r.NG.at[z], S_NG, dev).start()

    def spread_norm_sums():
        wait_in(r.NG.at[0:3], S_NG)
        r.NH[yx] = in_order(r.NG)
        for dev in plane_mates():
            copy(r.NH.at[yx], r.NH.at[yx], S_NH, dev).start()

    def take_target(my_role):
        if my_role == 0:
            wait_in(r.TG.at[0], S_DT)
        else:
            wait_in(r.TG.at[0, 0:7], S_DT)
        hand_over(r.TG, S_DT2)
        for half in range(2):
            r.F_TGT[:, half * 256 : half * 256 + 256] = mm(
                r.PERMT[0], r.TG[half].reshape(BLOCK, 256)
            )
        local(r.F_TGT, r.o_tgt, 7).start()

    def decoder():
        units = DEC_UNITS
        clear_sums()
        for u in range(4):
            ag_forward(units, u, (0,))
        ag_column(units, 0)
        ag_forward(units, 0)
        ag_column(units, 1)
        ag_forward(units, 1)
        wait_in(r.TREC.at[0:15], S_TARGET)
        cot = r.COT

        def place(i):
            at = aligned(i, 32)
            both = jnp.concatenate(
                [
                    r.COT1[at].astype(f32).reshape(4, 1, 8, 512),
                    r.COT2[at].astype(f32).reshape(4, 1, 8, 512),
                ],
                axis=1,
            )
            cot[aligned(i, CHUNK)] = both.reshape(CHUNK, 512)

        r.XT[...] = r.TREC[:, :, 0:512].reshape(TOKENS, 512)

        def counts(which):
            def get(blk):
                ext = r.TREC[8 * blk : 8 * blk + 8, :, 512:640].reshape(BLOCK, LANES)
                return ext.astype(f32)[:, 32 * which : 32 * which + 1]

            return get

        make_masks(0, counts(1), True)
        make_masks(1, counts(0), False)
        read_norms()
        ag_column(units, 2)
        ag_column(units, 3)
        ag_finish(units, 0)
        x_in = r.XT[...]
        project_all(0, 0, x_in, x_in)
        attend(0, 0)
        swap(0, attention_out(0, 0))
        ag_forward(units, 2)

        def first(at, n, total):
            hidden = norm_forward(r.XT[at].astype(f32) + total, 0, 2, at)
            r.RES[at] = hidden
            r.LOW[0, at] = hidden.astype(bf)

        swapped(0, first)
        ag_forward(units, 3)
        ag_finish(units, 1)
        wait_in(r.COT2, S_COT)
        repeat(4, place)
        r.Q[1] = mm(r.LOW[0], weight(SQUARE, 4)).astype(bf)
        wait_in(r.MREC.at[0], S_MEMORY)
        hand_over(r.MREC, S_MEMORY2)
        for half in range(2):
            r.MEM[:, half * 256 : half * 256 + 256] = r.MREC[half].reshape(TOKENS, 256)
        memory = r.MEM[...]
        r.K[1] = mm(memory, weight(SQUARE, 5)).astype(bf)
        r.V[1] = mm(memory, weight(SQUARE, 6)).astype(bf)
        attend(1, 1)
        swap(1, attention_out(1, 4))

        def second(at, n, total):
            hidden = norm_forward(r.RES[at] + total, 1, 3, at)
            r.RES[at] = hidden
            r.LOW[1, at] = hidden.astype(bf)

        swapped(1, second)
        ag_finish(units, 2)
        expand(r.LOW[1])
        ag_finish(units, 3)
        swap(2, contract)

        def third(at, n, total):
            out = norm_forward(r.RES[at] + total, 2, 4, at)
            rows = aligned(n, 32)
            split = out.reshape(4, 2, 8, 512)
            r.F_DEC[rows] = split[:, 0].reshape(32, 512).astype(bf)
            r.DSEND[rows] = split[:, 1].reshape(32, 512).astype(bf)
            value = norm_backward(cot[at], 2, 4, at)
            r.GRAD[at] = value
            r.GLOW[at] = value.astype(bf)

        swapped(2, third)
        expand_back_hidden()
        swap(3, expand_input)
        for h in range(2):
            expand_back_down(h)
            rs_first(units, 3, h)
        copy(r.DSEND, r.DREC, S_DEC, partner).start()
        local(r.F_DEC, r.o_dec, 5).start()

        def back_two(at, n, total):
            value = norm_backward(r.GRAD[at] + total, 1, 3, at)
            r.GRAD[at] = value
            r.GLOW[at] = value.astype(bf)

        swapped(3, back_two)
        attention_back_start(1, 4)
        swap(4, key_side(4))
        for h in range(2):
            expand_back_up(r.LOW[1], h)

        def back_memory(at, n, total):
            r.LOW[2, at] = total.astype(bf)

        swapped(4, back_memory)
        r.DMSEND[...] = r.LOW[2].reshape(2, 2, 4, 16, 512)
        my_t = lax.div(z, 2) * 4 + yx
        for t in range(8):
            dev = (2 * (t // 4)) * 4 + t % 4
            copy(
                r.DMSEND.at[t // 4, :, t % 4, :, my_half], r.MG.at[c, my_t], S_DM, dev
            ).start()
        for h in range(2):
            rs_second(units, 3, h)
            rs_first(units, 2, h)
        swap(5, query_side(4))
        put_square(7, mm_tn(r.GLOW[...], r.O[1]))
        put_square(6, mm_tn(r.MEM[...], r.DV[...]))
        rs_first(units, 1, 1)
        put_square(5, mm_tn(r.MEM[...], r.DK[...]))
        put_square(4, mm_tn(r.LOW[0], r.DQ[...]))
        rs_first(units, 1, 0)

        def back_three(at, n, total):
            value = norm_backward(r.GRAD[at] + total, 0, 2, at)
            r.GRAD[at] = value
            r.GLOW[at] = value.astype(bf)

        swapped(5, back_three)
        attention_back_start(0, 0)
        swap(6, all_sides(0))
        put_square(3, mm_tn(r.GLOW[...], r.O[0]))
        put_square(2, mm_tn(r.XT[...], r.DV[...]))
        rs_first(units, 0, 1)
        put_square(0, mm_tn(r.XT[...], r.DQ[...]))
        put_square(1, mm_tn(r.XT[...], r.DK[...]))
        rs_third(1, 3, 0)
        rs_third(1, 3, 1)
        rs_second(units, 2, 0)
        rs_second(units, 2, 1)
        rs_first(units, 0, 0)

        def back_four(at, n, total):
            r.DTSEND[aligned(n, 4)] = (
                (r.GRAD[at] + total).astype(bf).reshape(4, 16, 512)
            )

        swapped(6, back_four)
        for k in range(1, 16):
            dev = lax.rem(d + k, 16)
            copy(r.DTSEND.at[dev, :, my_half], r.TG.at[c, my_t], S_DT, dev).start()
        r.TG[c, my_t] = r.DTSEND[d, :, my_half]
        send_norm_sums()
        rs_second(units, 1, 1)
        rs_third(1, 2, 0)
        rs_second(units, 1, 0)
        rs_third(1, 2, 1)
        finish_unit(1, 6)
        rs_second(units, 0, 1)
        rs_third(1, 1, 1)
        rs_second(units, 0, 0)
        rs_third(1, 1, 0)
        finish_unit(1, 5)
        take_target(1)
        rs_third(1, 0, 1)
        rs_third(1, 0, 0)
        finish_unit(1, 4)
        finish_unit(1, 2)
        wait_in(r.SGREC, S_SG)
        r.F_SRC[...] = r.SGREC[...]
        local(r.F_SRC, r.o_src, 6).start()
        wait_out(r.DTSEND.at[0:15, :, 0:256], S_DT)
        wait_out(r.MG.at[0], S_DM)
        wait_out(r.DSEND, S_DEC)
        swaps_sent(7)
        spread_norm_sums()
        for g in (6, 5, 4):
            spread_unit(g)
        finish_unit(1, 3)
        finish_unit(1, 1)
        spread_unit(2)
        spread_unit(3)
        finish_unit(1, 0)
        spread_unit(1)
        ag_sent(units)
        rs_sent(1, units)
        z_sent(1)
        wait_out(r.NB.at[0:15], S_NORM)
        wait_out(r.SEXT, S_EXT)
        wait_out(r.XHALF.at[0], S_SOURCE)
        wait_out(r.TSEND.at[0:7], S_TARGET)

    pl.when(role == 0)(encoder)
    pl.when(role == 1)(decoder)

    copy(r.RQ, r.RQR, S_RQ, d, 1 - c).start()
    wait_in(r.NH.at[0:3], S_NH)
    total = in_order(r.NH)
    r.o_ng[...] = pltpu.roll(total, lax.rem(LANES - shift, LANES), 1)
    r.o_rl[...] = total
    for g in (6, 5, 4, 2, 3, 1, 0):
        if g == 0:
            wait_in(r.SV.at[0:15], S_SV)
            total = r.SV[0]
            for i in range(1, 16):
                total = total + r.SV[i]
        else:
            wait_in(r.SU.at[g, 0:3], (S_SU, g))
            total = in_order(r.SU, (g,))
        r.TT[g] = jnp.broadcast_to(jnp.sum(total, axis=1, keepdims=True), (8, LANES))
        role_of, u = ALL_UNITS[g]
        kind, _, j = unit_mats(role_of, u)
        for h in range(8):
            if kind == SQUARE:
                r.o_cs[j + h // 2 : j + h // 2 + 1, (h % 2) * LANES : (h % 2 + 1) * LANES] = total[h : h + 1]
            else:
                r.o_cw[j : j + 1, h * LANES : (h + 1) * LANES] = total[h : h + 1]
    copy(r.TT, r.TTR, S_TT, d, 1 - c).start()
    wait_in(r.RQR, S_RQ)
    r.o_rq[...] = r.RQ[...] + r.RQR[...]
    wait_in(r.TTR, S_TT)
    r.o_tt[...] = r.TT[...] + r.TTR[...]
    wait_out(r.RQ, S_RQ)
    wait_out(r.TT, S_TT)
    wait_out(r.NG.at[0:3], S_NG)
    wait_out(r.NH.at[0:3], S_NH)
    wait_out(r.SV.at[0:15], S_SV)
    for g in range(1, 7):
        wait_out(r.ST.at[g, 0:3], (S_ST, g))
        wait_out(r.SU.at[g, 0:3], (S_SU, g))
    local(r.F_DEC, r.o_dec, 5).wait()
    local(r.F_SRC, r.o_src, 6).wait()
    local(r.F_TGT, r.o_tgt, 7).wait()
    for g in range(7):
        store_unit(g).wait()


UPDATE_INPUTS = dict(
    square=0,
    wide=0,
    norm=0,
    square_rows=0,
    square_cols=0,
    wide_rows=0,
    wide_cols=0,
    moment=0,
)
UPDATE_OUTPUTS = dict(
    decoded=((16, 4, 512), jnp.bfloat16),
    source_grad=((16, 4, 512), jnp.float32),
    target_grad=((16, 8, 512), jnp.float32),
    square_grad=((12, 32, 256), jnp.float32),
    square_rows_new=((12, 32), jnp.float32),
    square_cols_new=((12, 256), jnp.float32),
    square_new=((12, 32, 256), jnp.float32),
    square_copy=((12, 32, 256), jnp.bfloat16),
    wide_grad=((4, 32, 1024), jnp.float32),
    wide_rows_new=((4, 32), jnp.float32),
    wide_cols_new=((4, 1024), jnp.float32),
    wide_new=((4, 32, 1024), jnp.float32),
    wide_copy=((4, 32, 1024), jnp.bfloat16),
    norm_grad=((10, 32), jnp.float32),
    norm_second_new=((10, 32), jnp.float32),
    norm_new=((10, 32), jnp.float32),
    norm_copy=((10, 32), jnp.bfloat16),
)


def update_kernel(*refs):
    r = named(refs, OUTPUTS, UPDATE_INPUTS, UPDATE_OUTPUTS, dict(rows_pad=0))
    c = lax.axis_index("mp")
    bf, f32 = jnp.bfloat16, jnp.float32

    def own_half(value):
        value = value.astype(f32).reshape(16, 8, 512)
        return jnp.where(c == 0, value[:, 0:4], value[:, 4:8])

    r.decoded[...] = own_half(r.o_dec[...]).astype(bf)
    r.source_grad[...] = r.o_src[...]
    r.target_grad[...] = r.o_tgt[...].reshape(16, 8, 512)
    pad = r.rows_pad
    pad[...] = jnp.zeros((BLOCK, LANES), f32)
    pad[0:12, 0:32] = r.square_rows[...]
    pad[12:16, 0:32] = r.wide_rows[...]
    lanes = lax.broadcasted_iota(jnp.int32, (BLOCK, LANES), 1)
    widths = jnp.where(lanes < 12, 1.0 / 512, 1.0 / FF)
    rows_new = 0.5 * pad[...].T + 0.5 * (r.o_rq[...] * widths)
    rows_back = rows_new.T
    r.square_rows_new[...] = rows_back[0:12, 0:32]
    r.wide_rows_new[...] = rows_back[12:16, 0:32]
    square_cols = 0.5 * r.square_cols[...] + 0.5 * (r.o_cs[...] / 512)
    wide_cols = 0.5 * r.wide_cols[...] + 0.5 * (r.o_cw[...] / 512)
    r.square_cols_new[...] = square_cols
    r.wide_cols_new[...] = wide_cols

    def level(m, total, width):
        return (0.5 * r.o_rl[10:11, m : m + 1] + 0.5 * (total / width)) / 512

    def update(master, grad, row, col, lvl):
        return master - RATE * grad * lax.rsqrt(row * col / lvl)

    for g, (role, u) in enumerate(ALL_UNITS):
        kind, _, j = unit_mats(role, u)
        if kind == SQUARE:
            for m in range(4):
                sums = r.o_tt[g]
                total = sums[2 * m : 2 * m + 1, 0:1] + sums[2 * m + 1 : 2 * m + 2, 0:1]
                grad = r.o_gs[j + m]
                new = update(
                    r.square[j + m],
                    grad,
                    rows_new[0:32, j + m : j + m + 1],
                    square_cols[j + m : j + m + 1],
                    level(j + m, total, 512),
                )
                r.square_grad[j + m] = grad
                r.square_new[j + m] = new
                r.square_copy[j + m] = new.astype(bf)
        else:
            total = jnp.sum(r.o_tt[g], axis=0, keepdims=True)[:, 0:1]
            grad = r.o_gw[j]
            new = update(
                r.wide[j],
                grad,
                rows_new[0:32, 12 + j : 13 + j],
                wide_cols[j : j + 1],
                level(12 + j, total, FF),
            )
            r.wide_grad[j] = grad
            r.wide_new[j] = new
            r.wide_copy[j] = new.astype(bf)
    norm_grad = r.o_ng[0:10, 0:32]
    second = 0.5 * r.moment[...] + 0.5 * norm_grad * norm_grad
    norm_new = r.norm[...] - NORM_RATE * norm_grad * lax.rsqrt(second)
    r.norm_grad[...] = norm_grad
    r.norm_second_new[...] = second
    r.norm_new[...] = norm_new
    r.norm_copy[...] = norm_new.astype(bf)


def small_shards(
    source,
    target,
    lengths,
    destinations,
    cotangent,
    square_master,
    wide_master,
    norm_master,
    square_rows,
    square_cols,
    wide_rows,
    wide_cols,
    gain_offset_moment,
):
    vmem = pl.BlockSpec(memory_space=pltpu.VMEM)
    smem = pl.BlockSpec(memory_space=pltpu.SMEM)
    anywhere = pl.BlockSpec(memory_space=pl.ANY)
    moved = pl.pallas_call(
        exchange_kernel,
        out_shape=[jax.ShapeDtypeStruct(*v) for v in OUTPUTS.values()],
        in_specs=[smem, smem] + [anywhere] * 5 + [vmem] * 3,
        out_specs=[anywhere] * 5 + [vmem] * (len(OUTPUTS) - 5),
        scratch_shapes=[pltpu.VMEM(*v) for v in SCRATCH.values()]
        + [pltpu.SemaphoreType.DMA((n,)) for n in (SEM_COUNT, SEM_COUNT, NEAR_COUNT)],
        compiler_params=pltpu.CompilerParams(
            collective_id=0, has_side_effects=True, vmem_limit_bytes=56 << 20
        ),
    )(
        lengths.T,
        destinations,
        source.reshape(BLOCK, 512),
        target.reshape(BLOCK, 512),
        cotangent.reshape(BLOCK, 512),
        square_master,
        wide_master,
        norm_master,
        square_rows,
        wide_rows,
    )
    return tuple(
        pl.pallas_call(
            update_kernel,
            out_shape=[jax.ShapeDtypeStruct(*v) for v in UPDATE_OUTPUTS.values()],
            in_specs=[vmem] * (len(OUTPUTS) + len(UPDATE_INPUTS)),
            out_specs=[vmem] * len(UPDATE_OUTPUTS),
            scratch_shapes=[pltpu.VMEM((BLOCK, LANES), jnp.float32)],
            compiler_params=pltpu.CompilerParams(vmem_limit_bytes=60 << 20),
        )(
            *moved,
            square_master,
            wide_master,
            norm_master,
            square_rows,
            square_cols,
            wide_rows,
            wide_cols,
            gain_offset_moment,
        )
    )


def solution(mesh):
    return jax.shard_map(
        small_shards if dict(mesh.shape) == {"dp": 16, "mp": 2} else shards,
        mesh=mesh,
        in_specs=(
            P("dp", None, None),
            P("dp", None, None),
            P("dp", None),
            P("dp"),
            P("dp", None, None),
            P(None, "dp", "mp"),
            P(None, "dp", "mp"),
            P(None, "dp"),
            P(None, "dp"),
            P(None, "mp"),
            P(None, "dp"),
            P(None, "mp"),
            P(None, "dp"),
        ),
        out_specs=(
            P("dp", "mp", None),
            P("dp", "mp", None),
            P("dp", None, None),
            P(None, "dp", "mp"),
            P(None, "dp"),
            P(None, "mp"),
            P(None, "dp", "mp"),
            P(None, "dp", "mp"),
            P(None, "dp", "mp"),
            P(None, "dp"),
            P(None, "mp"),
            P(None, "dp", "mp"),
            P(None, "dp", "mp"),
            P(None, "dp"),
            P(None, "dp"),
            P(None, "dp"),
            P(None, "dp"),
        ),
        check_vma=False,
    )
```

```python
import types

import jax
import jax.numpy as jnp
from jax import lax
from jax.experimental import pallas as pl
from jax.experimental.pallas import tpu as pltpu
from jax.sharding import PartitionSpec as P

FF = 2048
HEADS = 8
MICRO = 2


RATE = 0.03
NORM_RATE = 0.2


def rounded(input_tensor):
    return input_tensor.astype(jnp.bfloat16)


def identity(input_tensor):
    return input_tensor


def project(input_tensor, weight_matrix):
    return jnp.einsum(
        "rft,tv->rfv", input_tensor, weight_matrix, preferred_element_type=jnp.float32
    )


def project_back(input_tensor, weight_matrix):
    return jnp.einsum(
        "cxk,ak->cxa", input_tensor, weight_matrix, preferred_element_type=jnp.float32
    )


def outer_sum(first_factor_array, second_factor_array):
    return jnp.einsum(
        "zmb,zmf->bf", first_factor_array, second_factor_array, preferred_element_type=jnp.float32
    )


def split_heads(input_tensor, head_size):
    return input_tensor.reshape(
        input_tensor.shape[0], input_tensor.shape[1], input_tensor.shape[2] // head_size, head_size
    )


def merge_heads(input_tensor):
    return input_tensor.reshape(
        input_tensor.shape[0], input_tensor.shape[1], input_tensor.shape[2] * input_tensor.shape[3]
    )


def layer_norm(residual, gain_row, bias_row):
    centred = residual - jnp.mean(residual, axis=-1, keepdims=True)
    spread = lax.rsqrt(jnp.mean(centred * centred, axis=-1, keepdims=True) + 1e-05)
    normed = centred * spread
    return (normed * gain_row + bias_row, (normed, spread))


def norm_back(upstream, gain_row, kept_state, pick):
    normed, spread = kept_state
    scaled = upstream * gain_row
    centred_grad = (
        scaled
        - jnp.mean(scaled, axis=-1, keepdims=True)
        - normed * jnp.mean(scaled * normed, axis=-1, keepdims=True)
    )
    return (
        centred_grad * spread,
        jnp.sum(pick(upstream * normed), axis=(0, 1)),
        jnp.sum(pick(upstream), axis=(0, 1)),
    )


def attend_forward(query_in, key_in, matrices, start_index, allowed, head_size):
    queries = split_heads(rounded(project(query_in, matrices[start_index])), head_size)
    key_rows = split_heads(rounded(project(key_in, matrices[start_index + 1])), head_size)
    content_lines = split_heads(rounded(project(key_in, matrices[start_index + 2])), head_size)
    scores = jnp.einsum(
        "sqhe,skhe->shqk", queries, key_rows, preferred_element_type=jnp.float32
    ) * head_size ** (-0.5)
    scores = jnp.where(allowed[:, None], scores, -1000000000.0)
    attn_probs = jax.nn.softmax(scores, axis=-1)
    probs_low = rounded(attn_probs)
    mixed_heads = rounded(
        merge_heads(
            jnp.einsum(
                "shqk,skhe->sqhe", probs_low, content_lines, preferred_element_type=jnp.float32
            )
        )
    )
    partial_value = project_back(mixed_heads, matrices[start_index + 3])
    return (partial_value, (queries, key_rows, content_lines, attn_probs, probs_low, mixed_heads))


def attend_back(upstream, query_in, key_in, matrices, start_index, kept_state, head_size):
    queries, key_rows, content_lines, attn_probs, probs_low, mixed_heads = kept_state
    scale = head_size ** (-0.5)
    out_grad = outer_sum(upstream, mixed_heads)
    mixed_grad = split_heads(rounded(project(upstream, matrices[start_index + 3])), head_size)
    prob_grad = jnp.einsum(
        "sqhe,skhe->shqk", mixed_grad, content_lines, preferred_element_type=jnp.float32
    )
    value_grad = rounded(
        jnp.einsum("shqk,sqhe->skhe", probs_low, mixed_grad, preferred_element_type=jnp.float32)
    )
    score_grad = rounded(
        attn_probs * (prob_grad - jnp.sum(attn_probs * prob_grad, axis=-1, keepdims=True))
    )
    query_grad = rounded(
        jnp.einsum("shqk,skhe->sqhe", score_grad, key_rows, preferred_element_type=jnp.float32)
        * scale
    )
    key_grad = rounded(
        jnp.einsum("shqk,sqhe->skhe", score_grad, queries, preferred_element_type=jnp.float32)
        * scale
    )
    query_grad = merge_heads(query_grad)
    key_grad = merge_heads(key_grad)
    value_grad = merge_heads(value_grad)
    weight_grads = (
        outer_sum(query_in, query_grad),
        outer_sum(key_in, key_grad),
        outer_sum(key_in, value_grad),
        out_grad,
    )
    asking_piece = project_back(query_grad, matrices[start_index])
    key_part = project_back(key_grad, matrices[start_index + 1]) + project_back(
        value_grad, matrices[start_index + 2]
    )
    return (asking_piece, key_part, weight_grads)


def expand_forward(inputs, matrices, start_index):
    hidden = project(inputs, matrices[start_index])
    active = rounded(jax.nn.gelu(hidden))
    return (project_back(active, matrices[start_index + 1]), (hidden, active))


def expand_back(upstream, inputs, matrices, start_index, kept_state):
    hidden, active = kept_state
    down_grad = outer_sum(upstream, active)
    active_grad = rounded(project(upstream, matrices[start_index + 1]))
    unused, pullback = jax.vjp(jax.nn.gelu, hidden)
    hidden_grad = rounded(pullback(active_grad.astype(jnp.float32))[0])
    up_grad = outer_sum(inputs, hidden_grad)
    return (project_back(hidden_grad, matrices[start_index]), up_grad, down_grad)


def accumulate(totals, position, addend):
    totals[position] = addend if totals[position] is None else totals[position] + addend


def shards(
    source,
    target,
    lengths,
    destinations,
    cotangent,
    square_master,
    wide_master,
    norm_master,
    square_rows,
    square_cols,
    wide_rows,
    wide_cols,
    gain_offset_moment,
):
    peer_count = lax.axis_size("dp")
    sent_dev = source.shape[0]
    slot_count = source.shape[1]
    model_width = source.shape[2]
    per_peer = sent_dev // peer_count
    head_size = model_width // HEADS
    per_block = sent_dev // MICRO
    half_len = slot_count // lax.axis_size("mp")
    half_start = lax.axis_index("mp") * half_len
    send_order = jnp.argsort(destinations, stable=True)
    home_place = jnp.argsort(send_order, stable=True)

    def own_half(input_tensor):
        return lax.dynamic_slice_in_dim(input_tensor, half_start, half_len, 1)

    def share_total(partial_value):
        return lax.psum_scatter(partial_value, "mp", scatter_dimension=1, tiled=True)

    def add_branch(residual, partial_value):
        return residual + share_total(partial_value)

    def low_rows(value):
        return lax.all_gather(rounded(value), "mp", axis=1, tiled=True)

    def by_peer(input_tensor):
        return jnp.take(input_tensor, send_order, axis=0).reshape(
            (peer_count, per_peer) + input_tensor.shape[1:]
        )

    def flatten(input_tensor):
        return input_tensor.reshape((sent_dev,) + input_tensor.shape[2:])

    moved_lengths = flatten(
        lax.all_to_all(by_peer(lengths), "dp", split_axis=0, concat_axis=0, tiled=True)
    )
    square_low, wide_low, norm_low = (
        lax.all_gather(rounded(square_master), "dp", axis=1, tiled=True),
        lax.all_gather(rounded(wide_master), "dp", axis=1, tiled=True),
        lax.all_gather(rounded(norm_master), "dp", axis=1, tiled=True),
    )
    gain_rows = norm_low[:5].astype(jnp.float32)
    bias_rows = norm_low[5:].astype(jnp.float32)
    positions = jnp.arange(slot_count)
    causal = positions[None, :] <= positions[:, None]

    def key_mask(counts):
        return jnp.broadcast_to(
            positions[None, None, :] < counts[:, None, None],
            (counts.shape[0], slot_count, slot_count),
        )

    square_grads = [None] * 12
    wide_grads = [None] * 4
    gain_grads = [None] * 5
    bias_grads = [None] * 5

    def norm_step(upstream, position, kept_state):
        residual_grad, gain_grad, bias_grad = norm_back(
            upstream, gain_rows[position], kept_state, identity
        )
        accumulate(gain_grads, position, gain_grad)
        accumulate(bias_grads, position, bias_grad)
        return residual_grad

    def attend_step(upstream_low, query_in, key_in, start_index, kept_state):
        asking_piece, key_part, weight_grads = attend_back(
            upstream_low, query_in, key_in, square_low, start_index, kept_state, head_size
        )
        for offset in range(4):
            accumulate(square_grads, start_index + offset, weight_grads[offset])
        return (asking_piece, key_part)

    def expand_step(upstream_low, inputs, start_index, kept_state):
        partial_value, up_grad, down_grad = expand_back(
            upstream_low, inputs, wide_low, start_index, kept_state
        )
        accumulate(wide_grads, start_index, up_grad)
        accumulate(wide_grads, start_index + 1, down_grad)
        return partial_value

    encoder_kept = []
    encoded_pieces = []
    for micro_index in range(MICRO):
        row_start = micro_index * per_block
        source_block = source[row_start : row_start + per_block]
        allowed = key_mask(lengths[row_start : row_start + per_block, 0])
        partial_value, attend_kept = attend_forward(
            source_block, source_block, square_low, 0, allowed, head_size
        )
        hidden, hidden_kept = layer_norm(
            add_branch(own_half(source_block).astype(jnp.float32), partial_value),
            gain_rows[0],
            bias_rows[0],
        )
        hidden_low = low_rows(hidden)
        partial_value, expand_kept = expand_forward(hidden_low, wide_low, 0)
        memory, memory_kept = layer_norm(
            add_branch(hidden, partial_value), gain_rows[1], bias_rows[1]
        )
        encoded_pieces.append(low_rows(memory))
        encoder_kept.append((attend_kept, hidden_kept, hidden_low, expand_kept, memory_kept))
    memory_all = jnp.concatenate(encoded_pieces, axis=0)
    moved_memory, moved_target = (
        lax.all_to_all(by_peer(memory_all), "dp", split_axis=0, concat_axis=0, tiled=True),
        lax.all_to_all(by_peer(target), "dp", split_axis=0, concat_axis=0, tiled=True),
    )
    moved_memory = flatten(moved_memory)
    moved_target = flatten(moved_target)
    decoded_parts = []
    memory_back = []
    target_back = []
    for micro_index in range(MICRO):
        row_start = micro_index * per_block
        target_block = moved_target[row_start : row_start + per_block]
        memory_block = moved_memory[row_start : row_start + per_block]
        counts = moved_lengths[row_start : row_start + per_block]
        self_mask = key_mask(counts[:, 1]) & causal[None]
        cross_attention_mask = key_mask(counts[:, 0])
        partial_value, self_kept = attend_forward(
            target_block, target_block, square_low, 4, self_mask, head_size
        )
        first_norm, first_kept = layer_norm(
            add_branch(own_half(target_block).astype(jnp.float32), partial_value),
            gain_rows[2],
            bias_rows[2],
        )
        first_low = low_rows(first_norm)
        partial_value, cross_kept = attend_forward(
            first_low, memory_block, square_low, 8, cross_attention_mask, head_size
        )
        second_norm, second_kept = layer_norm(
            add_branch(first_norm, partial_value), gain_rows[3], bias_rows[3]
        )
        second_low = low_rows(second_norm)
        partial_value, expand_kept = expand_forward(second_low, wide_low, 2)
        output, output_kept = layer_norm(
            add_branch(second_norm, partial_value), gain_rows[4], bias_rows[4]
        )
        decoded_parts.append(identity(rounded(output)))
        upstream = norm_step(
            own_half(cotangent[row_start : row_start + per_block]).astype(jnp.float32),
            4,
            output_kept,
        )
        upstream = add_branch(upstream, expand_step(low_rows(upstream), second_low, 2, expand_kept))
        upstream = norm_step(upstream, 3, second_kept)
        asking_piece, key_part = attend_step(
            low_rows(upstream), first_low, memory_block, 8, cross_kept
        )
        asking_piece, key_part = share_total((asking_piece, key_part))
        memory_back.append(low_rows(key_part))
        upstream = norm_step(upstream + asking_piece, 2, first_kept)
        asking_piece, key_part = attend_step(
            low_rows(upstream), target_block, target_block, 4, self_kept
        )
        target_back.append(low_rows(add_branch(upstream, asking_piece + key_part)))
    returned_memory, returned_target = (
        lax.all_to_all(
            jnp.concatenate(memory_back, axis=0).reshape(
                peer_count, per_peer, slot_count, model_width
            ),
            "dp",
            split_axis=0,
            concat_axis=0,
            tiled=True,
        ),
        lax.all_to_all(
            jnp.concatenate(target_back, axis=0).reshape(
                peer_count, per_peer, slot_count, model_width
            ),
            "dp",
            split_axis=0,
            concat_axis=0,
            tiled=True,
        ),
    )
    memory_gradient = jnp.take(flatten(returned_memory), home_place, axis=0)
    target_grad = jnp.take(flatten(returned_target), home_place, axis=0).astype(jnp.float32)
    source_parts = []
    for micro_index in range(MICRO):
        row_start = micro_index * per_block
        source_block = source[row_start : row_start + per_block]
        attend_kept, hidden_kept, hidden_low, expand_kept, memory_kept = encoder_kept[micro_index]
        upstream = norm_step(
            own_half(memory_gradient[row_start : row_start + per_block]).astype(jnp.float32),
            1,
            memory_kept,
        )
        upstream = add_branch(upstream, expand_step(low_rows(upstream), hidden_low, 0, expand_kept))
        upstream = norm_step(upstream, 0, hidden_kept)
        asking_piece, key_part = attend_step(
            low_rows(upstream), source_block, source_block, 0, attend_kept
        )
        source_parts.append(identity(add_branch(upstream, asking_piece + key_part)))
    square_grad = jnp.stack(square_grads)
    wide_grad = jnp.stack(wide_grads)
    norm_grad = jnp.stack(gain_grads + bias_grads)
    square_grad, wide_grad, norm_grad = (
        lax.psum_scatter(square_grad, "dp", scatter_dimension=1, tiled=True),
        lax.psum_scatter(wide_grad, "dp", scatter_dimension=1, tiled=True),
        lax.psum_scatter(norm_grad, "dp", scatter_dimension=1, tiled=True),
    )
    row_square, row_wide, norm_grad = lax.psum(
        (
            jnp.sum(square_grad * square_grad, axis=2),
            jnp.sum(wide_grad * wide_grad, axis=2),
            norm_grad,
        ),
        "mp",
    )
    square_rows_new = 0.5 * square_rows + 0.5 * (row_square / model_width)
    wide_rows_new = 0.5 * wide_rows + 0.5 * (row_wide / FF)
    col_square, col_wide, level_square, level_wide = lax.psum(
        (
            jnp.sum(square_grad * square_grad, axis=1),
            jnp.sum(wide_grad * wide_grad, axis=1),
            jnp.sum(square_rows_new, axis=1),
            jnp.sum(wide_rows_new, axis=1),
        ),
        "dp",
    )
    square_cols_new = 0.5 * square_cols + 0.5 * (col_square / model_width)
    wide_cols_new = 0.5 * wide_cols + 0.5 * (col_wide / model_width)
    square_second = (
        square_rows_new[:, :, None]
        * square_cols_new[:, None, :]
        / (level_square / model_width)[:, None, None]
    )
    wide_second = (
        wide_rows_new[:, :, None]
        * wide_cols_new[:, None, :]
        / (level_wide / model_width)[:, None, None]
    )
    updated_square_masters = square_master - RATE * square_grad * lax.rsqrt(square_second)
    wide_new = wide_master - RATE * wide_grad * lax.rsqrt(wide_second)
    norm_second_new = 0.5 * gain_offset_moment + 0.5 * norm_grad * norm_grad
    norm_new = norm_master - NORM_RATE * norm_grad * lax.rsqrt(norm_second_new)
    return (
        jnp.concatenate(decoded_parts, axis=0),
        jnp.concatenate(source_parts, axis=0),
        target_grad,
        square_grad,
        square_rows_new,
        square_cols_new,
        updated_square_masters,
        rounded(updated_square_masters),
        wide_grad,
        wide_rows_new,
        wide_cols_new,
        wide_new,
        rounded(wide_new),
        norm_grad,
        norm_second_new,
        norm_new,
        rounded(norm_new),
    )


SQUARE, WIDE = 0, 1
LANES = 128
TOKENS = 256
BLOCK = 128
CHUNK = 64
MESH_IDS = pl.DeviceIdType.MESH
NEG = -1000000000.0
OUTSIDE = -3.0e38
ENC_UNITS = ((SQUARE, 0), (WIDE, 0), (WIDE, 1))
DEC_UNITS = ((SQUARE, 0), (SQUARE, 1), (WIDE, 0), (WIDE, 1))
ALL_UNITS = ((0, 0), (0, 1), (0, 2), (1, 0), (1, 1), (1, 2), (1, 3))


def mm(a, b):
    return jnp.dot(a, b, preferred_element_type=jnp.float32)


def mm_nt(a, b):
    return lax.dot_general(a, b, (((1,), (1,)), ((), ())), preferred_element_type=jnp.float32)


def mm_tn(a, b):
    return lax.dot_general(a, b, (((0,), (0,)), ((), ())), preferred_element_type=jnp.float32)


def repeat(count, body):
    lax.fori_loop(0, count, lambda i, carry: (body(i), carry)[1], 0, unroll=True)


def aligned(i, size):
    return pl.ds(pl.multiple_of(i * size, size), size)


def unit_mats(role, u):
    kind, i = (ENC_UNITS, DEC_UNITS)[role][u]
    if kind == SQUARE:
        return kind, i, 4 * i + 4 * role
    return kind, i, i + 2 * role


def named(refs, *groups):
    return types.SimpleNamespace(**dict(zip([name for group in groups for name in group], refs)))


class Sems:
    def __init__(self, send, recv, count):
        self.send, self.recv, self.count, self.names = send, recv, count, {}

    def at(self, name):
        i = self.names.setdefault(name, len(self.names))
        assert i < self.count
        return self.send.at[i], self.recv.at[i]


SEM_COUNT = 240
NEAR_COUNT = 18
(
    S_AX,
    S_AY,
    S_COT,
    S_DEC,
    S_DM,
    S_DT,
    S_FX,
    S_FY,
    S_M,
    S_MEMORY,
    S_NG,
    S_NORM,
    S_RA,
    S_RB,
    S_RQ,
    S_SA,
    S_SB,
    S_SG,
    S_SOURCE,
    S_ST,
    S_SU,
    S_SV,
    S_NH,
    S_EXT,
    S_SOURCE2,
    S_MEMORY2,
    S_DM2,
    S_DT2,
    S_T,
    S_TARGET,
    S_TT,
    S_Z,
) = range(32)

SCRATCH = dict(
    WS=((8, 4, 2, 2, 32, 256), jnp.bfloat16),
    WW=((2, 4, 2, 2, 32, 1024), jnp.bfloat16),
    GS=((8, 4, 2, 2, 32, 256), jnp.bfloat16),
    GW=((2, 4, 2, 2, 32, 1024), jnp.bfloat16),
    SB=((12, 32, 256), jnp.bfloat16),
    WB=((4, 32, 1024), jnp.bfloat16),
    R1AS=((8, 2, 2, 32, 256), jnp.bfloat16),
    R1BS=((8, 2, 2, 32, 256), jnp.bfloat16),
    R1AW=((2, 2, 2, 32, 1024), jnp.bfloat16),
    R1BW=((2, 2, 2, 32, 1024), jnp.bfloat16),
    R2AS=((8, 2, 32, 256), jnp.bfloat16),
    R2BS=((8, 2, 32, 256), jnp.bfloat16),
    R2AW=((2, 2, 32, 1024), jnp.bfloat16),
    R2BW=((2, 2, 32, 1024), jnp.bfloat16),
    R3S=((2, 12, 32, 256), jnp.bfloat16),
    R3W=((2, 4, 32, 1024), jnp.bfloat16),
    NB=((16, 16, LANES), jnp.bfloat16),
    RL=((16, LANES), jnp.float32),
    NORM=((16, 512), jnp.float32),
    EXT=((BLOCK, LANES), jnp.float32),
    SEXT=((BLOCK, LANES), jnp.bfloat16),
    XHALF=((2, BLOCK, 256), jnp.bfloat16),
    XEXT=((BLOCK, LANES), jnp.bfloat16),
    TSEND=((8, 16, 640), jnp.bfloat16),
    TREC=((16, 16, 640), jnp.bfloat16),
    COT2=((BLOCK, 512), jnp.bfloat16),
    COT=((TOKENS, 512), jnp.float32),
    XT=((TOKENS, 512), jnp.bfloat16),
    MSEND=((8, 2, 16, 512), jnp.bfloat16),
    MREC=((2, 2, 2, 4, 16, 256), jnp.bfloat16),
    MEM=((TOKENS, 512), jnp.bfloat16),
    DMSEND=((2, 2, 4, 16, 512), jnp.bfloat16),
    MG=((2, 8, 2, 16, 256), jnp.bfloat16),
    DTSEND=((16, 16, 512), jnp.bfloat16),
    TG=((2, 8, 16, 256), jnp.bfloat16),
    DSEND=((BLOCK, 512), jnp.bfloat16),
    DREC=((BLOCK, 512), jnp.bfloat16),
    SGSEND=((16, 4, 512), jnp.float32),
    SGREC=((16, 4, 512), jnp.float32),
    PERMT=((2, BLOCK, BLOCK), jnp.bfloat16),
    ALLOW=((2, 2, BLOCK, TOKENS), jnp.float32),
    FILL=((BLOCK, TOKENS), jnp.float32),
    Q=((2, TOKENS, 256), jnp.bfloat16),
    K=((2, TOKENS, 256), jnp.bfloat16),
    V=((2, TOKENS, 256), jnp.bfloat16),
    O=((2, TOKENS, 256), jnp.bfloat16),
    PROB=((2, 4, BLOCK, TOKENS), jnp.float32),
    DO=((TOKENS, 256), jnp.bfloat16),
    DQ=((TOKENS, 256), jnp.bfloat16),
    DK=((TOKENS, 256), jnp.bfloat16),
    DV=((TOKENS, 256), jnp.bfloat16),
    U=((TOKENS, 1024), jnp.float32),
    ACT=((TOKENS, 1024), jnp.bfloat16),
    DU=((TOKENS, 1024), jnp.bfloat16),
    RES=((TOKENS, 512), jnp.float32),
    LOW=((3, TOKENS, 512), jnp.bfloat16),
    XH=((3, TOKENS, 512), jnp.float32),
    RSD=((3, TOKENS, 1), jnp.float32),
    GRAD=((TOKENS, 512), jnp.float32),
    GLOW=((TOKENS, 512), jnp.bfloat16),
    PS=((2, TOKENS, 512), jnp.bfloat16),
    PR=((2, TOKENS, 512), jnp.bfloat16),
    NGR=((4, 16, LANES), jnp.float32),
    NG=((4, 16, LANES), jnp.float32),
    NH=((4, 16, LANES), jnp.float32),
    ST=((7, 4, 8, LANES), jnp.float32),
    SU=((7, 4, 8, LANES), jnp.float32),
    SV=((16, 8, LANES), jnp.float32),
    RQ=((BLOCK, LANES), jnp.float32),
    RQR=((BLOCK, LANES), jnp.float32),
    TT=((7, 8, LANES), jnp.float32),
    SM=((12, 32, 256), jnp.float32),
    WM=((4, 32, 1024), jnp.float32),
    SRC=((BLOCK, 512), jnp.bfloat16),
    TGT=((BLOCK, 512), jnp.bfloat16),
    I_NORM=((10, 32), jnp.float32),
    I_SR=((12, 32), jnp.float32),
    I_WR=((4, 32), jnp.float32),
    COT1=((BLOCK, 512), jnp.bfloat16),
    F_DEC=((BLOCK, 512), jnp.bfloat16),
    F_SRC=((16, 4, 512), jnp.float32),
    F_TGT=((16, 8, 512), jnp.float32),
    F_GS=((12, 32, 256), jnp.float32),
    F_GW=((4, 32, 1024), jnp.float32),
    TTR=((7, 8, LANES), jnp.float32),
)

INPUTS = dict(
    lengths=0,
    destinations=0,
    source=0,
    target=0,
    cotangent=0,
    square=0,
    wide=0,
    norm=0,
    square_rows=0,
    wide_rows=0,
)
OUTPUTS = dict(
    o_dec=((BLOCK, 512), jnp.bfloat16),
    o_src=((16, 4, 512), jnp.float32),
    o_tgt=((16, 8, 512), jnp.float32),
    o_gs=((12, 32, 256), jnp.float32),
    o_gw=((4, 32, 1024), jnp.float32),
    o_cs=((12, 256), jnp.float32),
    o_cw=((4, 1024), jnp.float32),
    o_rq=((BLOCK, LANES), jnp.float32),
    o_rl=((16, LANES), jnp.float32),
    o_tt=((7, 8, LANES), jnp.float32),
    o_ng=((16, LANES), jnp.float32),
)


def exchange_kernel(*refs):
    r = named(refs, INPUTS, OUTPUTS, SCRATCH)
    sems = Sems(refs[-3], refs[-2], SEM_COUNT)
    near = refs[-1]
    d = lax.axis_index("dp")
    c = lax.axis_index("mp")
    z = lax.div(d, 4)
    yx = lax.rem(d, 4)
    y = lax.div(yx, 2)
    x = lax.rem(yx, 2)
    role = lax.rem(z, 2)
    x_mate = d + 1 - 2 * x
    y_mate = d + 2 - 4 * y
    partner = d + 4 - 8 * role
    bf, f32 = jnp.bfloat16, jnp.float32

    G = (r.GS, r.GW)
    R1A, R1B = (r.R1AS, r.R1AW), (r.R1BS, r.R1BW)
    R2A, R2B = (r.R2AS, r.R2AW), (r.R2BS, r.R2BW)

    def z_mate(k):
        zz = lax.rem(z + k, 4)
        return zz, zz * 4 + yx

    def copy(src, dst, name, dev, core=None):
        send, recv = sems.at(name)
        return pltpu.make_async_remote_copy(
            src_ref=src,
            dst_ref=dst,
            send_sem=send,
            recv_sem=recv,
            device_id=(dev, c if core is None else core),
            device_id_type=MESH_IDS,
        )

    def local(src, dst, i):
        return pltpu.make_async_copy(src, dst, near.at[i])

    my_half = pl.ds(pl.multiple_of(c * 256, 256), 256)

    def hand_over(ref, name):
        copy(ref.at[c], ref.at[c], name, d, 1 - c).start()
        wait_in(ref.at[0], name)
        wait_out(ref.at[0], name)

    def plane_mates():
        return (x_mate, y_mate, z * 4 + 3 - yx)

    def in_order(ref, lead=()):
        total = ref[lead + (0,)]
        for i in range(1, 4):
            total = total + ref[lead + (i,)]
        return total

    def wait_in(dst, name):
        copy(dst, dst, name, x_mate).wait_recv()

    def wait_out(src, name):
        copy(src, src, name, x_mate).wait_send()

    loads = [
        local(r.target, r.TGT, 0),
        local(r.source, r.SRC, 1),
        local(r.square, r.SM, 2),
        local(r.wide, r.WM, 3),
        local(r.cotangent, r.COT1, 4),
        local(r.norm, r.I_NORM, 15),
        local(r.square_rows, r.I_SR, 16),
        local(r.wide_rows, r.I_WR, 17),
    ]
    for i in (2, 3, 5, 6, 7, 1, 0, 4):
        loads[i].start()
    barrier = pltpu.get_barrier_semaphore()
    for k in range(1, 16):
        pl.semaphore_signal(
            barrier, inc=1, device_id=(lax.rem(d + k, 16), c), device_id_type=MESH_IDS
        )
    pl.semaphore_signal(barrier, inc=1, device_id=(d, 1 - c), device_id_type=MESH_IDS)

    row_id = lax.broadcasted_iota(jnp.int32, (BLOCK, BLOCK), 0)
    col_id = lax.broadcasted_iota(jnp.int32, (BLOCK, BLOCK), 1)
    col_z = 2 * (col_id >> 6) + 1 - ((col_id >> 3) & 1)
    col_dev = (col_z * 4 + ((col_id >> 4) & 3)).astype(f32)
    same_slot = (row_id & 7) == (col_id & 7)

    def perm_of(dest_column):
        return jnp.where((dest_column == col_dev) & same_slot, 1.0, 0.0)

    def cast_weights(role_of, u):
        kind, i, j = unit_mats(role_of, u)
        if kind == SQUARE:
            for m in range(4):
                r.SB[j + m] = r.SM[j + m].astype(bf)

            @pl.when(role == role_of)
            def _():
                for m in range(4):
                    r.WS[4 * i + m, z, y, x] = r.SB[j + m]

        else:
            r.WB[j] = r.WM[j].astype(bf)

            @pl.when(role == role_of)
            def _():
                r.WW[i, z, y, x] = r.WB[j]

    def z_slot(kind, i, k=0, yy=None, xx=None):
        zz = lax.rem(z + 4 - k, 4)
        at = (zz, y if yy is None else yy, x if xx is None else xx)
        if kind == SQUARE:
            return r.WS.at[(slice(4 * i, 4 * i + 4),) + at]
        return r.WW.at[(i,) + at]

    def z_send(my_role, target_role, u):
        kind, i, j = unit_mats(target_role, u)
        src = r.SB.at[j : j + 4] if kind == SQUARE else r.WB.at[j]
        for k in (2,) if my_role == target_role else (1, 3):
            copy(src, z_slot(kind, i), (S_Z, u, k), z_mate(k)[1]).start()

    def z_sent(my_role):
        for target_role, u in ALL_UNITS:
            kind, i, j = unit_mats(target_role, u)
            src = r.SB.at[j : j + 4] if kind == SQUARE else r.WB.at[j]
            for k in (2,) if my_role == target_role else (1, 3):
                wait_out(src, (S_Z, u, k))

    def send_norms():
        for k in range(1, 16):
            dev = lax.rem(d + k, 16)
            copy(r.NB.at[d], r.NB.at[d], S_NORM, dev).start()

    def send_target(my_role):
        for t in range(8):
            dev = (2 * (t // 4) + 1) * 4 + t % 4
            send = copy(r.TSEND.at[t], r.TREC.at[d], S_TARGET, dev)
            if my_role == 0:
                send.start()
            else:
                pl.when(dev != d)(send.start)

                @pl.when(dev == d)
                def _():
                    r.TREC[d] = r.TSEND[t]

    def ag_plane(kind, i, u, k):
        block = z_slot(kind, i, k)
        copy(block, block, (S_AX, u, k), x_mate).start()
        copy(block, block, (S_AY, u, k), y_mate).start()

    def ag_column(units, u):
        kind, i = units[u]
        for k in (1, 3, 2):
            wait_in(z_slot(kind, i), (S_Z, u, k))
            ag_plane(kind, i, u, k)

    def by_x(u, k):
        return (k < 2) == (u % 2 == 0)

    def ag_forward(units, u, ks=(1, 3, 2)):
        kind, i = units[u]
        for k in ks:
            if by_x(u, k):
                wait_in(z_slot(kind, i), (S_AY, u, k))
                block = z_slot(kind, i, k, yy=1 - y)
                copy(block, block, (S_FX, u, k), x_mate).start()
            else:
                wait_in(z_slot(kind, i), (S_AX, u, k))
                block = z_slot(kind, i, k, xx=1 - x)
                copy(block, block, (S_FY, u, k), y_mate).start()

    def ag_finish(units, u):
        kind, i = units[u]
        block = z_slot(kind, i)
        for k in (0, 1, 3, 2):
            wait_in(block, (S_AX if by_x(u, k) else S_AY, u, k))
            wait_in(block, (S_FX if by_x(u, k) else S_FY, u, k))

    def ag_sent(units):
        for u, (kind, i) in enumerate(units):
            block = z_slot(kind, i)
            for k in range(4):
                wait_out(block, (S_AX, u, k))
                wait_out(block, (S_AY, u, k))
                wait_out(block, (S_FX if by_x(u, k) else S_FY, u, k))

    def half_unit(buf, kind, i, h, *rest):
        if kind == SQUARE:
            return buf[0], (slice(4 * i + 2 * h, 4 * i + 2 * h + 2),) + rest
        pad = (slice(None),) * (buf[1].ndim - 2 - len(rest))
        return buf[1], (i,) + rest + pad + (slice(512 * h, 512 * h + 512),)

    def part(buf, kind, i, h, *rest):
        ref, index = half_unit(buf, kind, i, h, *rest)
        return ref.at[index]

    def rs_first(units, u, h):
        kind, i = units[u]
        every = slice(None)
        copy(
            part(G, kind, i, h, slice(0, 2), 1 - y), part(R1A, kind, i, h), (S_RA, u, h), y_mate
        ).start()
        copy(
            part(G, kind, i, h, slice(2, 4), every, 1 - x),
            part(R1B, kind, i, h),
            (S_RB, u, h),
            x_mate,
        ).start()

    def add_into(place, other):
        ref, index = place
        ref[index] = (ref[index].astype(f32) + other[...].astype(f32)).astype(bf)

    def rs_second(units, u, h):
        kind, i = units[u]
        every = slice(None)
        ra, rb = part(R1A, kind, i, h), part(R1B, kind, i, h)
        wait_in(ra, (S_RA, u, h))
        add_into(half_unit(G, kind, i, h, slice(0, 2), y), ra)
        copy(
            part(G, kind, i, h, slice(0, 2), y, 1 - x), part(R2A, kind, i, h), (S_SA, u, h), x_mate
        ).start()
        wait_in(rb, (S_RB, u, h))
        add_into(half_unit(G, kind, i, h, slice(2, 4), every, x), rb)
        copy(
            part(G, kind, i, h, slice(2, 4), 1 - y, x), part(R2B, kind, i, h), (S_SB, u, h), y_mate
        ).start()

    def arrived(role_of, u, h, slot):
        kind, i, j = unit_mats(role_of, u)
        if kind == SQUARE:
            return r.R3S.at[slot, j + 2 * h : j + 2 * h + 2]
        return r.R3W.at[slot, j, :, 512 * h : 512 * h + 512]

    def rs_third(my_role, u, h):
        kind, i, j = unit_mats(my_role, u)
        ra, rb = part(R2A, kind, i, h), part(R2B, kind, i, h)
        wait_in(ra, (S_SA, u, h))
        add_into(half_unit(G, kind, i, h, slice(0, 2), y, x), ra)
        wait_in(rb, (S_SB, u, h))
        add_into(half_unit(G, kind, i, h, slice(2, 4), y, x), rb)
        for k in (2, 1, 3):
            slot = 1 if k == 3 else 0
            zz, dev = z_mate(k)
            copy(
                part(G, kind, i, h, zz, y, x),
                arrived(my_role, u, h, slot),
                (S_T, my_role, u, h, slot, k & 1),
                dev,
            ).start()

    def rs_sent(my_role, units):
        for u, (kind, i) in enumerate(units):
            for h in range(2):
                wait_out(part(R1A, kind, i, h), (S_RA, u, h))
                wait_out(part(R1B, kind, i, h), (S_RB, u, h))
                wait_out(part(R2A, kind, i, h), (S_SA, u, h))
                wait_out(part(R2B, kind, i, h), (S_SB, u, h))
                for k in (1, 2, 3):
                    slot = 1 if k == 3 else 0
                    wait_out(arrived(my_role, u, h, 0), (S_T, my_role, u, h, slot, k & 1))

    def final_sum(my_role, role_of, u):
        kind, i, j = unit_mats(role_of, u)
        for h in range(2):
            first = arrived(role_of, u, h, 0)
            second = arrived(role_of, u, h, 1)
            if my_role == role_of:
                wait_in(first, (S_T, role_of, u, h, 0, 0))
                ref, index = half_unit(G, kind, i, h, z, y, x)
                total = ref[index].astype(f32) + first[...].astype(f32)
            else:
                wait_in(first, (S_T, role_of, u, h, 0, 1))
                wait_in(second, (S_T, role_of, u, h, 1, 1))
                total = first[...].astype(f32) + second[...].astype(f32)
            if kind == SQUARE:
                r.F_GS[j + 2 * h : j + 2 * h + 2] = total
            else:
                r.F_GW[j, :, 512 * h : 512 * h + 512] = total

    def unit_stats(g):
        role_of, u = ALL_UNITS[g]
        kind, i, j = unit_mats(role_of, u)
        lanes = lax.broadcasted_iota(jnp.int32, (32, LANES), 1)
        rows = r.RQ[0:32, :]
        if kind == SQUARE:
            for m in range(4):
                grad = r.F_GS[j + m]
                sq = grad * grad
                cols = jnp.sum(sq, axis=0, keepdims=True)
                for h in range(2):
                    r.ST[g, z, 2 * m + h : 2 * m + h + 1, :] = cols[:, h * LANES : (h + 1) * LANES]
                rows = jnp.where(lanes == j + m, jnp.sum(sq, axis=1, keepdims=True), rows)
        else:
            grad = r.F_GW[j]
            sq = grad * grad
            cols = jnp.sum(sq, axis=0, keepdims=True)
            for h in range(8):
                r.ST[g, z, h : h + 1, :] = cols[:, h * LANES : (h + 1) * LANES]
            rows = jnp.where(lanes == 12 + j, jnp.sum(sq, axis=1, keepdims=True), rows)
        r.RQ[0:32, :] = rows
        if g == 0:
            r.SV[d] = r.ST[0, z]
            for k in range(1, 16):
                copy(r.SV.at[d], r.SV.at[d], S_SV, lax.rem(d + k, 16)).start()
            return
        for k in (1, 2, 3):
            copy(r.ST.at[g, z], r.ST.at[g, z], (S_ST, g), z_mate(k)[1]).start()

    def spread_unit(g):
        wait_in(r.ST.at[g, 0:3], (S_ST, g))
        r.SU[g, yx] = in_order(r.ST, (g,))
        for dev in plane_mates():
            copy(r.SU.at[g, yx], r.SU.at[g, yx], (S_SU, g), dev).start()

    def store_unit(g):
        kind, i, j = unit_mats(*ALL_UNITS[g])
        if kind == SQUARE:
            return local(r.F_GS.at[j : j + 4], r.o_gs.at[j : j + 4], 8 + g)
        return local(r.F_GW.at[j], r.o_gw.at[j], 8 + g)

    def finish_unit(my_role, g):
        final_sum(my_role, *ALL_UNITS[g])
        store_unit(g).start()
        unit_stats(g)

    def weight(kind, i, cols=None):
        if kind == SQUARE:
            return r.WS[i].reshape(512, 256)
        if cols is None:
            return r.WW[i].reshape(512, 1024)
        return r.WW[i, :, :, :, :, cols].reshape(512, 256)

    def put_square(i, value):
        r.GS[i] = value.astype(bf).reshape(4, 2, 2, 32, 256)

    def swap(number, partial):
        slot = number % 2
        for half in range(2):
            rows = slice(half * BLOCK, (half + 1) * BLOCK)
            if number >= 2:
                wait_out(r.PS.at[slot, rows], (S_M, number - 2, half))
            r.PS[slot, rows] = partial(rows).astype(bf)
            copy(
                r.PS.at[slot, rows], r.PR.at[slot, rows], (S_M, number, half), d, 1 - c
            ).start()

    def swapped(number, body):
        slot = number % 2
        for half in range(2):
            rows = slice(half * BLOCK, (half + 1) * BLOCK)
            wait_in(r.PR.at[slot, rows], (S_M, number, half))

            def chunk(i):
                at = pl.ds(pl.multiple_of(half * BLOCK + i * CHUNK, CHUNK), CHUNK)
                body(
                    at,
                    half * (BLOCK // CHUNK) + i,
                    r.PS[slot, at].astype(f32) + r.PR[slot, at].astype(f32),
                )

            repeat(BLOCK // CHUNK, chunk)

    def swaps_sent(count):
        for number in (count - 2, count - 1):
            for half in range(2):
                wait_out(r.PS.at[0, 0:BLOCK], (S_M, number, half))

    def norm_forward(residual, kept, which, at):
        centred = residual - jnp.mean(residual, axis=-1, keepdims=True)
        spread = lax.rsqrt(jnp.mean(centred * centred, axis=-1, keepdims=True) + 1e-05)
        normed = centred * spread
        r.XH[kept, at] = normed
        r.RSD[kept, at] = spread
        return normed * r.NORM[which : which + 1, :] + r.NORM[5 + which : 6 + which, :]

    def norm_backward(upstream, kept, which, at):
        normed = r.XH[kept, at]
        scaled = upstream * r.NORM[which : which + 1, :]
        both = upstream * normed
        gain_sum = jnp.sum(both, axis=0, keepdims=True)
        bias_sum = jnp.sum(upstream, axis=0, keepdims=True)
        for b in range(4):
            lanes = slice(b * LANES, (b + 1) * LANES)
            r.NGR[b, which : which + 1, :] += gain_sum[:, lanes]
            r.NGR[b, 5 + which : 6 + which, :] += bias_sum[:, lanes]
        return r.RSD[kept, at] * (
            scaled
            - jnp.mean(scaled, axis=-1, keepdims=True)
            - normed * jnp.mean(scaled * normed, axis=-1, keepdims=True)
        )

    head_lane = lax.broadcasted_iota(jnp.int32, (1, LANES), 1)
    first_head = jnp.where(head_lane < 64, 1.0, 0.0)
    second_head = 1.0 - first_head

    def stacked(value):
        wide_value = value.astype(f32)
        return jnp.concatenate([wide_value * first_head, wide_value * second_head], axis=0).astype(bf)

    def unstacked(value):
        return value[0:BLOCK] * first_head + value[BLOCK:] * second_head

    def pairs(body):
        for blk in range(2):
            for pr in range(2):
                body(blk, slice(blk * BLOCK, (blk + 1) * BLOCK), slice(pr * LANES, (pr + 1) * LANES), 2 * blk + pr)

    def make_masks(slot, count_of, causal):
        row = lax.broadcasted_iota(jnp.int32, (BLOCK, TOKENS), 0)
        col = lax.broadcasted_iota(jnp.int32, (BLOCK, TOKENS), 1) & (BLOCK - 1)
        same = (row >> 3) == (col >> 3)
        r.FILL[...] = jnp.where(same, NEG, OUTSIDE)
        for blk in range(2):
            ok = same & ((col & 7).astype(f32) < count_of(blk))
            if causal:
                ok = ok & ((col & 7) <= (row & 7))
            r.ALLOW[slot, blk] = jnp.where(ok, 1.0, 0.0)

    def attend(kept, mask_slot):
        def one(blk, rows, lanes, n):
            keys = stacked(r.K[kept, rows, lanes])
            scores = mm_nt(r.Q[kept, rows, lanes], keys) * 0.125
            scores = jnp.where(r.ALLOW[mask_slot, blk] > 0.5, scores, r.FILL[...])
            halves = []
            for h in range(2):
                s = scores[:, h * BLOCK : (h + 1) * BLOCK]
                e = jnp.exp(s - jnp.max(s, axis=-1, keepdims=True))
                halves.append(e / jnp.sum(e, axis=-1, keepdims=True))
            probs = jnp.concatenate(halves, axis=1)
            r.PROB[kept, n] = probs
            r.O[kept, rows, lanes] = mm(
                probs.astype(bf), stacked(r.V[kept, rows, lanes])
            ).astype(bf)

        pairs(one)

    def attend_back(kept):
        def one(blk, rows, lanes, n):
            queries = r.Q[kept, rows, lanes]
            keys = stacked(r.K[kept, rows, lanes])
            values = stacked(r.V[kept, rows, lanes])
            out_grad = r.DO[rows, lanes]
            probs = r.PROB[kept, n]
            weighted = probs * mm_nt(out_grad, values)
            halves = []
            for h in range(2):
                w = weighted[:, h * BLOCK : (h + 1) * BLOCK]
                p = probs[:, h * BLOCK : (h + 1) * BLOCK]
                halves.append(w - p * jnp.sum(w, axis=-1, keepdims=True))
            score_grad = jnp.concatenate(halves, axis=1).astype(bf)
            r.DQ[rows, lanes] = (mm(score_grad, keys) * 0.125).astype(bf)
            r.DK[rows, lanes] = (unstacked(mm_tn(score_grad, queries)) * 0.125).astype(bf)
            r.DV[rows, lanes] = unstacked(mm_tn(probs.astype(bf), out_grad)).astype(bf)

        pairs(one)

    def project_all(kept, base, queries, keys):
        r.Q[kept] = mm(queries, weight(SQUARE, base)).astype(bf)
        r.K[kept] = mm(keys, weight(SQUARE, base + 1)).astype(bf)
        r.V[kept] = mm(keys, weight(SQUARE, base + 2)).astype(bf)

    def attention_out(kept, base):
        return lambda rows: mm_nt(r.O[kept, rows], weight(SQUARE, base + 3))

    def attention_back_start(kept, base):
        upstream = r.GLOW[...]
        r.DO[...] = mm(upstream, weight(SQUARE, base + 3)).astype(bf)
        attend_back(kept)

    def query_side(base):
        return lambda rows: mm_nt(r.DQ[rows], weight(SQUARE, base))

    def key_side(base):
        return lambda rows: mm_nt(r.DK[rows], weight(SQUARE, base + 1)) + mm_nt(
            r.DV[rows], weight(SQUARE, base + 2)
        )

    def all_sides(base):
        return lambda rows: query_side(base)(rows) + key_side(base)(rows)

    def expand(inputs):
        def one(n):
            cols = aligned(n, 256)
            hidden = mm(inputs, weight(WIDE, 0, cols))
            r.U[:, cols] = hidden
            bent = jnp.tanh(0.7978845608 * (hidden + 0.044715 * hidden * hidden * hidden))
            r.ACT[:, cols] = (0.5 * hidden * (1.0 + bent)).astype(bf)

        repeat(4, one)

    def contract(rows):
        return mm_nt(r.ACT[rows], weight(WIDE, 1))

    def expand_back_down(h):
        upstream = r.GLOW[...]

        def one(n):
            cols = aligned(2 * h + n, 256)
            r.GW[1, :, :, :, :, cols] = (
                mm_tn(upstream, r.ACT[:, cols]).astype(bf).reshape(4, 2, 2, 32, 256)
            )

        repeat(2, one)

    def expand_back_hidden():
        upstream = r.GLOW[...]

        def one(n):
            cols = aligned(n, 256)
            active_grad = mm(upstream, weight(WIDE, 1, cols)).astype(bf).astype(f32)
            hidden = r.U[:, cols]
            square = hidden * hidden
            bent = jnp.tanh(0.7978845608 * (hidden + 0.044715 * hidden * square))
            slope = 0.5 * (1.0 + bent) + 0.5 * hidden * (1.0 - bent * bent) * 0.7978845608 * (
                1.0 + 3.0 * 0.044715 * square
            )
            r.DU[:, cols] = (active_grad * slope).astype(bf)

        repeat(4, one)

    def expand_back_up(inputs, h):
        def one(n):
            cols = aligned(2 * h + n, 256)
            r.GW[0, :, :, :, :, cols] = (
                mm_tn(inputs, r.DU[:, cols]).astype(bf).reshape(4, 2, 2, 32, 256)
            )

        repeat(2, one)

    def expand_input(rows):
        return mm_nt(r.DU[rows], weight(WIDE, 0))

    def clear_sums():
        r.NGR[...] = jnp.zeros((4, 16, LANES), f32)
        sums = jnp.sum(r.RL[...], axis=1, keepdims=True)
        rows = lax.broadcasted_iota(jnp.int32, (16, LANES), 0)
        lanes = lax.broadcasted_iota(jnp.int32, (16, LANES), 1)
        line = jnp.sum(jnp.where(rows == lanes, sums, 0.0), axis=0, keepdims=True)
        for b in range(4):
            r.NGR[b, 10:11, :] = line
        r.RQ[...] = jnp.zeros((BLOCK, LANES), f32)

    def read_norms():
        wait_in(r.NB.at[0:15], S_NORM)
        for b in range(4):
            total = r.NB[4 * b].astype(f32)
            for i in range(1, 4):
                total = total + r.NB[4 * b + i].astype(f32)
            r.NORM[:, b * LANES : (b + 1) * LANES] = total

    def by_role(body):
        pl.when(role == 0)(lambda: body(0))
        pl.when(role == 1)(lambda: body(1))

    def start_unit(u):
        def body(my_role):
            if u < 3:
                z_send(my_role, 0, u)
            units = (ENC_UNITS, DEC_UNITS)[my_role]
            if u < len(units):
                ag_plane(*units[u], u, 0)

        by_role(body)

    loads[2].wait()
    cast_weights(0, 0)
    cast_weights(1, 0)
    pl.semaphore_wait(barrier, 16)
    start_unit(0)
    loads[3].wait()
    cast_weights(0, 1)
    cast_weights(1, 1)
    start_unit(1)
    cast_weights(0, 2)
    cast_weights(1, 2)
    start_unit(2)
    cast_weights(1, 3)
    start_unit(3)

    r.NORM[...] = jnp.zeros((16, 512), f32)
    for i in (5, 6, 7):
        loads[i].wait()
    r.NORM[0:10, 0:32] = r.I_NORM[...]
    shift = lax.rem(d, 4) * 32
    r.NB[d] = pltpu.roll(r.NORM[:, 0:LANES], shift, 1).astype(bf)
    r.RL[...] = jnp.zeros((16, LANES), f32)
    r.RL[0:12, 0:32] = r.I_SR[...]
    r.RL[12:16, 0:32] = r.I_WR[...]

    send_norms()

    lane = lax.broadcasted_iota(jnp.int32, (8, LANES), 1)
    for s in range(16):
        r.EXT[8 * s : 8 * s + 8, :] = jnp.where(
            lane < 32,
            r.lengths[0, s],
            jnp.where(lane < 64, r.lengths[1, s], r.destinations[s]),
        ).astype(f32)
    ext_low = r.EXT[...].astype(bf)
    r.SEXT[...] = ext_low

    loads[1].wait()

    @pl.when(role == 1)
    def _():
        copy(r.SRC.at[:, my_half], r.XHALF.at[c], S_SOURCE, partner).start()
        copy(r.SEXT, r.XEXT, S_EXT, partner).start()

    def later_units(my_role, us):
        for u in us:
            z_send(my_role, 1, u)

    by_role(lambda my_role: later_units(my_role, (0, 1)))

    perm_f = perm_of(r.EXT[:, 64:65])
    r.PERMT[0] = perm_f.astype(bf)
    perm = perm_f.T.astype(bf)
    loads[0].wait()
    r.TSEND[:, :, 0:512] = mm(perm, r.TGT[...]).astype(bf).reshape(8, 16, 512)
    r.TSEND[:, :, 512:640] = mm(perm, ext_low).astype(bf).reshape(8, 16, LANES)

    loads[4].wait()

    def last_starts(my_role):
        send_target(my_role)
        later_units(my_role, (2, 3))
        if my_role == 0:
            copy(r.COT1, r.COT2, S_COT, partner).start()

    by_role(last_starts)

    def encoder():
        units = ENC_UNITS
        clear_sums()
        for u in range(3):
            ag_forward(units, u, (0,))
        ag_column(units, 0)
        ag_forward(units, 0)
        ag_column(units, 1)
        wait_in(r.XEXT, S_EXT)
        wait_in(r.XHALF.at[0], S_SOURCE)
        hand_over(r.XHALF, S_SOURCE2)
        r.XT[0:BLOCK] = r.SRC[...]
        for half in range(2):
            r.XT[BLOCK:, half * 256 : half * 256 + 256] = r.XHALF[half]
        def counts(blk):
            return r.EXT[:, 0:1] if blk == 0 else r.XEXT[...].astype(f32)[:, 0:1]

        make_masks(0, counts, False)
        r.PERMT[1] = perm_of(r.XEXT[...].astype(f32)[:, 64:65]).astype(bf)
        read_norms()
        ag_column(units, 2)
        ag_finish(units, 0)
        x_in = r.XT[...]
        project_all(0, 0, x_in, x_in)
        attend(0, 0)
        swap(0, attention_out(0, 0))
        ag_forward(units, 1)

        def first(at, n, total):
            hidden = norm_forward(r.XT[at].astype(f32) + total, 0, 0, at)
            r.RES[at] = hidden
            r.LOW[0, at] = hidden.astype(bf)

        swapped(0, first)
        ag_finish(units, 1)
        expand(r.LOW[0])
        ag_forward(units, 2)
        ag_finish(units, 2)
        swap(1, contract)

        def second(at, n, total):
            r.LOW[1, at] = norm_forward(r.RES[at] + total, 1, 1, at).astype(bf)

        swapped(1, second)
        for jj in range(2):
            block = r.LOW[1, jj * BLOCK : (jj + 1) * BLOCK]
            r.MSEND[:, jj] = mm_tn(r.PERMT[jj], block).astype(bf).reshape(8, 16, 512)
        zz = lax.div(z, 2)
        for t in range(8):
            dev = (2 * (t // 4) + 1) * 4 + t % 4
            copy(
                r.MSEND.at[t, :, :, my_half], r.MREC.at[c, zz, :, yx], S_MEMORY, dev
            ).start()

        wait_in(r.MG.at[0], S_DM)
        hand_over(r.MG, S_DM2)
        for jj in range(2):
            for half in range(2):
                r.GRAD[jj * BLOCK : (jj + 1) * BLOCK, half * 256 : half * 256 + 256] = mm(
                    r.PERMT[jj], r.MG[half, :, jj].reshape(BLOCK, 256)
                )

        def back_one(i):
            at = aligned(i, CHUNK)
            value = norm_backward(r.GRAD[at], 1, 1, at)
            r.GRAD[at] = value
            r.GLOW[at] = value.astype(bf)

        repeat(TOKENS // CHUNK, back_one)
        for h in range(2):
            expand_back_down(h)
            rs_first(units, 2, h)
        expand_back_hidden()
        swap(2, expand_input)
        for h in range(2):
            expand_back_up(r.LOW[0], h)
            rs_first(units, 1, h)

        def back_two(at, n, total):
            value = norm_backward(r.GRAD[at] + total, 0, 0, at)
            r.GRAD[at] = value
            r.GLOW[at] = value.astype(bf)

        swapped(2, back_two)
        rs_second(units, 2, 0)
        attention_back_start(0, 0)
        swap(3, all_sides(0))
        rs_second(units, 2, 1)
        put_square(3, mm_tn(r.GLOW[...], r.O[0]))
        put_square(2, mm_tn(r.XT[...], r.DV[...]))
        rs_first(units, 0, 1)
        put_square(0, mm_tn(r.XT[...], r.DQ[...]))
        put_square(1, mm_tn(r.XT[...], r.DK[...]))

        def back_three(at, n, total):
            r.GRAD[at] = r.GRAD[at] + total

        swapped(3, back_three)
        for target_ref, value in ((r.F_SRC, r.GRAD[0:BLOCK]), (r.SGSEND, r.GRAD[BLOCK:])):
            value = value.reshape(16, 8, 512)
            target_ref[...] = jnp.where(c == 0, value[:, 0:4], value[:, 4:8])
        local(r.F_SRC, r.o_src, 6).start()
        copy(r.SGSEND, r.SGREC, S_SG, partner).start()
        send_norm_sums()
        rs_first(units, 0, 0)
        rs_second(units, 1, 0)
        rs_second(units, 1, 1)
        rs_third(0, 2, 0)
        rs_third(0, 2, 1)
        finish_unit(0, 6)
        wait_in(r.DREC, S_DEC)
        r.F_DEC[...] = r.DREC[...]
        local(r.F_DEC, r.o_dec, 5).start()
        take_target(0)
        finish_unit(0, 5)
        rs_second(units, 0, 1)
        rs_second(units, 0, 0)
        rs_third(0, 1, 0)
        rs_third(0, 1, 1)
        finish_unit(0, 4)
        finish_unit(0, 2)
        rs_third(0, 0, 1)
        rs_third(0, 0, 0)
        finish_unit(0, 3)
        wait_out(r.MREC.at[0], S_MEMORY)
        wait_out(r.SGSEND, S_SG)
        swaps_sent(4)
        spread_norm_sums()
        for g in (6, 5, 4):
            spread_unit(g)
        finish_unit(0, 1)
        spread_unit(2)
        spread_unit(3)
        finish_unit(0, 0)
        spread_unit(1)
        ag_sent(units)
        rs_sent(0, units)
        z_sent(0)
        wait_out(r.NB.at[0:15], S_NORM)
        wait_out(r.COT1, S_COT)
        wait_out(r.TSEND, S_TARGET)

    def send_norm_sums():
        r.NG[z] = r.NGR[z]
        for k in (1, 2, 3):
            zz, dev = z_mate(k)
            copy(r.NGR.at[zz], r.NG.at[z], S_NG, dev).start()

    def spread_norm_sums():
        wait_in(r.NG.at[0:3], S_NG)
        r.NH[yx] = in_order(r.NG)
        for dev in plane_mates():
            copy(r.NH.at[yx], r.NH.at[yx], S_NH, dev).start()

    def take_target(my_role):
        if my_role == 0:
            wait_in(r.TG.at[0], S_DT)
        else:
            wait_in(r.TG.at[0, 0:7], S_DT)
        hand_over(r.TG, S_DT2)
        for half in range(2):
            r.F_TGT[:, :, half * 256 : half * 256 + 256] = mm(
                r.PERMT[0], r.TG[half].reshape(BLOCK, 256)
            ).reshape(16, 8, 256)
        local(r.F_TGT, r.o_tgt, 7).start()

    def decoder():
        units = DEC_UNITS
        clear_sums()
        for u in range(4):
            ag_forward(units, u, (0,))
        ag_column(units, 0)
        ag_forward(units, 0)
        ag_column(units, 1)
        ag_forward(units, 1)
        wait_in(r.TREC.at[0:15], S_TARGET)
        cot = r.COT

        def place(i):
            at = aligned(i, 32)
            both = jnp.concatenate(
                [
                    r.COT1[at].astype(f32).reshape(4, 1, 8, 512),
                    r.COT2[at].astype(f32).reshape(4, 1, 8, 512),
                ],
                axis=1,
            )
            cot[aligned(i, CHUNK)] = both.reshape(CHUNK, 512)

        r.XT[...] = r.TREC[:, :, 0:512].reshape(TOKENS, 512)

        def counts(which):
            def get(blk):
                ext = r.TREC[8 * blk : 8 * blk + 8, :, 512:640].reshape(BLOCK, LANES)
                return ext.astype(f32)[:, 32 * which : 32 * which + 1]

            return get

        make_masks(0, counts(1), True)
        make_masks(1, counts(0), False)
        read_norms()
        ag_column(units, 2)
        ag_column(units, 3)
        ag_finish(units, 0)
        x_in = r.XT[...]
        project_all(0, 0, x_in, x_in)
        attend(0, 0)
        swap(0, attention_out(0, 0))
        ag_forward(units, 2)

        def first(at, n, total):
            hidden = norm_forward(r.XT[at].astype(f32) + total, 0, 2, at)
            r.RES[at] = hidden
            r.LOW[0, at] = hidden.astype(bf)

        swapped(0, first)
        ag_forward(units, 3)
        ag_finish(units, 1)
        wait_in(r.COT2, S_COT)
        repeat(4, place)
        r.Q[1] = mm(r.LOW[0], weight(SQUARE, 4)).astype(bf)
        wait_in(r.MREC.at[0], S_MEMORY)
        hand_over(r.MREC, S_MEMORY2)
        for half in range(2):
            r.MEM[:, half * 256 : half * 256 + 256] = r.MREC[half].reshape(TOKENS, 256)
        memory = r.MEM[...]
        r.K[1] = mm(memory, weight(SQUARE, 5)).astype(bf)
        r.V[1] = mm(memory, weight(SQUARE, 6)).astype(bf)
        attend(1, 1)
        swap(1, attention_out(1, 4))

        def second(at, n, total):
            hidden = norm_forward(r.RES[at] + total, 1, 3, at)
            r.RES[at] = hidden
            r.LOW[1, at] = hidden.astype(bf)

        swapped(1, second)
        ag_finish(units, 2)
        expand(r.LOW[1])
        ag_finish(units, 3)
        swap(2, contract)

        def third(at, n, total):
            out = norm_forward(r.RES[at] + total, 2, 4, at)
            rows = aligned(n, 32)
            split = out.reshape(4, 2, 8, 512)
            r.F_DEC[rows] = split[:, 0].reshape(32, 512).astype(bf)
            r.DSEND[rows] = split[:, 1].reshape(32, 512).astype(bf)
            value = norm_backward(cot[at], 2, 4, at)
            r.GRAD[at] = value
            r.GLOW[at] = value.astype(bf)

        swapped(2, third)
        expand_back_hidden()
        swap(3, expand_input)
        for h in range(2):
            expand_back_down(h)
            rs_first(units, 3, h)
        local(r.F_DEC, r.o_dec, 5).start()

        def back_two(at, n, total):
            value = norm_backward(r.GRAD[at] + total, 1, 3, at)
            r.GRAD[at] = value
            r.GLOW[at] = value.astype(bf)

        swapped(3, back_two)
        attention_back_start(1, 4)
        swap(4, key_side(4))
        for h in range(2):
            expand_back_up(r.LOW[1], h)

        def back_memory(at, n, total):
            r.LOW[2, at] = total.astype(bf)

        swapped(4, back_memory)
        r.DMSEND[...] = r.LOW[2].reshape(2, 2, 4, 16, 512)
        my_t = lax.div(z, 2) * 4 + yx
        for t in range(8):
            dev = (2 * (t // 4)) * 4 + t % 4
            copy(
                r.DMSEND.at[t // 4, :, t % 4, :, my_half], r.MG.at[c, my_t], S_DM, dev
            ).start()
        copy(r.DSEND, r.DREC, S_DEC, partner).start()
        for h in range(2):
            rs_second(units, 3, h)
            rs_first(units, 2, h)
        swap(5, query_side(4))
        put_square(7, mm_tn(r.GLOW[...], r.O[1]))
        put_square(6, mm_tn(r.MEM[...], r.DV[...]))
        rs_first(units, 1, 1)
        put_square(5, mm_tn(r.MEM[...], r.DK[...]))
        put_square(4, mm_tn(r.LOW[0], r.DQ[...]))
        rs_first(units, 1, 0)

        def back_three(at, n, total):
            value = norm_backward(r.GRAD[at] + total, 0, 2, at)
            r.GRAD[at] = value
            r.GLOW[at] = value.astype(bf)

        swapped(5, back_three)
        attention_back_start(0, 0)
        swap(6, all_sides(0))
        put_square(3, mm_tn(r.GLOW[...], r.O[0]))
        put_square(2, mm_tn(r.XT[...], r.DV[...]))
        rs_first(units, 0, 1)
        put_square(0, mm_tn(r.XT[...], r.DQ[...]))
        put_square(1, mm_tn(r.XT[...], r.DK[...]))
        rs_third(1, 3, 0)
        rs_third(1, 3, 1)
        rs_second(units, 2, 0)
        rs_second(units, 2, 1)
        rs_first(units, 0, 0)

        def back_four(at, n, total):
            r.DTSEND[aligned(n, 4)] = (
                (r.GRAD[at] + total).astype(bf).reshape(4, 16, 512)
            )

        swapped(6, back_four)
        for k in range(1, 16):
            dev = lax.rem(d + k, 16)
            copy(r.DTSEND.at[dev, :, my_half], r.TG.at[c, my_t], S_DT, dev).start()
        r.TG[c, my_t] = r.DTSEND[d, :, my_half]
        send_norm_sums()
        rs_second(units, 1, 1)
        rs_third(1, 2, 0)
        rs_second(units, 1, 0)
        rs_third(1, 2, 1)
        finish_unit(1, 6)
        rs_second(units, 0, 1)
        rs_third(1, 1, 1)
        rs_second(units, 0, 0)
        rs_third(1, 1, 0)
        finish_unit(1, 5)
        take_target(1)
        rs_third(1, 0, 1)
        rs_third(1, 0, 0)
        finish_unit(1, 4)
        finish_unit(1, 2)
        wait_in(r.SGREC, S_SG)
        r.F_SRC[...] = r.SGREC[...]
        local(r.F_SRC, r.o_src, 6).start()
        wait_out(r.DTSEND.at[0:15, :, 0:256], S_DT)
        wait_out(r.MG.at[0], S_DM)
        wait_out(r.DSEND, S_DEC)
        swaps_sent(7)
        spread_norm_sums()
        for g in (6, 5, 4):
            spread_unit(g)
        finish_unit(1, 3)
        finish_unit(1, 1)
        spread_unit(2)
        spread_unit(3)
        finish_unit(1, 0)
        spread_unit(1)
        ag_sent(units)
        rs_sent(1, units)
        z_sent(1)
        wait_out(r.NB.at[0:15], S_NORM)
        wait_out(r.SEXT, S_EXT)
        wait_out(r.XHALF.at[0], S_SOURCE)
        wait_out(r.TSEND.at[0:7], S_TARGET)

    pl.when(role == 0)(encoder)
    pl.when(role == 1)(decoder)

    copy(r.RQ, r.RQR, S_RQ, d, 1 - c).start()
    wait_in(r.NH.at[0:3], S_NH)
    total = in_order(r.NH)
    r.o_ng[...] = pltpu.roll(total, lax.rem(LANES - shift, LANES), 1)
    r.o_rl[...] = total
    for g in (6, 5, 4, 2, 3, 1, 0):
        if g == 0:
            wait_in(r.SV.at[0:15], S_SV)
            total = r.SV[0]
            for i in range(1, 16):
                total = total + r.SV[i]
        else:
            wait_in(r.SU.at[g, 0:3], (S_SU, g))
            total = in_order(r.SU, (g,))
        r.TT[g] = jnp.broadcast_to(jnp.sum(total, axis=1, keepdims=True), (8, LANES))
        role_of, u = ALL_UNITS[g]
        kind, _, j = unit_mats(role_of, u)
        for h in range(8):
            if kind == SQUARE:
                r.o_cs[j + h // 2 : j + h // 2 + 1, (h % 2) * LANES : (h % 2 + 1) * LANES] = total[h : h + 1]
            else:
                r.o_cw[j : j + 1, h * LANES : (h + 1) * LANES] = total[h : h + 1]
    copy(r.TT, r.TTR, S_TT, d, 1 - c).start()
    wait_in(r.RQR, S_RQ)
    r.o_rq[...] = r.RQ[...] + r.RQR[...]
    wait_in(r.TTR, S_TT)
    r.o_tt[...] = r.TT[...] + r.TTR[...]
    wait_out(r.RQ, S_RQ)
    wait_out(r.TT, S_TT)
    wait_out(r.NG.at[0:3], S_NG)
    wait_out(r.NH.at[0:3], S_NH)
    wait_out(r.SV.at[0:15], S_SV)
    for g in range(1, 7):
        wait_out(r.ST.at[g, 0:3], (S_ST, g))
        wait_out(r.SU.at[g, 0:3], (S_SU, g))
    local(r.F_DEC, r.o_dec, 5).wait()
    local(r.F_SRC, r.o_src, 6).wait()
    local(r.F_TGT, r.o_tgt, 7).wait()
    for g in range(7):
        store_unit(g).wait()


UPDATE_INPUTS = dict(
    square=0,
    wide=0,
    norm=0,
    square_rows=0,
    square_cols=0,
    wide_rows=0,
    wide_cols=0,
    moment=0,
)
UPDATE_OUTPUTS = dict(
    decoded=((16, 4, 512), jnp.bfloat16),
    source_grad=((16, 4, 512), jnp.float32),
    target_grad=((16, 8, 512), jnp.float32),
    square_grad=((12, 32, 256), jnp.float32),
    square_rows_new=((12, 32), jnp.float32),
    square_cols_new=((12, 256), jnp.float32),
    square_new=((12, 32, 256), jnp.float32),
    square_copy=((12, 32, 256), jnp.bfloat16),
    wide_grad=((4, 32, 1024), jnp.float32),
    wide_rows_new=((4, 32), jnp.float32),
    wide_cols_new=((4, 1024), jnp.float32),
    wide_new=((4, 32, 1024), jnp.float32),
    wide_copy=((4, 32, 1024), jnp.bfloat16),
    norm_grad=((10, 32), jnp.float32),
    norm_second_new=((10, 32), jnp.float32),
    norm_new=((10, 32), jnp.float32),
    norm_copy=((10, 32), jnp.bfloat16),
)


def update_kernel(*refs):
    r = named(refs, OUTPUTS, UPDATE_INPUTS, UPDATE_OUTPUTS, dict(rows_pad=0))
    c = lax.axis_index("mp")
    bf, f32 = jnp.bfloat16, jnp.float32

    def own_half(value):
        value = value.astype(f32).reshape(16, 8, 512)
        return jnp.where(c == 0, value[:, 0:4], value[:, 4:8])

    r.decoded[...] = own_half(r.o_dec[...]).astype(bf)
    r.source_grad[...] = r.o_src[...]
    r.target_grad[...] = r.o_tgt[...]
    pad = r.rows_pad
    pad[...] = jnp.zeros((BLOCK, LANES), f32)
    pad[0:12, 0:32] = r.square_rows[...]
    pad[12:16, 0:32] = r.wide_rows[...]
    lanes = lax.broadcasted_iota(jnp.int32, (BLOCK, LANES), 1)
    widths = jnp.where(lanes < 12, 1.0 / 512, 1.0 / FF)
    rows_new = 0.5 * pad[...].T + 0.5 * (r.o_rq[...] * widths)
    rows_back = rows_new.T
    r.square_rows_new[...] = rows_back[0:12, 0:32]
    r.wide_rows_new[...] = rows_back[12:16, 0:32]
    square_cols = 0.5 * r.square_cols[...] + 0.5 * (r.o_cs[...] / 512)
    wide_cols = 0.5 * r.wide_cols[...] + 0.5 * (r.o_cw[...] / 512)
    r.square_cols_new[...] = square_cols
    r.wide_cols_new[...] = wide_cols

    def level(m, total, width):
        return (0.5 * r.o_rl[10:11, m : m + 1] + 0.5 * (total / width)) / 512

    def update(master, grad, row, col, lvl):
        return master - RATE * grad * lax.rsqrt(row * col / lvl)

    for g, (role, u) in enumerate(ALL_UNITS):
        kind, _, j = unit_mats(role, u)
        if kind == SQUARE:
            for m in range(4):
                sums = r.o_tt[g]
                total = sums[2 * m : 2 * m + 1, 0:1] + sums[2 * m + 1 : 2 * m + 2, 0:1]
                grad = r.o_gs[j + m]
                new = update(
                    r.square[j + m],
                    grad,
                    rows_new[0:32, j + m : j + m + 1],
                    square_cols[j + m : j + m + 1],
                    level(j + m, total, 512),
                )
                r.square_grad[j + m] = grad
                r.square_new[j + m] = new
                r.square_copy[j + m] = new.astype(bf)
        else:
            total = jnp.sum(r.o_tt[g], axis=0, keepdims=True)[:, 0:1]
            grad = r.o_gw[j]
            new = update(
                r.wide[j],
                grad,
                rows_new[0:32, 12 + j : 13 + j],
                wide_cols[j : j + 1],
                level(12 + j, total, FF),
            )
            r.wide_grad[j] = grad
            r.wide_new[j] = new
            r.wide_copy[j] = new.astype(bf)
    norm_grad = r.o_ng[0:10, 0:32]
    second = 0.5 * r.moment[...] + 0.5 * norm_grad * norm_grad
    norm_new = r.norm[...] - NORM_RATE * norm_grad * lax.rsqrt(second)
    r.norm_grad[...] = norm_grad
    r.norm_second_new[...] = second
    r.norm_new[...] = norm_new
    r.norm_copy[...] = norm_new.astype(bf)


def small_shards(
    source,
    target,
    lengths,
    destinations,
    cotangent,
    square_master,
    wide_master,
    norm_master,
    square_rows,
    square_cols,
    wide_rows,
    wide_cols,
    gain_offset_moment,
):
    vmem = pl.BlockSpec(memory_space=pltpu.VMEM)
    smem = pl.BlockSpec(memory_space=pltpu.SMEM)
    anywhere = pl.BlockSpec(memory_space=pl.ANY)
    moved = pl.pallas_call(
        exchange_kernel,
        out_shape=[jax.ShapeDtypeStruct(*v) for v in OUTPUTS.values()],
        in_specs=[smem, smem] + [anywhere] * 5 + [anywhere] * 3,
        out_specs=[anywhere] * 5 + [vmem] * (len(OUTPUTS) - 5),
        scratch_shapes=[pltpu.VMEM(*v) for v in SCRATCH.values()]
        + [pltpu.SemaphoreType.DMA((n,)) for n in (SEM_COUNT, SEM_COUNT, NEAR_COUNT)],
        compiler_params=pltpu.CompilerParams(
            collective_id=0, has_side_effects=True, vmem_limit_bytes=56 << 20
        ),
    )(
        lengths.T,
        destinations,
        source.reshape(BLOCK, 512),
        target.reshape(BLOCK, 512),
        cotangent.reshape(BLOCK, 512),
        square_master,
        wide_master,
        norm_master,
        square_rows,
        wide_rows,
    )
    return tuple(
        pl.pallas_call(
            update_kernel,
            out_shape=[jax.ShapeDtypeStruct(*v) for v in UPDATE_OUTPUTS.values()],
            in_specs=[vmem] * (len(OUTPUTS) + len(UPDATE_INPUTS)),
            out_specs=[vmem] * len(UPDATE_OUTPUTS),
            scratch_shapes=[pltpu.VMEM((BLOCK, LANES), jnp.float32)],
            compiler_params=pltpu.CompilerParams(vmem_limit_bytes=60 << 20),
        )(
            *moved,
            square_master,
            wide_master,
            norm_master,
            square_rows,
            square_cols,
            wide_rows,
            wide_cols,
            gain_offset_moment,
        )
    )


def solution(mesh):
    return jax.shard_map(
        small_shards if dict(mesh.shape) == {"dp": 16, "mp": 2} else shards,
        mesh=mesh,
        in_specs=(
            P("dp", None, None),
            P("dp", None, None),
            P("dp", None),
            P("dp"),
            P("dp", None, None),
            P(None, "dp", "mp"),
            P(None, "dp", "mp"),
            P(None, "dp"),
            P(None, "dp"),
            P(None, "mp"),
            P(None, "dp"),
            P(None, "mp"),
            P(None, "dp"),
        ),
        out_specs=(
            P("dp", "mp", None),
            P("dp", "mp", None),
            P("dp", None, None),
            P(None, "dp", "mp"),
            P(None, "dp"),
            P(None, "mp"),
            P(None, "dp", "mp"),
            P(None, "dp", "mp"),
            P(None, "dp", "mp"),
            P(None, "dp"),
            P(None, "mp"),
            P(None, "dp", "mp"),
            P(None, "dp", "mp"),
            P(None, "dp"),
            P(None, "dp"),
            P(None, "dp"),
            P(None, "dp"),
        ),
        check_vma=False,
    )
```

```python
import types

import jax
import jax.numpy as jnp
from jax import lax
from jax.experimental import pallas as pl
from jax.experimental.pallas import tpu as pltpu
from jax.sharding import PartitionSpec as P

FF = 2048
HEADS = 8
MICRO = 2


RATE = 0.03
NORM_RATE = 0.2


def rounded(input_tensor):
    return input_tensor.astype(jnp.bfloat16)


def identity(input_tensor):
    return input_tensor


def project(input_tensor, weight_matrix):
    return jnp.einsum(
        "rft,tv->rfv", input_tensor, weight_matrix, preferred_element_type=jnp.float32
    )


def project_back(input_tensor, weight_matrix):
    return jnp.einsum(
        "cxk,ak->cxa", input_tensor, weight_matrix, preferred_element_type=jnp.float32
    )


def outer_sum(first_factor_array, second_factor_array):
    return jnp.einsum(
        "zmb,zmf->bf", first_factor_array, second_factor_array, preferred_element_type=jnp.float32
    )


def split_heads(input_tensor, head_size):
    return input_tensor.reshape(
        input_tensor.shape[0], input_tensor.shape[1], input_tensor.shape[2] // head_size, head_size
    )


def merge_heads(input_tensor):
    return input_tensor.reshape(
        input_tensor.shape[0], input_tensor.shape[1], input_tensor.shape[2] * input_tensor.shape[3]
    )


def layer_norm(residual, gain_row, bias_row):
    centred = residual - jnp.mean(residual, axis=-1, keepdims=True)
    spread = lax.rsqrt(jnp.mean(centred * centred, axis=-1, keepdims=True) + 1e-05)
    normed = centred * spread
    return (normed * gain_row + bias_row, (normed, spread))


def norm_back(upstream, gain_row, kept_state, pick):
    normed, spread = kept_state
    scaled = upstream * gain_row
    centred_grad = (
        scaled
        - jnp.mean(scaled, axis=-1, keepdims=True)
        - normed * jnp.mean(scaled * normed, axis=-1, keepdims=True)
    )
    return (
        centred_grad * spread,
        jnp.sum(pick(upstream * normed), axis=(0, 1)),
        jnp.sum(pick(upstream), axis=(0, 1)),
    )


def attend_forward(query_in, key_in, matrices, start_index, allowed, head_size):
    queries = split_heads(rounded(project(query_in, matrices[start_index])), head_size)
    key_rows = split_heads(rounded(project(key_in, matrices[start_index + 1])), head_size)
    content_lines = split_heads(rounded(project(key_in, matrices[start_index + 2])), head_size)
    scores = jnp.einsum(
        "sqhe,skhe->shqk", queries, key_rows, preferred_element_type=jnp.float32
    ) * head_size ** (-0.5)
    scores = jnp.where(allowed[:, None], scores, -1000000000.0)
    attn_probs = jax.nn.softmax(scores, axis=-1)
    probs_low = rounded(attn_probs)
    mixed_heads = rounded(
        merge_heads(
            jnp.einsum(
                "shqk,skhe->sqhe", probs_low, content_lines, preferred_element_type=jnp.float32
            )
        )
    )
    partial_value = project_back(mixed_heads, matrices[start_index + 3])
    return (partial_value, (queries, key_rows, content_lines, attn_probs, probs_low, mixed_heads))


def attend_back(upstream, query_in, key_in, matrices, start_index, kept_state, head_size):
    queries, key_rows, content_lines, attn_probs, probs_low, mixed_heads = kept_state
    scale = head_size ** (-0.5)
    out_grad = outer_sum(upstream, mixed_heads)
    mixed_grad = split_heads(rounded(project(upstream, matrices[start_index + 3])), head_size)
    prob_grad = jnp.einsum(
        "sqhe,skhe->shqk", mixed_grad, content_lines, preferred_element_type=jnp.float32
    )
    value_grad = rounded(
        jnp.einsum("shqk,sqhe->skhe", probs_low, mixed_grad, preferred_element_type=jnp.float32)
    )
    score_grad = rounded(
        attn_probs * (prob_grad - jnp.sum(attn_probs * prob_grad, axis=-1, keepdims=True))
    )
    query_grad = rounded(
        jnp.einsum("shqk,skhe->sqhe", score_grad, key_rows, preferred_element_type=jnp.float32)
        * scale
    )
    key_grad = rounded(
        jnp.einsum("shqk,sqhe->skhe", score_grad, queries, preferred_element_type=jnp.float32)
        * scale
    )
    query_grad = merge_heads(query_grad)
    key_grad = merge_heads(key_grad)
    value_grad = merge_heads(value_grad)
    weight_grads = (
        outer_sum(query_in, query_grad),
        outer_sum(key_in, key_grad),
        outer_sum(key_in, value_grad),
        out_grad,
    )
    asking_piece = project_back(query_grad, matrices[start_index])
    key_part = project_back(key_grad, matrices[start_index + 1]) + project_back(
        value_grad, matrices[start_index + 2]
    )
    return (asking_piece, key_part, weight_grads)


def expand_forward(inputs, matrices, start_index):
    hidden = project(inputs, matrices[start_index])
    active = rounded(jax.nn.gelu(hidden))
    return (project_back(active, matrices[start_index + 1]), (hidden, active))


def expand_back(upstream, inputs, matrices, start_index, kept_state):
    hidden, active = kept_state
    down_grad = outer_sum(upstream, active)
    active_grad = rounded(project(upstream, matrices[start_index + 1]))
    unused, pullback = jax.vjp(jax.nn.gelu, hidden)
    hidden_grad = rounded(pullback(active_grad.astype(jnp.float32))[0])
    up_grad = outer_sum(inputs, hidden_grad)
    return (project_back(hidden_grad, matrices[start_index]), up_grad, down_grad)


def accumulate(totals, position, addend):
    totals[position] = addend if totals[position] is None else totals[position] + addend


def shards(
    source,
    target,
    lengths,
    destinations,
    cotangent,
    square_master,
    wide_master,
    norm_master,
    square_rows,
    square_cols,
    wide_rows,
    wide_cols,
    gain_offset_moment,
):
    peer_count = lax.axis_size("dp")
    sent_dev = source.shape[0]
    slot_count = source.shape[1]
    model_width = source.shape[2]
    per_peer = sent_dev // peer_count
    head_size = model_width // HEADS
    per_block = sent_dev // MICRO
    half_len = slot_count // lax.axis_size("mp")
    half_start = lax.axis_index("mp") * half_len
    send_order = jnp.argsort(destinations, stable=True)
    home_place = jnp.argsort(send_order, stable=True)

    def own_half(input_tensor):
        return lax.dynamic_slice_in_dim(input_tensor, half_start, half_len, 1)

    def share_total(partial_value):
        return lax.psum_scatter(partial_value, "mp", scatter_dimension=1, tiled=True)

    def add_branch(residual, partial_value):
        return residual + share_total(partial_value)

    def low_rows(value):
        return lax.all_gather(rounded(value), "mp", axis=1, tiled=True)

    def by_peer(input_tensor):
        return jnp.take(input_tensor, send_order, axis=0).reshape(
            (peer_count, per_peer) + input_tensor.shape[1:]
        )

    def flatten(input_tensor):
        return input_tensor.reshape((sent_dev,) + input_tensor.shape[2:])

    moved_lengths = flatten(
        lax.all_to_all(by_peer(lengths), "dp", split_axis=0, concat_axis=0, tiled=True)
    )
    square_low, wide_low, norm_low = (
        lax.all_gather(rounded(square_master), "dp", axis=1, tiled=True),
        lax.all_gather(rounded(wide_master), "dp", axis=1, tiled=True),
        lax.all_gather(rounded(norm_master), "dp", axis=1, tiled=True),
    )
    gain_rows = norm_low[:5].astype(jnp.float32)
    bias_rows = norm_low[5:].astype(jnp.float32)
    positions = jnp.arange(slot_count)
    causal = positions[None, :] <= positions[:, None]

    def key_mask(counts):
        return jnp.broadcast_to(
            positions[None, None, :] < counts[:, None, None],
            (counts.shape[0], slot_count, slot_count),
        )

    square_grads = [None] * 12
    wide_grads = [None] * 4
    gain_grads = [None] * 5
    bias_grads = [None] * 5

    def norm_step(upstream, position, kept_state):
        residual_grad, gain_grad, bias_grad = norm_back(
            upstream, gain_rows[position], kept_state, identity
        )
        accumulate(gain_grads, position, gain_grad)
        accumulate(bias_grads, position, bias_grad)
        return residual_grad

    def attend_step(upstream_low, query_in, key_in, start_index, kept_state):
        asking_piece, key_part, weight_grads = attend_back(
            upstream_low, query_in, key_in, square_low, start_index, kept_state, head_size
        )
        for offset in range(4):
            accumulate(square_grads, start_index + offset, weight_grads[offset])
        return (asking_piece, key_part)

    def expand_step(upstream_low, inputs, start_index, kept_state):
        partial_value, up_grad, down_grad = expand_back(
            upstream_low, inputs, wide_low, start_index, kept_state
        )
        accumulate(wide_grads, start_index, up_grad)
        accumulate(wide_grads, start_index + 1, down_grad)
        return partial_value

    encoder_kept = []
    encoded_pieces = []
    for micro_index in range(MICRO):
        row_start = micro_index * per_block
        source_block = source[row_start : row_start + per_block]
        allowed = key_mask(lengths[row_start : row_start + per_block, 0])
        partial_value, attend_kept = attend_forward(
            source_block, source_block, square_low, 0, allowed, head_size
        )
        hidden, hidden_kept = layer_norm(
            add_branch(own_half(source_block).astype(jnp.float32), partial_value),
            gain_rows[0],
            bias_rows[0],
        )
        hidden_low = low_rows(hidden)
        partial_value, expand_kept = expand_forward(hidden_low, wide_low, 0)
        memory, memory_kept = layer_norm(
            add_branch(hidden, partial_value), gain_rows[1], bias_rows[1]
        )
        encoded_pieces.append(low_rows(memory))
        encoder_kept.append((attend_kept, hidden_kept, hidden_low, expand_kept, memory_kept))
    memory_all = jnp.concatenate(encoded_pieces, axis=0)
    moved_memory, moved_target = (
        lax.all_to_all(by_peer(memory_all), "dp", split_axis=0, concat_axis=0, tiled=True),
        lax.all_to_all(by_peer(target), "dp", split_axis=0, concat_axis=0, tiled=True),
    )
    moved_memory = flatten(moved_memory)
    moved_target = flatten(moved_target)
    decoded_parts = []
    memory_back = []
    target_back = []
    for micro_index in range(MICRO):
        row_start = micro_index * per_block
        target_block = moved_target[row_start : row_start + per_block]
        memory_block = moved_memory[row_start : row_start + per_block]
        counts = moved_lengths[row_start : row_start + per_block]
        self_mask = key_mask(counts[:, 1]) & causal[None]
        cross_attention_mask = key_mask(counts[:, 0])
        partial_value, self_kept = attend_forward(
            target_block, target_block, square_low, 4, self_mask, head_size
        )
        first_norm, first_kept = layer_norm(
            add_branch(own_half(target_block).astype(jnp.float32), partial_value),
            gain_rows[2],
            bias_rows[2],
        )
        first_low = low_rows(first_norm)
        partial_value, cross_kept = attend_forward(
            first_low, memory_block, square_low, 8, cross_attention_mask, head_size
        )
        second_norm, second_kept = layer_norm(
            add_branch(first_norm, partial_value), gain_rows[3], bias_rows[3]
        )
        second_low = low_rows(second_norm)
        partial_value, expand_kept = expand_forward(second_low, wide_low, 2)
        output, output_kept = layer_norm(
            add_branch(second_norm, partial_value), gain_rows[4], bias_rows[4]
        )
        decoded_parts.append(identity(rounded(output)))
        upstream = norm_step(
            own_half(cotangent[row_start : row_start + per_block]).astype(jnp.float32),
            4,
            output_kept,
        )
        upstream = add_branch(upstream, expand_step(low_rows(upstream), second_low, 2, expand_kept))
        upstream = norm_step(upstream, 3, second_kept)
        asking_piece, key_part = attend_step(
            low_rows(upstream), first_low, memory_block, 8, cross_kept
        )
        asking_piece, key_part = share_total((asking_piece, key_part))
        memory_back.append(low_rows(key_part))
        upstream = norm_step(upstream + asking_piece, 2, first_kept)
        asking_piece, key_part = attend_step(
            low_rows(upstream), target_block, target_block, 4, self_kept
        )
        target_back.append(low_rows(add_branch(upstream, asking_piece + key_part)))
    returned_memory, returned_target = (
        lax.all_to_all(
            jnp.concatenate(memory_back, axis=0).reshape(
                peer_count, per_peer, slot_count, model_width
            ),
            "dp",
            split_axis=0,
            concat_axis=0,
            tiled=True,
        ),
        lax.all_to_all(
            jnp.concatenate(target_back, axis=0).reshape(
                peer_count, per_peer, slot_count, model_width
            ),
            "dp",
            split_axis=0,
            concat_axis=0,
            tiled=True,
        ),
    )
    memory_gradient = jnp.take(flatten(returned_memory), home_place, axis=0)
    target_grad = jnp.take(flatten(returned_target), home_place, axis=0).astype(jnp.float32)
    source_parts = []
    for micro_index in range(MICRO):
        row_start = micro_index * per_block
        source_block = source[row_start : row_start + per_block]
        attend_kept, hidden_kept, hidden_low, expand_kept, memory_kept = encoder_kept[micro_index]
        upstream = norm_step(
            own_half(memory_gradient[row_start : row_start + per_block]).astype(jnp.float32),
            1,
            memory_kept,
        )
        upstream = add_branch(upstream, expand_step(low_rows(upstream), hidden_low, 0, expand_kept))
        upstream = norm_step(upstream, 0, hidden_kept)
        asking_piece, key_part = attend_step(
            low_rows(upstream), source_block, source_block, 0, attend_kept
        )
        source_parts.append(identity(add_branch(upstream, asking_piece + key_part)))
    square_grad = jnp.stack(square_grads)
    wide_grad = jnp.stack(wide_grads)
    norm_grad = jnp.stack(gain_grads + bias_grads)
    square_grad, wide_grad, norm_grad = (
        lax.psum_scatter(square_grad, "dp", scatter_dimension=1, tiled=True),
        lax.psum_scatter(wide_grad, "dp", scatter_dimension=1, tiled=True),
        lax.psum_scatter(norm_grad, "dp", scatter_dimension=1, tiled=True),
    )
    row_square, row_wide, norm_grad = lax.psum(
        (
            jnp.sum(square_grad * square_grad, axis=2),
            jnp.sum(wide_grad * wide_grad, axis=2),
            norm_grad,
        ),
        "mp",
    )
    square_rows_new = 0.5 * square_rows + 0.5 * (row_square / model_width)
    wide_rows_new = 0.5 * wide_rows + 0.5 * (row_wide / FF)
    col_square, col_wide, level_square, level_wide = lax.psum(
        (
            jnp.sum(square_grad * square_grad, axis=1),
            jnp.sum(wide_grad * wide_grad, axis=1),
            jnp.sum(square_rows_new, axis=1),
            jnp.sum(wide_rows_new, axis=1),
        ),
        "dp",
    )
    square_cols_new = 0.5 * square_cols + 0.5 * (col_square / model_width)
    wide_cols_new = 0.5 * wide_cols + 0.5 * (col_wide / model_width)
    square_second = (
        square_rows_new[:, :, None]
        * square_cols_new[:, None, :]
        / (level_square / model_width)[:, None, None]
    )
    wide_second = (
        wide_rows_new[:, :, None]
        * wide_cols_new[:, None, :]
        / (level_wide / model_width)[:, None, None]
    )
    updated_square_masters = square_master - RATE * square_grad * lax.rsqrt(square_second)
    wide_new = wide_master - RATE * wide_grad * lax.rsqrt(wide_second)
    norm_second_new = 0.5 * gain_offset_moment + 0.5 * norm_grad * norm_grad
    norm_new = norm_master - NORM_RATE * norm_grad * lax.rsqrt(norm_second_new)
    return (
        jnp.concatenate(decoded_parts, axis=0),
        jnp.concatenate(source_parts, axis=0),
        target_grad,
        square_grad,
        square_rows_new,
        square_cols_new,
        updated_square_masters,
        rounded(updated_square_masters),
        wide_grad,
        wide_rows_new,
        wide_cols_new,
        wide_new,
        rounded(wide_new),
        norm_grad,
        norm_second_new,
        norm_new,
        rounded(norm_new),
    )


SQUARE, WIDE = 0, 1
LANES = 128
TOKENS = 256
BLOCK = 128
CHUNK = 64
MESH_IDS = pl.DeviceIdType.MESH
NEG = -1000000000.0
OUTSIDE = -3.0e38
ENC_UNITS = ((SQUARE, 0), (WIDE, 0), (WIDE, 1))
DEC_UNITS = ((SQUARE, 0), (SQUARE, 1), (WIDE, 0), (WIDE, 1))
ALL_UNITS = ((0, 0), (0, 1), (0, 2), (1, 0), (1, 1), (1, 2), (1, 3))


def mm(a, b):
    return jnp.dot(a, b, preferred_element_type=jnp.float32)


def mm_nt(a, b):
    return lax.dot_general(a, b, (((1,), (1,)), ((), ())), preferred_element_type=jnp.float32)


def mm_tn(a, b):
    return lax.dot_general(a, b, (((0,), (0,)), ((), ())), preferred_element_type=jnp.float32)


def repeat(count, body):
    lax.fori_loop(0, count, lambda i, carry: (body(i), carry)[1], 0, unroll=True)


def aligned(i, size):
    return pl.ds(pl.multiple_of(i * size, size), size)


def unit_mats(role, u):
    kind, i = (ENC_UNITS, DEC_UNITS)[role][u]
    if kind == SQUARE:
        return kind, i, 4 * i + 4 * role
    return kind, i, i + 2 * role


def named(refs, *groups):
    return types.SimpleNamespace(**dict(zip([name for group in groups for name in group], refs)))


class Sems:
    def __init__(self, send, recv, count):
        self.send, self.recv, self.count, self.names = send, recv, count, {}

    def at(self, name):
        i = self.names.setdefault(name, len(self.names))
        assert i < self.count
        return self.send.at[i], self.recv.at[i]


SEM_COUNT = 240
NEAR_COUNT = 18
(
    S_AX,
    S_AY,
    S_COT,
    S_DEC,
    S_DM,
    S_DT,
    S_FX,
    S_FY,
    S_M,
    S_MEMORY,
    S_NG,
    S_NORM,
    S_RA,
    S_RB,
    S_RQ,
    S_SA,
    S_SB,
    S_SG,
    S_SOURCE,
    S_ST,
    S_SU,
    S_SV,
    S_NH,
    S_EXT,
    S_SOURCE2,
    S_MEMORY2,
    S_DM2,
    S_DT2,
    S_T,
    S_TARGET,
    S_TT,
    S_Z,
) = range(32)

SCRATCH = dict(
    WS=((8, 4, 2, 2, 32, 256), jnp.bfloat16),
    WW=((2, 4, 2, 2, 32, 1024), jnp.bfloat16),
    GS=((8, 4, 2, 2, 32, 256), jnp.bfloat16),
    GW=((2, 4, 2, 2, 32, 1024), jnp.bfloat16),
    SB=((12, 32, 256), jnp.bfloat16),
    WB=((4, 32, 1024), jnp.bfloat16),
    R1AS=((8, 2, 2, 32, 256), jnp.bfloat16),
    R1BS=((8, 2, 2, 32, 256), jnp.bfloat16),
    R1AW=((2, 2, 2, 32, 1024), jnp.bfloat16),
    R1BW=((2, 2, 2, 32, 1024), jnp.bfloat16),
    R2AS=((8, 2, 32, 256), jnp.bfloat16),
    R2BS=((8, 2, 32, 256), jnp.bfloat16),
    R2AW=((2, 2, 32, 1024), jnp.bfloat16),
    R2BW=((2, 2, 32, 1024), jnp.bfloat16),
    R3S=((2, 12, 32, 256), jnp.bfloat16),
    R3W=((2, 4, 32, 1024), jnp.bfloat16),
    NB=((16, 16, LANES), jnp.bfloat16),
    RL=((16, LANES), jnp.float32),
    NORM=((16, 512), jnp.float32),
    EXT=((BLOCK, LANES), jnp.float32),
    SEXT=((BLOCK, LANES), jnp.bfloat16),
    XHALF=((2, BLOCK, 256), jnp.bfloat16),
    XEXT=((BLOCK, LANES), jnp.bfloat16),
    TSEND=((8, 16, 640), jnp.bfloat16),
    TREC=((16, 16, 640), jnp.bfloat16),
    COT2=((BLOCK, 512), jnp.bfloat16),
    COT=((TOKENS, 512), jnp.float32),
    XT=((TOKENS, 512), jnp.bfloat16),
    MSEND=((8, 2, 16, 512), jnp.bfloat16),
    MREC=((2, 2, 2, 4, 16, 256), jnp.bfloat16),
    MEM=((TOKENS, 512), jnp.bfloat16),
    DMSEND=((2, 2, 4, 16, 512), jnp.bfloat16),
    MG=((2, 8, 2, 16, 256), jnp.bfloat16),
    DTSEND=((16, 16, 512), jnp.bfloat16),
    TG=((2, 8, 16, 256), jnp.bfloat16),
    DSEND=((BLOCK, 512), jnp.bfloat16),
    DREC=((BLOCK, 512), jnp.bfloat16),
    SGSEND=((16, 4, 512), jnp.float32),
    SGREC=((16, 4, 512), jnp.float32),
    PERMT=((2, BLOCK, BLOCK), jnp.bfloat16),
    ALLOW=((2, 2, BLOCK, TOKENS), jnp.float32),
    FILL=((BLOCK, TOKENS), jnp.float32),
    Q=((2, TOKENS, 256), jnp.bfloat16),
    K=((2, TOKENS, 256), jnp.bfloat16),
    V=((2, TOKENS, 256), jnp.bfloat16),
    O=((2, TOKENS, 256), jnp.bfloat16),
    PROB=((2, 4, BLOCK, TOKENS), jnp.float32),
    DO=((TOKENS, 256), jnp.bfloat16),
    DQ=((TOKENS, 256), jnp.bfloat16),
    DK=((TOKENS, 256), jnp.bfloat16),
    DV=((TOKENS, 256), jnp.bfloat16),
    U=((TOKENS, 1024), jnp.float32),
    ACT=((TOKENS, 1024), jnp.bfloat16),
    DU=((TOKENS, 1024), jnp.bfloat16),
    RES=((TOKENS, 512), jnp.float32),
    LOW=((3, TOKENS, 512), jnp.bfloat16),
    XH=((3, TOKENS, 512), jnp.float32),
    RSD=((3, TOKENS, 1), jnp.float32),
    GRAD=((TOKENS, 512), jnp.float32),
    GLOW=((TOKENS, 512), jnp.bfloat16),
    PS=((2, TOKENS, 512), jnp.bfloat16),
    PR=((2, TOKENS, 512), jnp.bfloat16),
    NGR=((4, 16, LANES), jnp.float32),
    NG=((4, 16, LANES), jnp.float32),
    NH=((4, 16, LANES), jnp.float32),
    ST=((7, 4, 8, LANES), jnp.float32),
    SU=((7, 4, 8, LANES), jnp.float32),
    SV=((16, 8, LANES), jnp.float32),
    RQ=((BLOCK, LANES), jnp.float32),
    RQR=((BLOCK, LANES), jnp.float32),
    TT=((7, 8, LANES), jnp.float32),
    SM=((12, 32, 256), jnp.float32),
    WM=((4, 32, 1024), jnp.float32),
    SRC=((BLOCK, 512), jnp.bfloat16),
    TGT=((BLOCK, 512), jnp.bfloat16),
    I_NORM=((10, 32), jnp.float32),
    I_SR=((12, 32), jnp.float32),
    I_WR=((4, 32), jnp.float32),
    COT1=((BLOCK, 512), jnp.bfloat16),
    F_DEC=((BLOCK, 512), jnp.bfloat16),
    F_SRC=((16, 4, 512), jnp.float32),
    F_TGT=((16, 8, 512), jnp.float32),
    F_GS=((12, 32, 256), jnp.float32),
    F_GW=((4, 32, 1024), jnp.float32),
    TTR=((7, 8, LANES), jnp.float32),
)

INPUTS = dict(
    lengths=0,
    destinations=0,
    source=0,
    target=0,
    cotangent=0,
    square=0,
    wide=0,
    norm=0,
    square_rows=0,
    wide_rows=0,
)
OUTPUTS = dict(
    o_dec=((BLOCK, 512), jnp.bfloat16),
    o_src=((16, 4, 512), jnp.float32),
    o_tgt=((16, 8, 512), jnp.float32),
    o_gs=((12, 32, 256), jnp.float32),
    o_gw=((4, 32, 1024), jnp.float32),
    o_cs=((12, 256), jnp.float32),
    o_cw=((4, 1024), jnp.float32),
    o_rq=((BLOCK, LANES), jnp.float32),
    o_rl=((16, LANES), jnp.float32),
    o_tt=((7, 8, LANES), jnp.float32),
    o_ng=((16, LANES), jnp.float32),
)


def exchange_kernel(*refs):
    r = named(refs, INPUTS, OUTPUTS, SCRATCH)
    sems = Sems(refs[-3], refs[-2], SEM_COUNT)
    near = refs[-1]
    d = lax.axis_index("dp")
    c = lax.axis_index("mp")
    z = lax.div(d, 4)
    yx = lax.rem(d, 4)
    y = lax.div(yx, 2)
    x = lax.rem(yx, 2)
    role = lax.rem(z, 2)
    x_mate = d + 1 - 2 * x
    y_mate = d + 2 - 4 * y
    partner = d + 4 - 8 * role
    bf, f32 = jnp.bfloat16, jnp.float32

    G = (r.GS, r.GW)
    R1A, R1B = (r.R1AS, r.R1AW), (r.R1BS, r.R1BW)
    R2A, R2B = (r.R2AS, r.R2AW), (r.R2BS, r.R2BW)

    def z_mate(k):
        zz = lax.rem(z + k, 4)
        return zz, zz * 4 + yx

    def copy(src, dst, name, dev, core=None):
        send, recv = sems.at(name)
        return pltpu.make_async_remote_copy(
            src_ref=src,
            dst_ref=dst,
            send_sem=send,
            recv_sem=recv,
            device_id=(dev, c if core is None else core),
            device_id_type=MESH_IDS,
        )

    def local(src, dst, i):
        return pltpu.make_async_copy(src, dst, near.at[i])

    my_half = pl.ds(pl.multiple_of(c * 256, 256), 256)

    def hand_over(ref, name):
        copy(ref.at[c], ref.at[c], name, d, 1 - c).start()
        wait_in(ref.at[0], name)
        wait_out(ref.at[0], name)

    def plane_mates():
        return (x_mate, y_mate, z * 4 + 3 - yx)

    def in_order(ref, lead=()):
        total = ref[lead + (0,)]
        for i in range(1, 4):
            total = total + ref[lead + (i,)]
        return total

    def wait_in(dst, name):
        copy(dst, dst, name, x_mate).wait_recv()

    def wait_out(src, name):
        copy(src, src, name, x_mate).wait_send()

    loads = [
        local(r.target, r.TGT, 0),
        local(r.source, r.SRC, 1),
        local(r.square, r.SM, 2),
        local(r.wide, r.WM, 3),
        local(r.cotangent, r.COT1, 4),
        local(r.norm, r.I_NORM, 15),
        local(r.square_rows, r.I_SR, 16),
        local(r.wide_rows, r.I_WR, 17),
    ]
    for i in (2, 3, 5, 6, 7, 1, 0, 4):
        loads[i].start()
    barrier = pltpu.get_barrier_semaphore()
    for k in range(1, 16):
        pl.semaphore_signal(
            barrier, inc=1, device_id=(lax.rem(d + k, 16), c), device_id_type=MESH_IDS
        )
    pl.semaphore_signal(barrier, inc=1, device_id=(d, 1 - c), device_id_type=MESH_IDS)

    row_id = lax.broadcasted_iota(jnp.int32, (BLOCK, BLOCK), 0)
    col_id = lax.broadcasted_iota(jnp.int32, (BLOCK, BLOCK), 1)
    col_z = 2 * (col_id >> 6) + 1 - ((col_id >> 3) & 1)
    col_dev = (col_z * 4 + ((col_id >> 4) & 3)).astype(f32)
    same_slot = (row_id & 7) == (col_id & 7)

    def perm_of(dest_column):
        return jnp.where((dest_column == col_dev) & same_slot, 1.0, 0.0)

    def cast_weights(role_of, u):
        kind, i, j = unit_mats(role_of, u)
        if kind == SQUARE:
            for m in range(4):
                r.SB[j + m] = r.SM[j + m].astype(bf)

            @pl.when(role == role_of)
            def _():
                for m in range(4):
                    r.WS[4 * i + m, z, y, x] = r.SB[j + m]

        else:
            r.WB[j] = r.WM[j].astype(bf)

            @pl.when(role == role_of)
            def _():
                r.WW[i, z, y, x] = r.WB[j]

    def z_slot(kind, i, k=0, yy=None, xx=None):
        zz = lax.rem(z + 4 - k, 4)
        at = (zz, y if yy is None else yy, x if xx is None else xx)
        if kind == SQUARE:
            return r.WS.at[(slice(4 * i, 4 * i + 4),) + at]
        return r.WW.at[(i,) + at]

    def z_send(my_role, target_role, u):
        kind, i, j = unit_mats(target_role, u)
        src = r.SB.at[j : j + 4] if kind == SQUARE else r.WB.at[j]
        for k in (2,) if my_role == target_role else (1, 3):
            copy(src, z_slot(kind, i), (S_Z, u, k), z_mate(k)[1]).start()

    def z_sent(my_role):
        for target_role, u in ALL_UNITS:
            kind, i, j = unit_mats(target_role, u)
            src = r.SB.at[j : j + 4] if kind == SQUARE else r.WB.at[j]
            for k in (2,) if my_role == target_role else (1, 3):
                wait_out(src, (S_Z, u, k))

    def send_norms():
        for k in range(1, 16):
            dev = lax.rem(d + k, 16)
            copy(r.NB.at[d], r.NB.at[d], S_NORM, dev).start()

    def send_target(my_role):
        for t in range(8):
            dev = (2 * (t // 4) + 1) * 4 + t % 4
            send = copy(r.TSEND.at[t], r.TREC.at[d], S_TARGET, dev)
            if my_role == 0:
                send.start()
            else:
                pl.when(dev != d)(send.start)

                @pl.when(dev == d)
                def _():
                    r.TREC[d] = r.TSEND[t]

    def ag_plane(kind, i, u, k):
        block = z_slot(kind, i, k)
        copy(block, block, (S_AX, u, k), x_mate).start()
        copy(block, block, (S_AY, u, k), y_mate).start()

    def ag_column(units, u):
        kind, i = units[u]
        for k in (1, 3, 2):
            wait_in(z_slot(kind, i), (S_Z, u, k))
            ag_plane(kind, i, u, k)

    def by_x(u, k):
        return (k < 2) == (u % 2 == 0)

    def ag_forward(units, u, ks=(1, 3, 2)):
        kind, i = units[u]
        for k in ks:
            if by_x(u, k):
                wait_in(z_slot(kind, i), (S_AY, u, k))
                block = z_slot(kind, i, k, yy=1 - y)
                copy(block, block, (S_FX, u, k), x_mate).start()
            else:
                wait_in(z_slot(kind, i), (S_AX, u, k))
                block = z_slot(kind, i, k, xx=1 - x)
                copy(block, block, (S_FY, u, k), y_mate).start()

    def ag_finish(units, u):
        kind, i = units[u]
        block = z_slot(kind, i)
        for k in (0, 1, 3, 2):
            wait_in(block, (S_AX if by_x(u, k) else S_AY, u, k))
            wait_in(block, (S_FX if by_x(u, k) else S_FY, u, k))

    def ag_sent(units):
        for u, (kind, i) in enumerate(units):
            block = z_slot(kind, i)
            for k in range(4):
                wait_out(block, (S_AX, u, k))
                wait_out(block, (S_AY, u, k))
                wait_out(block, (S_FX if by_x(u, k) else S_FY, u, k))

    def half_unit(buf, kind, i, h, *rest):
        if kind == SQUARE:
            return buf[0], (slice(4 * i + 2 * h, 4 * i + 2 * h + 2),) + rest
        pad = (slice(None),) * (buf[1].ndim - 2 - len(rest))
        return buf[1], (i,) + rest + pad + (slice(512 * h, 512 * h + 512),)

    def part(buf, kind, i, h, *rest):
        ref, index = half_unit(buf, kind, i, h, *rest)
        return ref.at[index]

    def rs_first(units, u, h):
        kind, i = units[u]
        every = slice(None)
        copy(
            part(G, kind, i, h, slice(0, 2), 1 - y), part(R1A, kind, i, h), (S_RA, u, h), y_mate
        ).start()
        copy(
            part(G, kind, i, h, slice(2, 4), every, 1 - x),
            part(R1B, kind, i, h),
            (S_RB, u, h),
            x_mate,
        ).start()

    def add_into(place, other):
        ref, index = place
        ref[index] = (ref[index].astype(f32) + other[...].astype(f32)).astype(bf)

    def rs_second(units, u, h):
        kind, i = units[u]
        every = slice(None)
        ra, rb = part(R1A, kind, i, h), part(R1B, kind, i, h)
        wait_in(ra, (S_RA, u, h))
        add_into(half_unit(G, kind, i, h, slice(0, 2), y), ra)
        copy(
            part(G, kind, i, h, slice(0, 2), y, 1 - x), part(R2A, kind, i, h), (S_SA, u, h), x_mate
        ).start()
        wait_in(rb, (S_RB, u, h))
        add_into(half_unit(G, kind, i, h, slice(2, 4), every, x), rb)
        copy(
            part(G, kind, i, h, slice(2, 4), 1 - y, x), part(R2B, kind, i, h), (S_SB, u, h), y_mate
        ).start()

    def arrived(role_of, u, h, slot):
        kind, i, j = unit_mats(role_of, u)
        if kind == SQUARE:
            return r.R3S.at[slot, j + 2 * h : j + 2 * h + 2]
        return r.R3W.at[slot, j, :, 512 * h : 512 * h + 512]

    def rs_third(my_role, u, h):
        kind, i, j = unit_mats(my_role, u)
        ra, rb = part(R2A, kind, i, h), part(R2B, kind, i, h)
        wait_in(ra, (S_SA, u, h))
        add_into(half_unit(G, kind, i, h, slice(0, 2), y, x), ra)
        wait_in(rb, (S_SB, u, h))
        add_into(half_unit(G, kind, i, h, slice(2, 4), y, x), rb)
        for k in (2, 1, 3):
            slot = 1 if k == 3 else 0
            zz, dev = z_mate(k)
            copy(
                part(G, kind, i, h, zz, y, x),
                arrived(my_role, u, h, slot),
                (S_T, my_role, u, h, slot, k & 1),
                dev,
            ).start()

    def rs_sent(my_role, units):
        for u, (kind, i) in enumerate(units):
            for h in range(2):
                wait_out(part(R1A, kind, i, h), (S_RA, u, h))
                wait_out(part(R1B, kind, i, h), (S_RB, u, h))
                wait_out(part(R2A, kind, i, h), (S_SA, u, h))
                wait_out(part(R2B, kind, i, h), (S_SB, u, h))
                for k in (1, 2, 3):
                    slot = 1 if k == 3 else 0
                    wait_out(arrived(my_role, u, h, 0), (S_T, my_role, u, h, slot, k & 1))

    def final_sum(my_role, role_of, u):
        kind, i, j = unit_mats(role_of, u)
        for h in range(2):
            first = arrived(role_of, u, h, 0)
            second = arrived(role_of, u, h, 1)
            if my_role == role_of:
                wait_in(first, (S_T, role_of, u, h, 0, 0))
                ref, index = half_unit(G, kind, i, h, z, y, x)
                total = ref[index].astype(f32) + first[...].astype(f32)
            else:
                wait_in(first, (S_T, role_of, u, h, 0, 1))
                wait_in(second, (S_T, role_of, u, h, 1, 1))
                total = first[...].astype(f32) + second[...].astype(f32)
            if kind == SQUARE:
                r.F_GS[j + 2 * h : j + 2 * h + 2] = total
            else:
                r.F_GW[j, :, 512 * h : 512 * h + 512] = total

    def unit_stats(g):
        role_of, u = ALL_UNITS[g]
        kind, i, j = unit_mats(role_of, u)
        lanes = lax.broadcasted_iota(jnp.int32, (32, LANES), 1)
        rows = r.RQ[0:32, :]
        if kind == SQUARE:
            for m in range(4):
                grad = r.F_GS[j + m]
                sq = grad * grad
                cols = jnp.sum(sq, axis=0, keepdims=True)
                for h in range(2):
                    r.ST[g, z, 2 * m + h : 2 * m + h + 1, :] = cols[:, h * LANES : (h + 1) * LANES]
                rows = jnp.where(lanes == j + m, jnp.sum(sq, axis=1, keepdims=True), rows)
        else:
            grad = r.F_GW[j]
            sq = grad * grad
            cols = jnp.sum(sq, axis=0, keepdims=True)
            for h in range(8):
                r.ST[g, z, h : h + 1, :] = cols[:, h * LANES : (h + 1) * LANES]
            rows = jnp.where(lanes == 12 + j, jnp.sum(sq, axis=1, keepdims=True), rows)
        r.RQ[0:32, :] = rows
        if g == 0:
            r.SV[d] = r.ST[0, z]
            for k in range(1, 16):
                copy(r.SV.at[d], r.SV.at[d], S_SV, lax.rem(d + k, 16)).start()
            return
        for k in (1, 2, 3):
            copy(r.ST.at[g, z], r.ST.at[g, z], (S_ST, g), z_mate(k)[1]).start()

    def spread_unit(g):
        wait_in(r.ST.at[g, 0:3], (S_ST, g))
        r.SU[g, yx] = in_order(r.ST, (g,))
        for dev in plane_mates():
            copy(r.SU.at[g, yx], r.SU.at[g, yx], (S_SU, g), dev).start()

    def store_unit(g):
        kind, i, j = unit_mats(*ALL_UNITS[g])
        if kind == SQUARE:
            return local(r.F_GS.at[j : j + 4], r.o_gs.at[j : j + 4], 8 + g)
        return local(r.F_GW.at[j], r.o_gw.at[j], 8 + g)

    def finish_unit(my_role, g):
        final_sum(my_role, *ALL_UNITS[g])
        store_unit(g).start()
        unit_stats(g)

    def weight(kind, i, cols=None):
        if kind == SQUARE:
            return r.WS[i].reshape(512, 256)
        if cols is None:
            return r.WW[i].reshape(512, 1024)
        return r.WW[i, :, :, :, :, cols].reshape(512, 256)

    def put_square(i, value):
        r.GS[i] = value.astype(bf).reshape(4, 2, 2, 32, 256)

    def swap(number, partial):
        slot = number % 2
        for half in range(2):
            rows = slice(half * BLOCK, (half + 1) * BLOCK)
            if number >= 2:
                wait_out(r.PS.at[slot, rows], (S_M, number - 2, half))
            r.PS[slot, rows] = partial(rows).astype(bf)
            copy(
                r.PS.at[slot, rows], r.PR.at[slot, rows], (S_M, number, half), d, 1 - c
            ).start()

    def swapped(number, body):
        slot = number % 2
        for half in range(2):
            rows = slice(half * BLOCK, (half + 1) * BLOCK)
            wait_in(r.PR.at[slot, rows], (S_M, number, half))

            def chunk(i):
                at = pl.ds(pl.multiple_of(half * BLOCK + i * CHUNK, CHUNK), CHUNK)
                body(
                    at,
                    half * (BLOCK // CHUNK) + i,
                    r.PS[slot, at].astype(f32) + r.PR[slot, at].astype(f32),
                )

            repeat(BLOCK // CHUNK, chunk)

    def swaps_sent(count):
        for number in (count - 2, count - 1):
            for half in range(2):
                wait_out(r.PS.at[0, 0:BLOCK], (S_M, number, half))

    def norm_forward(residual, kept, which, at):
        centred = residual - jnp.mean(residual, axis=-1, keepdims=True)
        spread = lax.rsqrt(jnp.mean(centred * centred, axis=-1, keepdims=True) + 1e-05)
        normed = centred * spread
        r.XH[kept, at] = normed
        r.RSD[kept, at] = spread
        return normed * r.NORM[which : which + 1, :] + r.NORM[5 + which : 6 + which, :]

    def norm_backward(upstream, kept, which, at):
        normed = r.XH[kept, at]
        scaled = upstream * r.NORM[which : which + 1, :]
        both = upstream * normed
        gain_sum = jnp.sum(both, axis=0, keepdims=True)
        bias_sum = jnp.sum(upstream, axis=0, keepdims=True)
        for b in range(4):
            lanes = slice(b * LANES, (b + 1) * LANES)
            r.NGR[b, which : which + 1, :] += gain_sum[:, lanes]
            r.NGR[b, 5 + which : 6 + which, :] += bias_sum[:, lanes]
        return r.RSD[kept, at] * (
            scaled
            - jnp.mean(scaled, axis=-1, keepdims=True)
            - normed * jnp.mean(scaled * normed, axis=-1, keepdims=True)
        )

    head_lane = lax.broadcasted_iota(jnp.int32, (1, LANES), 1)
    first_head = jnp.where(head_lane < 64, 1.0, 0.0)
    second_head = 1.0 - first_head

    def stacked(value):
        wide_value = value.astype(f32)
        return jnp.concatenate([wide_value * first_head, wide_value * second_head], axis=0).astype(bf)

    def unstacked(value):
        return value[0:BLOCK] * first_head + value[BLOCK:] * second_head

    def pairs(body):
        for blk in range(2):
            for pr in range(2):
                body(blk, slice(blk * BLOCK, (blk + 1) * BLOCK), slice(pr * LANES, (pr + 1) * LANES), 2 * blk + pr)

    def make_masks(slot, count_of, causal):
        row = lax.broadcasted_iota(jnp.int32, (BLOCK, TOKENS), 0)
        col = lax.broadcasted_iota(jnp.int32, (BLOCK, TOKENS), 1) & (BLOCK - 1)
        same = (row >> 3) == (col >> 3)
        r.FILL[...] = jnp.where(same, NEG, OUTSIDE)
        for blk in range(2):
            ok = same & ((col & 7).astype(f32) < count_of(blk))
            if causal:
                ok = ok & ((col & 7) <= (row & 7))
            r.ALLOW[slot, blk] = jnp.where(ok, 1.0, 0.0)

    def attend(kept, mask_slot):
        def one(blk, rows, lanes, n):
            keys = stacked(r.K[kept, rows, lanes])
            scores = mm_nt(r.Q[kept, rows, lanes], keys) * 0.125
            scores = jnp.where(r.ALLOW[mask_slot, blk] > 0.5, scores, r.FILL[...])
            halves = []
            for h in range(2):
                s = scores[:, h * BLOCK : (h + 1) * BLOCK]
                e = jnp.exp(s - jnp.max(s, axis=-1, keepdims=True))
                halves.append(e / jnp.sum(e, axis=-1, keepdims=True))
            probs = jnp.concatenate(halves, axis=1)
            r.PROB[kept, n] = probs
            r.O[kept, rows, lanes] = mm(
                probs.astype(bf), stacked(r.V[kept, rows, lanes])
            ).astype(bf)

        pairs(one)

    def attend_back(kept):
        def one(blk, rows, lanes, n):
            queries = r.Q[kept, rows, lanes]
            keys = stacked(r.K[kept, rows, lanes])
            values = stacked(r.V[kept, rows, lanes])
            out_grad = r.DO[rows, lanes]
            probs = r.PROB[kept, n]
            weighted = probs * mm_nt(out_grad, values)
            halves = []
            for h in range(2):
                w = weighted[:, h * BLOCK : (h + 1) * BLOCK]
                p = probs[:, h * BLOCK : (h + 1) * BLOCK]
                halves.append(w - p * jnp.sum(w, axis=-1, keepdims=True))
            score_grad = jnp.concatenate(halves, axis=1).astype(bf)
            r.DQ[rows, lanes] = (mm(score_grad, keys) * 0.125).astype(bf)
            r.DK[rows, lanes] = (unstacked(mm_tn(score_grad, queries)) * 0.125).astype(bf)
            r.DV[rows, lanes] = unstacked(mm_tn(probs.astype(bf), out_grad)).astype(bf)

        pairs(one)

    def project_all(kept, base, queries, keys):
        r.Q[kept] = mm(queries, weight(SQUARE, base)).astype(bf)
        r.K[kept] = mm(keys, weight(SQUARE, base + 1)).astype(bf)
        r.V[kept] = mm(keys, weight(SQUARE, base + 2)).astype(bf)

    def attention_out(kept, base):
        return lambda rows: mm_nt(r.O[kept, rows], weight(SQUARE, base + 3))

    def attention_back_start(kept, base):
        upstream = r.GLOW[...]
        r.DO[...] = mm(upstream, weight(SQUARE, base + 3)).astype(bf)
        attend_back(kept)

    def query_side(base):
        return lambda rows: mm_nt(r.DQ[rows], weight(SQUARE, base))

    def key_side(base):
        return lambda rows: mm_nt(r.DK[rows], weight(SQUARE, base + 1)) + mm_nt(
            r.DV[rows], weight(SQUARE, base + 2)
        )

    def all_sides(base):
        return lambda rows: query_side(base)(rows) + key_side(base)(rows)

    def expand(inputs):
        def one(n):
            cols = aligned(n, 256)
            hidden = mm(inputs, weight(WIDE, 0, cols))
            r.U[:, cols] = hidden
            bent = jnp.tanh(0.7978845608 * (hidden + 0.044715 * hidden * hidden * hidden))
            r.ACT[:, cols] = (0.5 * hidden * (1.0 + bent)).astype(bf)

        repeat(4, one)

    def contract(rows):
        return mm_nt(r.ACT[rows], weight(WIDE, 1))

    def expand_back_down(h):
        upstream = r.GLOW[...]

        def one(n):
            cols = aligned(2 * h + n, 256)
            r.GW[1, :, :, :, :, cols] = (
                mm_tn(upstream, r.ACT[:, cols]).astype(bf).reshape(4, 2, 2, 32, 256)
            )

        repeat(2, one)

    def expand_back_hidden():
        upstream = r.GLOW[...]

        def one(n):
            cols = aligned(n, 256)
            active_grad = mm(upstream, weight(WIDE, 1, cols)).astype(bf).astype(f32)
            hidden = r.U[:, cols]
            square = hidden * hidden
            bent = jnp.tanh(0.7978845608 * (hidden + 0.044715 * hidden * square))
            slope = 0.5 * (1.0 + bent) + 0.5 * hidden * (1.0 - bent * bent) * 0.7978845608 * (
                1.0 + 3.0 * 0.044715 * square
            )
            r.DU[:, cols] = (active_grad * slope).astype(bf)

        repeat(4, one)

    def expand_back_up(inputs, h):
        def one(n):
            cols = aligned(2 * h + n, 256)
            r.GW[0, :, :, :, :, cols] = (
                mm_tn(inputs, r.DU[:, cols]).astype(bf).reshape(4, 2, 2, 32, 256)
            )

        repeat(2, one)

    def expand_input(rows):
        return mm_nt(r.DU[rows], weight(WIDE, 0))

    def clear_sums():
        r.NGR[...] = jnp.zeros((4, 16, LANES), f32)
        sums = jnp.sum(r.RL[...], axis=1, keepdims=True)
        rows = lax.broadcasted_iota(jnp.int32, (16, LANES), 0)
        lanes = lax.broadcasted_iota(jnp.int32, (16, LANES), 1)
        line = jnp.sum(jnp.where(rows == lanes, sums, 0.0), axis=0, keepdims=True)
        for b in range(4):
            r.NGR[b, 10:11, :] = line
        r.RQ[...] = jnp.zeros((BLOCK, LANES), f32)

    def read_norms():
        wait_in(r.NB.at[0:15], S_NORM)
        for b in range(4):
            total = r.NB[4 * b].astype(f32)
            for i in range(1, 4):
                total = total + r.NB[4 * b + i].astype(f32)
            r.NORM[:, b * LANES : (b + 1) * LANES] = total

    def by_role(body):
        pl.when(role == 0)(lambda: body(0))
        pl.when(role == 1)(lambda: body(1))

    def start_unit(u):
        def body(my_role):
            if u < 3:
                z_send(my_role, 0, u)
            units = (ENC_UNITS, DEC_UNITS)[my_role]
            if u < len(units):
                ag_plane(*units[u], u, 0)

        by_role(body)

    def later_units(my_role, us):
        for u in us:
            z_send(my_role, 1, u)

    loads[2].wait()
    cast_weights(0, 0)
    cast_weights(1, 0)
    pl.semaphore_wait(barrier, 16)
    start_unit(0)
    loads[3].wait()
    cast_weights(0, 1)
    cast_weights(1, 1)
    start_unit(1)
    by_role(lambda my_role: later_units(my_role, (0,)))
    cast_weights(0, 2)
    cast_weights(1, 2)
    start_unit(2)
    cast_weights(1, 3)
    start_unit(3)

    r.NORM[...] = jnp.zeros((16, 512), f32)
    for i in (5, 6, 7):
        loads[i].wait()
    r.NORM[0:10, 0:32] = r.I_NORM[...]
    shift = lax.rem(d, 4) * 32
    r.NB[d] = pltpu.roll(r.NORM[:, 0:LANES], shift, 1).astype(bf)
    r.RL[...] = jnp.zeros((16, LANES), f32)
    r.RL[0:12, 0:32] = r.I_SR[...]
    r.RL[12:16, 0:32] = r.I_WR[...]

    send_norms()

    lane = lax.broadcasted_iota(jnp.int32, (8, LANES), 1)
    for s in range(16):
        r.EXT[8 * s : 8 * s + 8, :] = jnp.where(
            lane < 32,
            r.lengths[0, s],
            jnp.where(lane < 64, r.lengths[1, s], r.destinations[s]),
        ).astype(f32)
    ext_low = r.EXT[...].astype(bf)
    r.SEXT[...] = ext_low

    loads[1].wait()

    @pl.when(role == 1)
    def _():
        copy(r.SRC.at[:, my_half], r.XHALF.at[c], S_SOURCE, partner).start()
        copy(r.SEXT, r.XEXT, S_EXT, partner).start()

    by_role(lambda my_role: later_units(my_role, (1,)))

    perm_f = perm_of(r.EXT[:, 64:65])
    r.PERMT[0] = perm_f.astype(bf)
    perm = perm_f.T.astype(bf)
    loads[0].wait()
    r.TSEND[:, :, 0:512] = mm(perm, r.TGT[...]).astype(bf).reshape(8, 16, 512)
    r.TSEND[:, :, 512:640] = mm(perm, ext_low).astype(bf).reshape(8, 16, LANES)

    loads[4].wait()

    def last_starts(my_role):
        send_target(my_role)
        later_units(my_role, (2, 3))
        if my_role == 0:
            copy(r.COT1, r.COT2, S_COT, partner).start()

    by_role(last_starts)

    def encoder():
        units = ENC_UNITS
        clear_sums()
        for u in range(3):
            ag_forward(units, u, (0,))
        ag_column(units, 0)
        ag_forward(units, 0)
        ag_column(units, 1)
        wait_in(r.XEXT, S_EXT)
        wait_in(r.XHALF.at[0], S_SOURCE)
        hand_over(r.XHALF, S_SOURCE2)
        r.XT[0:BLOCK] = r.SRC[...]
        for half in range(2):
            r.XT[BLOCK:, half * 256 : half * 256 + 256] = r.XHALF[half]
        def counts(blk):
            return r.EXT[:, 0:1] if blk == 0 else r.XEXT[...].astype(f32)[:, 0:1]

        make_masks(0, counts, False)
        r.PERMT[1] = perm_of(r.XEXT[...].astype(f32)[:, 64:65]).astype(bf)
        read_norms()
        ag_column(units, 2)
        ag_finish(units, 0)
        x_in = r.XT[...]
        project_all(0, 0, x_in, x_in)
        attend(0, 0)
        swap(0, attention_out(0, 0))
        ag_forward(units, 1)

        def first(at, n, total):
            hidden = norm_forward(r.XT[at].astype(f32) + total, 0, 0, at)
            r.RES[at] = hidden
            r.LOW[0, at] = hidden.astype(bf)

        swapped(0, first)
        ag_finish(units, 1)
        expand(r.LOW[0])
        ag_forward(units, 2)
        ag_finish(units, 2)
        swap(1, contract)

        def second(at, n, total):
            r.LOW[1, at] = norm_forward(r.RES[at] + total, 1, 1, at).astype(bf)

        swapped(1, second)
        for jj in range(2):
            block = r.LOW[1, jj * BLOCK : (jj + 1) * BLOCK]
            r.MSEND[:, jj] = mm_tn(r.PERMT[jj], block).astype(bf).reshape(8, 16, 512)
        zz = lax.div(z, 2)
        for t in range(8):
            dev = (2 * (t // 4) + 1) * 4 + t % 4
            copy(
                r.MSEND.at[t, :, :, my_half], r.MREC.at[c, zz, :, yx], S_MEMORY, dev
            ).start()

        wait_in(r.MG.at[0], S_DM)
        hand_over(r.MG, S_DM2)
        for jj in range(2):
            for half in range(2):
                r.GRAD[jj * BLOCK : (jj + 1) * BLOCK, half * 256 : half * 256 + 256] = mm(
                    r.PERMT[jj], r.MG[half, :, jj].reshape(BLOCK, 256)
                )

        def back_one(i):
            at = aligned(i, CHUNK)
            value = norm_backward(r.GRAD[at], 1, 1, at)
            r.GRAD[at] = value
            r.GLOW[at] = value.astype(bf)

        repeat(TOKENS // CHUNK, back_one)
        for h in range(2):
            expand_back_down(h)
            rs_first(units, 2, h)
        expand_back_hidden()
        swap(2, expand_input)
        for h in range(2):
            expand_back_up(r.LOW[0], h)
            rs_first(units, 1, h)

        def back_two(at, n, total):
            value = norm_backward(r.GRAD[at] + total, 0, 0, at)
            r.GRAD[at] = value
            r.GLOW[at] = value.astype(bf)

        swapped(2, back_two)
        rs_second(units, 2, 0)
        attention_back_start(0, 0)
        swap(3, all_sides(0))
        rs_second(units, 2, 1)
        put_square(3, mm_tn(r.GLOW[...], r.O[0]))
        put_square(2, mm_tn(r.XT[...], r.DV[...]))
        rs_first(units, 0, 1)
        put_square(0, mm_tn(r.XT[...], r.DQ[...]))
        put_square(1, mm_tn(r.XT[...], r.DK[...]))

        def back_three(at, n, total):
            r.GRAD[at] = r.GRAD[at] + total

        swapped(3, back_three)
        for target_ref, value in ((r.F_SRC, r.GRAD[0:BLOCK]), (r.SGSEND, r.GRAD[BLOCK:])):
            value = value.reshape(16, 8, 512)
            target_ref[...] = jnp.where(c == 0, value[:, 0:4], value[:, 4:8])
        local(r.F_SRC, r.o_src, 6).start()
        copy(r.SGSEND, r.SGREC, S_SG, partner).start()
        send_norm_sums()
        rs_first(units, 0, 0)
        rs_second(units, 1, 0)
        rs_second(units, 1, 1)
        rs_third(0, 2, 0)
        rs_third(0, 2, 1)
        finish_unit(0, 6)
        wait_in(r.DREC, S_DEC)
        r.F_DEC[...] = r.DREC[...]
        local(r.F_DEC, r.o_dec, 5).start()
        take_target(0)
        finish_unit(0, 5)
        rs_second(units, 0, 1)
        rs_second(units, 0, 0)
        rs_third(0, 1, 0)
        rs_third(0, 1, 1)
        finish_unit(0, 4)
        finish_unit(0, 2)
        rs_third(0, 0, 1)
        rs_third(0, 0, 0)
        finish_unit(0, 3)
        wait_out(r.MREC.at[0], S_MEMORY)
        wait_out(r.SGSEND, S_SG)
        swaps_sent(4)
        spread_norm_sums()
        for g in (6, 5, 4):
            spread_unit(g)
        finish_unit(0, 1)
        spread_unit(2)
        spread_unit(3)
        finish_unit(0, 0)
        spread_unit(1)
        ag_sent(units)
        rs_sent(0, units)
        z_sent(0)
        wait_out(r.NB.at[0:15], S_NORM)
        wait_out(r.COT1, S_COT)
        wait_out(r.TSEND, S_TARGET)

    def send_norm_sums():
        r.NG[z] = r.NGR[z]
        for k in (1, 2, 3):
            zz, dev = z_mate(k)
            copy(r.NGR.at[zz], r.NG.at[z], S_NG, dev).start()

    def spread_norm_sums():
        wait_in(r.NG.at[0:3], S_NG)
        r.NH[yx] = in_order(r.NG)
        for dev in plane_mates():
            copy(r.NH.at[yx], r.NH.at[yx], S_NH, dev).start()

    def take_target(my_role):
        if my_role == 0:
            wait_in(r.TG.at[0], S_DT)
        else:
            wait_in(r.TG.at[0, 0:7], S_DT)
        hand_over(r.TG, S_DT2)
        for half in range(2):
            r.F_TGT[:, :, half * 256 : half * 256 + 256] = mm(
                r.PERMT[0], r.TG[half].reshape(BLOCK, 256)
            ).reshape(16, 8, 256)
        local(r.F_TGT, r.o_tgt, 7).start()

    def decoder():
        units = DEC_UNITS
        clear_sums()
        for u in range(4):
            ag_forward(units, u, (0,))
        ag_column(units, 0)
        ag_forward(units, 0)
        ag_column(units, 1)
        ag_forward(units, 1)
        wait_in(r.TREC.at[0:15], S_TARGET)
        cot = r.COT

        def place(i):
            at = aligned(i, 32)
            both = jnp.concatenate(
                [
                    r.COT1[at].astype(f32).reshape(4, 1, 8, 512),
                    r.COT2[at].astype(f32).reshape(4, 1, 8, 512),
                ],
                axis=1,
            )
            cot[aligned(i, CHUNK)] = both.reshape(CHUNK, 512)

        r.XT[...] = r.TREC[:, :, 0:512].reshape(TOKENS, 512)

        def counts(which):
            def get(blk):
                ext = r.TREC[8 * blk : 8 * blk + 8, :, 512:640].reshape(BLOCK, LANES)
                return ext.astype(f32)[:, 32 * which : 32 * which + 1]

            return get

        make_masks(0, counts(1), True)
        make_masks(1, counts(0), False)
        read_norms()
        ag_column(units, 2)
        ag_column(units, 3)
        ag_finish(units, 0)
        x_in = r.XT[...]
        project_all(0, 0, x_in, x_in)
        attend(0, 0)
        swap(0, attention_out(0, 0))
        ag_forward(units, 2)

        def first(at, n, total):
            hidden = norm_forward(r.XT[at].astype(f32) + total, 0, 2, at)
            r.RES[at] = hidden
            r.LOW[0, at] = hidden.astype(bf)

        swapped(0, first)
        ag_forward(units, 3)
        ag_finish(units, 1)
        wait_in(r.COT2, S_COT)
        repeat(4, place)
        r.Q[1] = mm(r.LOW[0], weight(SQUARE, 4)).astype(bf)
        wait_in(r.MREC.at[0], S_MEMORY)
        hand_over(r.MREC, S_MEMORY2)
        for half in range(2):
            r.MEM[:, half * 256 : half * 256 + 256] = r.MREC[half].reshape(TOKENS, 256)
        memory = r.MEM[...]
        r.K[1] = mm(memory, weight(SQUARE, 5)).astype(bf)
        r.V[1] = mm(memory, weight(SQUARE, 6)).astype(bf)
        attend(1, 1)
        swap(1, attention_out(1, 4))

        def second(at, n, total):
            hidden = norm_forward(r.RES[at] + total, 1, 3, at)
            r.RES[at] = hidden
            r.LOW[1, at] = hidden.astype(bf)

        swapped(1, second)
        ag_finish(units, 2)
        expand(r.LOW[1])
        ag_finish(units, 3)
        swap(2, contract)

        def third(at, n, total):
            out = norm_forward(r.RES[at] + total, 2, 4, at)
            rows = aligned(n, 32)
            split = out.reshape(4, 2, 8, 512)
            r.F_DEC[rows] = split[:, 0].reshape(32, 512).astype(bf)
            r.DSEND[rows] = split[:, 1].reshape(32, 512).astype(bf)
            value = norm_backward(cot[at], 2, 4, at)
            r.GRAD[at] = value
            r.GLOW[at] = value.astype(bf)

        swapped(2, third)
        expand_back_hidden()
        swap(3, expand_input)
        for h in range(2):
            expand_back_down(h)
            rs_first(units, 3, h)
        local(r.F_DEC, r.o_dec, 5).start()

        def back_two(at, n, total):
            value = norm_backward(r.GRAD[at] + total, 1, 3, at)
            r.GRAD[at] = value
            r.GLOW[at] = value.astype(bf)

        swapped(3, back_two)
        attention_back_start(1, 4)
        swap(4, key_side(4))
        for h in range(2):
            expand_back_up(r.LOW[1], h)

        def back_memory(at, n, total):
            r.LOW[2, at] = total.astype(bf)

        swapped(4, back_memory)
        r.DMSEND[...] = r.LOW[2].reshape(2, 2, 4, 16, 512)
        my_t = lax.div(z, 2) * 4 + yx
        for t in range(8):
            dev = (2 * (t // 4)) * 4 + t % 4
            copy(
                r.DMSEND.at[t // 4, :, t % 4, :, my_half], r.MG.at[c, my_t], S_DM, dev
            ).start()
        copy(r.DSEND, r.DREC, S_DEC, partner).start()
        for h in range(2):
            rs_second(units, 3, h)
            rs_first(units, 2, h)
        swap(5, query_side(4))
        put_square(7, mm_tn(r.GLOW[...], r.O[1]))
        put_square(6, mm_tn(r.MEM[...], r.DV[...]))
        rs_first(units, 1, 1)
        put_square(5, mm_tn(r.MEM[...], r.DK[...]))
        put_square(4, mm_tn(r.LOW[0], r.DQ[...]))
        rs_first(units, 1, 0)

        def back_three(at, n, total):
            value = norm_backward(r.GRAD[at] + total, 0, 2, at)
            r.GRAD[at] = value
            r.GLOW[at] = value.astype(bf)

        swapped(5, back_three)
        attention_back_start(0, 0)
        swap(6, all_sides(0))
        put_square(3, mm_tn(r.GLOW[...], r.O[0]))
        put_square(2, mm_tn(r.XT[...], r.DV[...]))
        rs_first(units, 0, 1)
        put_square(0, mm_tn(r.XT[...], r.DQ[...]))
        put_square(1, mm_tn(r.XT[...], r.DK[...]))
        rs_third(1, 3, 0)
        rs_third(1, 3, 1)
        rs_second(units, 2, 0)
        rs_second(units, 2, 1)
        rs_first(units, 0, 0)

        def back_four(at, n, total):
            r.DTSEND[aligned(n, 4)] = (
                (r.GRAD[at] + total).astype(bf).reshape(4, 16, 512)
            )

        swapped(6, back_four)
        for k in range(1, 16):
            dev = lax.rem(d + k, 16)
            copy(r.DTSEND.at[dev, :, my_half], r.TG.at[c, my_t], S_DT, dev).start()
        r.TG[c, my_t] = r.DTSEND[d, :, my_half]
        send_norm_sums()
        rs_second(units, 1, 1)
        rs_third(1, 2, 0)
        rs_second(units, 1, 0)
        rs_third(1, 2, 1)
        finish_unit(1, 6)
        rs_second(units, 0, 1)
        rs_third(1, 1, 1)
        rs_second(units, 0, 0)
        rs_third(1, 1, 0)
        finish_unit(1, 5)
        take_target(1)
        rs_third(1, 0, 1)
        rs_third(1, 0, 0)
        finish_unit(1, 4)
        finish_unit(1, 2)
        wait_in(r.SGREC, S_SG)
        r.F_SRC[...] = r.SGREC[...]
        local(r.F_SRC, r.o_src, 6).start()
        wait_out(r.DTSEND.at[0:15, :, 0:256], S_DT)
        wait_out(r.MG.at[0], S_DM)
        wait_out(r.DSEND, S_DEC)
        swaps_sent(7)
        spread_norm_sums()
        for g in (6, 5, 4):
            spread_unit(g)
        finish_unit(1, 3)
        finish_unit(1, 1)
        spread_unit(2)
        spread_unit(3)
        finish_unit(1, 0)
        spread_unit(1)
        ag_sent(units)
        rs_sent(1, units)
        z_sent(1)
        wait_out(r.NB.at[0:15], S_NORM)
        wait_out(r.SEXT, S_EXT)
        wait_out(r.XHALF.at[0], S_SOURCE)
        wait_out(r.TSEND.at[0:7], S_TARGET)

    pl.when(role == 0)(encoder)
    pl.when(role == 1)(decoder)

    copy(r.RQ, r.RQR, S_RQ, d, 1 - c).start()
    wait_in(r.NH.at[0:3], S_NH)
    total = in_order(r.NH)
    r.o_ng[...] = pltpu.roll(total, lax.rem(LANES - shift, LANES), 1)
    r.o_rl[...] = total
    for g in (6, 5, 4, 2, 3, 1, 0):
        if g == 0:
            wait_in(r.SV.at[0:15], S_SV)
            total = r.SV[0]
            for i in range(1, 16):
                total = total + r.SV[i]
        else:
            wait_in(r.SU.at[g, 0:3], (S_SU, g))
            total = in_order(r.SU, (g,))
        r.TT[g] = jnp.broadcast_to(jnp.sum(total, axis=1, keepdims=True), (8, LANES))
        role_of, u = ALL_UNITS[g]
        kind, _, j = unit_mats(role_of, u)
        for h in range(8):
            if kind == SQUARE:
                r.o_cs[j + h // 2 : j + h // 2 + 1, (h % 2) * LANES : (h % 2 + 1) * LANES] = total[h : h + 1]
            else:
                r.o_cw[j : j + 1, h * LANES : (h + 1) * LANES] = total[h : h + 1]
    copy(r.TT, r.TTR, S_TT, d, 1 - c).start()
    wait_in(r.RQR, S_RQ)
    r.o_rq[...] = r.RQ[...] + r.RQR[...]
    wait_in(r.TTR, S_TT)
    r.o_tt[...] = r.TT[...] + r.TTR[...]
    wait_out(r.RQ, S_RQ)
    wait_out(r.TT, S_TT)
    wait_out(r.NG.at[0:3], S_NG)
    wait_out(r.NH.at[0:3], S_NH)
    wait_out(r.SV.at[0:15], S_SV)
    for g in range(1, 7):
        wait_out(r.ST.at[g, 0:3], (S_ST, g))
        wait_out(r.SU.at[g, 0:3], (S_SU, g))
    local(r.F_DEC, r.o_dec, 5).wait()
    local(r.F_SRC, r.o_src, 6).wait()
    local(r.F_TGT, r.o_tgt, 7).wait()
    for g in range(7):
        store_unit(g).wait()


UPDATE_INPUTS = dict(
    square=0,
    wide=0,
    norm=0,
    square_rows=0,
    square_cols=0,
    wide_rows=0,
    wide_cols=0,
    moment=0,
)
UPDATE_OUTPUTS = dict(
    decoded=((16, 4, 512), jnp.bfloat16),
    source_grad=((16, 4, 512), jnp.float32),
    target_grad=((16, 8, 512), jnp.float32),
    square_grad=((12, 32, 256), jnp.float32),
    square_rows_new=((12, 32), jnp.float32),
    square_cols_new=((12, 256), jnp.float32),
    square_new=((12, 32, 256), jnp.float32),
    square_copy=((12, 32, 256), jnp.bfloat16),
    wide_grad=((4, 32, 1024), jnp.float32),
    wide_rows_new=((4, 32), jnp.float32),
    wide_cols_new=((4, 1024), jnp.float32),
    wide_new=((4, 32, 1024), jnp.float32),
    wide_copy=((4, 32, 1024), jnp.bfloat16),
    norm_grad=((10, 32), jnp.float32),
    norm_second_new=((10, 32), jnp.float32),
    norm_new=((10, 32), jnp.float32),
    norm_copy=((10, 32), jnp.bfloat16),
)


def update_kernel(*refs):
    r = named(refs, OUTPUTS, UPDATE_INPUTS, UPDATE_OUTPUTS, dict(rows_pad=0))
    c = lax.axis_index("mp")
    bf, f32 = jnp.bfloat16, jnp.float32

    def own_half(value):
        value = value.astype(f32).reshape(16, 8, 512)
        return jnp.where(c == 0, value[:, 0:4], value[:, 4:8])

    r.decoded[...] = own_half(r.o_dec[...]).astype(bf)
    r.source_grad[...] = r.o_src[...]
    r.target_grad[...] = r.o_tgt[...]
    pad = r.rows_pad
    pad[...] = jnp.zeros((BLOCK, LANES), f32)
    pad[0:12, 0:32] = r.square_rows[...]
    pad[12:16, 0:32] = r.wide_rows[...]
    lanes = lax.broadcasted_iota(jnp.int32, (BLOCK, LANES), 1)
    widths = jnp.where(lanes < 12, 1.0 / 512, 1.0 / FF)
    rows_new = 0.5 * pad[...].T + 0.5 * (r.o_rq[...] * widths)
    rows_back = rows_new.T
    r.square_rows_new[...] = rows_back[0:12, 0:32]
    r.wide_rows_new[...] = rows_back[12:16, 0:32]
    square_cols = 0.5 * r.square_cols[...] + 0.5 * (r.o_cs[...] / 512)
    wide_cols = 0.5 * r.wide_cols[...] + 0.5 * (r.o_cw[...] / 512)
    r.square_cols_new[...] = square_cols
    r.wide_cols_new[...] = wide_cols

    def level(m, total, width):
        return (0.5 * r.o_rl[10:11, m : m + 1] + 0.5 * (total / width)) / 512

    def update(master, grad, row, col, lvl):
        return master - RATE * grad * lax.rsqrt(row * col / lvl)

    for g, (role, u) in enumerate(ALL_UNITS):
        kind, _, j = unit_mats(role, u)
        if kind == SQUARE:
            for m in range(4):
                sums = r.o_tt[g]
                total = sums[2 * m : 2 * m + 1, 0:1] + sums[2 * m + 1 : 2 * m + 2, 0:1]
                grad = r.o_gs[j + m]
                new = update(
                    r.square[j + m],
                    grad,
                    rows_new[0:32, j + m : j + m + 1],
                    square_cols[j + m : j + m + 1],
                    level(j + m, total, 512),
                )
                r.square_grad[j + m] = grad
                r.square_new[j + m] = new
                r.square_copy[j + m] = new.astype(bf)
        else:
            total = jnp.sum(r.o_tt[g], axis=0, keepdims=True)[:, 0:1]
            grad = r.o_gw[j]
            new = update(
                r.wide[j],
                grad,
                rows_new[0:32, 12 + j : 13 + j],
                wide_cols[j : j + 1],
                level(12 + j, total, FF),
            )
            r.wide_grad[j] = grad
            r.wide_new[j] = new
            r.wide_copy[j] = new.astype(bf)
    norm_grad = r.o_ng[0:10, 0:32]
    second = 0.5 * r.moment[...] + 0.5 * norm_grad * norm_grad
    norm_new = r.norm[...] - NORM_RATE * norm_grad * lax.rsqrt(second)
    r.norm_grad[...] = norm_grad
    r.norm_second_new[...] = second
    r.norm_new[...] = norm_new
    r.norm_copy[...] = norm_new.astype(bf)


def small_shards(
    source,
    target,
    lengths,
    destinations,
    cotangent,
    square_master,
    wide_master,
    norm_master,
    square_rows,
    square_cols,
    wide_rows,
    wide_cols,
    gain_offset_moment,
):
    vmem = pl.BlockSpec(memory_space=pltpu.VMEM)
    smem = pl.BlockSpec(memory_space=pltpu.SMEM)
    anywhere = pl.BlockSpec(memory_space=pl.ANY)
    moved = pl.pallas_call(
        exchange_kernel,
        out_shape=[jax.ShapeDtypeStruct(*v) for v in OUTPUTS.values()],
        in_specs=[smem, smem] + [anywhere] * 5 + [anywhere] * 3,
        out_specs=[anywhere] * 5 + [vmem] * (len(OUTPUTS) - 5),
        scratch_shapes=[pltpu.VMEM(*v) for v in SCRATCH.values()]
        + [pltpu.SemaphoreType.DMA((n,)) for n in (SEM_COUNT, SEM_COUNT, NEAR_COUNT)],
        compiler_params=pltpu.CompilerParams(
            collective_id=0, has_side_effects=True, vmem_limit_bytes=56 << 20
        ),
    )(
        lengths.T,
        destinations,
        source.reshape(BLOCK, 512),
        target.reshape(BLOCK, 512),
        cotangent.reshape(BLOCK, 512),
        square_master,
        wide_master,
        norm_master,
        square_rows,
        wide_rows,
    )
    return tuple(
        pl.pallas_call(
            update_kernel,
            out_shape=[jax.ShapeDtypeStruct(*v) for v in UPDATE_OUTPUTS.values()],
            in_specs=[vmem] * (len(OUTPUTS) + len(UPDATE_INPUTS)),
            out_specs=[vmem] * len(UPDATE_OUTPUTS),
            scratch_shapes=[pltpu.VMEM((BLOCK, LANES), jnp.float32)],
            compiler_params=pltpu.CompilerParams(vmem_limit_bytes=60 << 20),
        )(
            *moved,
            square_master,
            wide_master,
            norm_master,
            square_rows,
            square_cols,
            wide_rows,
            wide_cols,
            gain_offset_moment,
        )
    )


def solution(mesh):
    return jax.shard_map(
        small_shards if dict(mesh.shape) == {"dp": 16, "mp": 2} else shards,
        mesh=mesh,
        in_specs=(
            P("dp", None, None),
            P("dp", None, None),
            P("dp", None),
            P("dp"),
            P("dp", None, None),
            P(None, "dp", "mp"),
            P(None, "dp", "mp"),
            P(None, "dp"),
            P(None, "dp"),
            P(None, "mp"),
            P(None, "dp"),
            P(None, "mp"),
            P(None, "dp"),
        ),
        out_specs=(
            P("dp", "mp", None),
            P("dp", "mp", None),
            P("dp", None, None),
            P(None, "dp", "mp"),
            P(None, "dp"),
            P(None, "mp"),
            P(None, "dp", "mp"),
            P(None, "dp", "mp"),
            P(None, "dp", "mp"),
            P(None, "dp"),
            P(None, "mp"),
            P(None, "dp", "mp"),
            P(None, "dp", "mp"),
            P(None, "dp"),
            P(None, "dp"),
            P(None, "dp"),
            P(None, "dp"),
        ),
        check_vma=False,
    )
```
